32 devices in a mesh: parts: 2 (over y), dp: 8 (over z, x), tensor: 2 (over core).
Axes of the slice: x: 2, y: 2, z: 4, core: 2. Of those that a mesh axis runs over, the one named last changes fastest.
Arguments:
- sent_rows: bfloat16 [4096, 8192], P(('parts', 'dp'), 'tensor'), parts along dimension 0, may hold values from -6 to 6
- norm_gain: float32 [8192], P('tensor'), may hold values from 0.5 to 12
- qkv_weight: bfloat16 [8192, 1280], P('tensor', 'dp'), may hold values from -0.0625 to 0.0625
- route_counts: int32 [16, 8], P('parts'), parts along dimension 0, may hold values from 0 to 32, as said below
- response_lengths: int32 [16, 8], P(('parts', 'dp')), parts along dimension 0, may hold values from 1 to 64, 128 in all within a row
- prefix_lengths: int32 [16, 8], P(('parts', 'dp')), parts along dimension 0, may hold values from 0 to 8191
Outputs:
- new_keys: bfloat16 [2048, 128], P(('parts', 'dp')), parts along dimension 0
- new_values: bfloat16 [2048, 128], P(('parts', 'dp')), parts along dimension 0
- attended: bfloat16 [2048, 1024], P(('parts', 'dp'), 'tensor'), parts along dimension 0
The draws below stay inside these ranges and needn't reach their ends.
There are 2 independent parts, one for each index of `parts`. The reference program is written for one: setup_inputs(seed, part) draws one part's arguments, and reference() takes and returns one part's arrays. A program takes and returns all parts, laid end to end along the dimension named above; an argument that names none is the same for every part. Nothing has to cross between parts.
Inputs may be any that keep to these rules, and one draw needn't show every extreme that they name: route_counts[s, d] rows go from group s to group d; every column sums to 128; every column holds at least one entry equal to 32, and its entries pair up into pairs that sum to 32.
All inputs are finite; a program needn't handle non-finite values.
Results may differ from the reference program's by a relative error of at most 0.004.
The reference program's roundings to bfloat16 on the way (of `packed`, `normed`, `projected`, `queries` and `weights`) count: a program that leaves them out, or rounds other values in their place, can miss the bound.
Values may be sent and summed in bfloat16 or wider, within the bound.
No kernel may reach another device: no remote copies, remote signals or barrier semaphores. Data moves between devices by JAX's collectives and lax.ppermute only.
A program may use at most 128 MiB of HBM per device.

```python
import math
import jax
import jax.numpy as jnp
import numpy as np
from jax import lax

D = 8192
HD = 128
HQ = 8
NSEQ = 8
TOK_DEV = 128
QKV = 1280
ROWS = 256
SLOT = 32
MOST = 64
N_DP = 8


def draw_norm_gain(key, part):
    key = jax.random.fold_in(key, 7)
    upper = 2.0
    level = jax.random.uniform(key, (D,), jnp.float32, jnp.log(0.5), jnp.log(upper))
    return jnp.exp(level).astype(jnp.float32)


def draw_route_counts(key, part):
    key = jax.random.fold_in(key, 11)
    half = SLOT // 2
    keys = jax.random.split(key, N_DP)
    orders = jax.vmap(lambda inner: jax.random.permutation(inner, N_DP))(keys)
    moves = jax.random.randint(jax.random.fold_in(key, 1), (N_DP, N_DP // 2), 0, half + 1)
    moves = moves.at[:, 0].set(half)
    lines = jnp.arange(N_DP, dtype=jnp.int32)[:, None]
    table = jnp.zeros((N_DP, N_DP), jnp.int32)
    table = table.at[lines, orders[:, 0::2]].set(half + moves)
    table = table.at[lines, orders[:, 1::2]].set(half - moves)
    return table.T.astype(jnp.int32)


def place_ends(drawn, key, smallest, high):
    extent = drawn.shape
    index_at = [jax.random.randint(jax.random.fold_in(key, axis), (), 0, extent[axis]) for axis in range(len(extent))]
    drawn = drawn.at[tuple(index_at)].set(smallest)
    longest = extent.index(max(extent))
    index_at[longest] = (index_at[longest] + 1) % extent[longest]
    return drawn.at[tuple(index_at)].set(high)


def block_scale(own_key, shape, cuts, smallest, top_value):
    level, own = 1.0, jax.random.fold_in(own_key, 6)
    for dim, shards_of in cuts:
        steps = jnp.exp(jax.random.uniform(jax.random.fold_in(own, dim), (shards_of,), jnp.float32, smallest / len(cuts), top_value / len(cuts)))
        level = level * jnp.repeat(steps, shape[dim] // shards_of).reshape([-1 if axis == dim else 1 for axis in range(len(shape))])
    return level


def split_up(amount, total, reach, lean):
    portions = [(1 << 20) // math.isqrt(standing ** lean) + 1 for standing in range(2, amount + 1)]
    spare, counts = total - reach - (amount - 1), [1] * (amount - 1)
    while spare > 0:
        candidates = [i for i in range(amount - 1) if counts[i] < reach]
        pool, budget = sum([portions[i] for i in candidates]), spare
        for i in candidates:
            more = min(reach - counts[i], max(1, budget * portions[i] // pool), spare)
            counts[i] = counts[i] + more
            spare = spare - more
    return np.array([reach] + counts)


def ragged_sizes(stream_key, amount, total, limit, skew):
    if amount == 2:
        one = jax.random.randint(stream_key, (), max(1, total - limit), min(limit, total - 1) + 1)
        return jnp.stack([one, total - one])
    sizes = jnp.asarray(split_up(amount, total, limit, skew), jnp.int32)
    pairs = (amount - 1) // 2
    source_of, sink = sizes[1:1 + 2 * pairs:2], sizes[2:2 + 2 * pairs:2]
    room = jnp.minimum(source_of - 1, limit - sink)
    passed = jax.random.randint(jax.random.fold_in(stream_key, 1), (pairs,), 0, 1 << 20) % (room + 1)
    sizes = sizes.at[1:1 + 2 * pairs:2].set(source_of - passed).at[2:2 + 2 * pairs:2].set(sink + passed)
    return sizes[jax.random.permutation(jax.random.fold_in(stream_key, 2), amount)]


def scatter_about(key, dims, spread, most, pieces=(), held_as=jnp.bfloat16):
    level = block_scale(key, dims, pieces, -0.22, 0.18) if pieces else 1.0
    drawn = jax.random.normal(key, dims, jnp.float32) * spread * level
    return jnp.minimum(jnp.maximum(drawn, -most), most).astype(held_as)


def setup_inputs(seed: int = 0, part: int = 0) -> dict:
    arg_keys = jax.random.split(jax.random.key(seed), 7)
    own_keys = jax.random.split(jax.random.fold_in(arg_keys[6], part), 7)
    sent_rows = scatter_about(own_keys[0], (N_DP * ROWS, D), 1.0, 6.0, ((0, 8), (1, 2)))
    norm_gain = draw_norm_gain(jax.random.fold_in(arg_keys[6], 71), part)
    qkv_weight = scatter_about(arg_keys[2], (D, QKV), D ** -0.5, 0.0625, ((0, 2), (1, 8)))
    route_counts = draw_route_counts(jax.random.fold_in(jax.random.fold_in(arg_keys[6], part), 71), part)
    response_lengths = jax.vmap(lambda own: ragged_sizes(own, NSEQ, TOK_DEV, MOST, 2))(jax.random.split(own_keys[4], N_DP)).reshape((N_DP, NSEQ)).astype(jnp.int32)
    prefix_lengths = place_ends(jax.random.randint(own_keys[5], (N_DP, NSEQ), 0, 8192), jax.random.fold_in(own_keys[5], 1), 0, 8191).astype(jnp.int32)
    return dict(sent_rows=sent_rows, norm_gain=norm_gain, qkv_weight=qkv_weight, route_counts=route_counts, response_lengths=response_lengths, prefix_lengths=prefix_lengths)


def rotate(block, positions):
    half = block.shape[-1] // 2
    freq = jnp.exp(-jnp.log(500000.0) * jnp.arange(half, dtype=jnp.float32) * 2.0 / block.shape[-1])
    angle = positions.astype(jnp.float32)[:, None] * freq[None, :]
    if block.ndim == 3:
        angle = angle[:, None, :]
    cosine = jnp.cos(angle)
    sine = jnp.sin(angle)
    first = block[..., :half]
    second = block[..., half:]
    return jnp.concatenate([first * cosine - second * sine, second * cosine + first * sine], axis=-1)

def positions_of(lengths, prefix, count):
    ends = jnp.cumsum(lengths).astype(jnp.int32)
    starts = ends - lengths
    place = jnp.arange(count, dtype=jnp.int32)
    member = (place[:, None] >= starts[None, :]) & (place[:, None] < ends[None, :])
    which = jnp.arange(lengths.shape[0], dtype=jnp.int32)
    sequence = lax.optimization_barrier(jnp.sum(jnp.where(member, which[None, :], 0), axis=1)).astype(jnp.int32)
    position = lax.optimization_barrier(jnp.sum(jnp.where(member, prefix[None, :] + place[:, None] - starts[None, :], 0), axis=1)).astype(jnp.int32)
    return (sequence, position)

def pack_rows(received, column, slot, count):
    ends = jnp.cumsum(column).astype(jnp.int32)
    starts = ends - column
    place = jnp.arange(count, dtype=jnp.int32)
    member = (place[:, None] >= starts[None, :]) & (place[:, None] < ends[None, :])
    source = jnp.arange(column.shape[0], dtype=jnp.int32)
    anchor = lax.optimization_barrier(jnp.sum(jnp.where(member, source[None, :], 0), axis=1))
    within = lax.optimization_barrier(jnp.sum(jnp.where(member, place[:, None] - starts[None, :], 0), axis=1))
    index = (anchor * slot + within).astype(jnp.int32)
    return jnp.take(received, index, axis=0)

def attend(queries, keys, values, sequence, position):
    scores = jnp.einsum('qhd,kd->hqk', queries.astype(jnp.float32), keys.astype(jnp.float32)) / jnp.sqrt(jnp.float32(keys.shape[-1]))
    allowed = (sequence[:, None] == sequence[None, :]) & (position[None, :] <= position[:, None])
    scores = jnp.where(allowed[None, :, :], scores, jnp.float32(-1e+30))
    top = lax.optimization_barrier(jnp.max(scores, axis=-1, keepdims=True))
    expo = jnp.exp(scores - top)
    weights = (expo / lax.optimization_barrier(jnp.sum(expo, axis=-1, keepdims=True))).astype(jnp.bfloat16)
    out = jnp.einsum('hqk,kd->qhd', weights.astype(jnp.float32), values.astype(jnp.float32))
    return out.astype(jnp.bfloat16)

def reference(sent_rows, norm_gain, qkv_weight, route_counts, response_lengths, prefix_lengths):
    grouped = sent_rows.reshape(N_DP, ROWS, D)

    def one_group(dest):
        received = lax.dynamic_slice_in_dim(grouped, (dest * SLOT).astype(jnp.int32), SLOT, 1).reshape(N_DP * SLOT, D)
        column = lax.dynamic_slice_in_dim(route_counts, dest, 1, 1)[:, 0]
        packed = pack_rows(received, column, SLOT, TOK_DEV)
        wide = packed.astype(jnp.float32)
        total = lax.optimization_barrier(jnp.sum(wide * wide, axis=1))
        normed = (wide * lax.rsqrt(total / D + 1e-05)[:, None] * norm_gain[None, :]).astype(jnp.bfloat16)
        projected = jnp.dot(normed, qkv_weight, preferred_element_type=jnp.float32).astype(jnp.bfloat16)
        lengths = lax.dynamic_slice_in_dim(response_lengths, dest, 1, 0)[0]
        prefix = lax.dynamic_slice_in_dim(prefix_lengths, dest, 1, 0)[0]
        sequence, position = positions_of(lengths, prefix, TOK_DEV)
        heads = projected[:, :HQ * HD].reshape(TOK_DEV, HQ, HD)
        queries = rotate(heads.astype(jnp.float32), position).astype(jnp.bfloat16)
        keys = rotate(projected[:, HQ * HD:HQ * HD + HD].astype(jnp.float32), position).astype(jnp.bfloat16)
        values = projected[:, HQ * HD + HD:]
        out = attend(queries, keys, values, sequence, position)
        return (keys, values, out.reshape(TOK_DEV, HQ * HD))
    keys, values, out = lax.map(one_group, jnp.arange(N_DP, dtype=jnp.int32))
    return (keys.reshape(N_DP * TOK_DEV, HD), values.reshape(N_DP * TOK_DEV, HD), out.reshape(N_DP * TOK_DEV, HQ * HD))
```

```python
import jax
import jax.numpy as jnp
from jax import lax
from jax.sharding import PartitionSpec as P

D = 8192
HD = 128
HQ = 8
TOK_DEV = 128
BLOCK = 16
AHEAD = 16


def rotary(positions):
    half = HD // 2
    freq = jnp.exp(-jnp.log(500000.0) * jnp.arange(half, dtype=jnp.float32) * 2.0 / HD)
    angle = positions.astype(jnp.float32)[:, None] * freq[None, :]
    return (jnp.cos(angle), jnp.sin(angle))


def rotate(block, cosine, sine):
    half = HD // 2
    if block.ndim == 3:
        cosine = cosine[:, None, :]
        sine = sine[:, None, :]
    first = block[..., :half]
    second = block[..., half:]
    return jnp.concatenate(
        [first * cosine - second * sine, second * cosine + first * sine], axis=-1
    )


def members(lengths, count):
    ends = jnp.cumsum(lengths)
    starts = ends - lengths
    place = jnp.arange(count, dtype=jnp.int32)
    member = (place[:, None] >= starts[None, :]) & (place[:, None] < ends[None, :])
    return (member, place[:, None] - starts[None, :])


def positions_of(lengths, prefix, count):
    member, within = members(lengths, count)
    which = jnp.arange(lengths.shape[0], dtype=jnp.int32)
    sequence = jnp.sum(jnp.where(member, which[None, :], 0), axis=1)
    position = jnp.sum(jnp.where(member, prefix[None, :] + within, 0), axis=1)
    return (sequence, position)


def pick_of(column, slot, count):
    member, within = members(column, count)
    source = jnp.arange(column.shape[0], dtype=jnp.int32)
    index = jnp.sum(jnp.where(member, source[None, :] * slot + within, 0), axis=1)
    slots = jnp.arange(column.shape[0] * slot, dtype=jnp.int32)
    return (index[:, None] == slots[None, :]).astype(jnp.bfloat16)


def attend(queries, keys, values, allowed):
    scores = jnp.einsum(
        "qhd,kd->hqk", queries, keys, preferred_element_type=jnp.float32
    ) / jnp.sqrt(jnp.float32(HD))
    scores = jnp.where(allowed[None, :, :], scores, jnp.float32(-1e30))
    top = jnp.max(scores, axis=-1, keepdims=True)
    expo = jnp.exp(scores - top)
    weights = (expo / jnp.sum(expo, axis=-1, keepdims=True)).astype(jnp.bfloat16)
    out = jnp.einsum("hqk,kd->qhd", weights, values, preferred_element_type=jnp.float32)
    return out.astype(jnp.bfloat16)


def norm(rows, norm_gain):
    wide = rows.astype(jnp.float32)
    total = lax.psum(jnp.sum(wide * wide, axis=1), "tensor")
    return (wide * lax.rsqrt(total / D + 1e-05)[:, None] * norm_gain[None, :]).astype(
        jnp.bfloat16
    )


def product(rows, columns):
    return lax.dot_general(
        rows, columns, (((1,), (1,)), ((), ())), preferred_element_type=jnp.float32
    )


def sum_cores(partial):
    width = HQ * HD * partial.shape[1] // (HQ * HD + 2 * HD)
    share = width // lax.axis_size("tensor")
    core = lax.axis_index("tensor")
    rest = partial[:, width:]

    def half(t):
        return jnp.concatenate(
            [lax.dynamic_slice_in_dim(partial, t * share, share, 1), rest], axis=1
        )

    other = lax.ppermute(half(1 - core), "tensor", [(0, 1), (1, 0)])
    return (half(core) + other).astype(jnp.bfloat16)


def gather_line(mine, groups):
    lines = groups // 2
    group = lax.axis_index("dp")
    z = group // 2
    x = group % 2
    early, late = mine[:AHEAD], mine[AHEAD:]
    depth = mine.shape[1]

    def over(block, low, high):
        pairs = [(i, i ^ 1) for i in range(2 * low, 2 * high)]
        return lax.ppermute(block, "dp", pairs)

    def along(block, low, high, step):
        return lax.ppermute(block, "dp", [(i, i + 2 * step) for i in range(2 * low, 2 * high)])

    early_over = over(early, 0, lines)
    early = jnp.concatenate([early, early_over], axis=0)
    pieces = [(z, early, late, over(late, 0, lines))]
    up_early, up_late, down_early, down_late = early, late, early, late
    for k in range(1, lines):
        up_late = along(up_late, k - 1, lines - 1, 1)
        down_late = along(down_late, 1, lines - k + 1, -1)
        up_early = along(up_early, k - 1, lines - 1, 1)
        down_early = along(down_early, 1, lines - k + 1, -1)
        up_over = over(up_late, k, lines)
        down_over = over(down_late, 0, lines - k)
        pieces.append((jnp.where(z >= k, z - k, lines), up_early, up_late, up_over))
        pieces.append((jnp.where(z < lines - k, z + k, lines), down_early, down_late, down_over))
    whole = jnp.zeros((2 * (lines + 1), mine.shape[0], depth), mine.dtype)
    for place, first, own, other in pieces:
        for at, head, tail in ((x, first[:AHEAD], own), (1 - x, first[AHEAD:], other)):
            whole = lax.dynamic_update_slice(whole, head[None], (2 * place + at, 0, 0))
            whole = lax.dynamic_update_slice(whole, tail[None], (2 * place + at, AHEAD, 0))
    return whole[: 2 * lines].reshape(groups * mine.shape[0], depth)


def paired(sent_rows, norm_gain, qkv_weight, groups):
    part = lax.axis_index("parts")
    normed = norm(sent_rows, norm_gain)
    theirs = lax.ppermute(normed, "parts", [(0, 1), (1, 0)])
    turned = qkv_weight.T
    count = turned.shape[0] // (2 * BLOCK)
    mine = lax.dynamic_index_in_dim(
        turned.reshape(count, 2, BLOCK, turned.shape[1]), part, 1, False
    ).reshape(count * BLOCK, turned.shape[1])
    columns = gather_line(mine, groups)
    own = sum_cores(product(normed, columns))
    other = sum_cores(product(theirs, columns))
    first = jnp.where(part == 0, own, other)
    second = jnp.where(part == 0, other, own)
    ready = jnp.concatenate([first, second], axis=0)
    arrived = lax.all_to_all(ready, ("parts", "dp"), 0, 0, tiled=True)
    return arrived.reshape(2, sent_rows.shape[0], arrived.shape[1])


def single(sent_rows, norm_gain, qkv_weight):
    columns = lax.all_gather(qkv_weight.T, "dp", axis=0, tiled=True)
    ready = sum_cores(product(norm(sent_rows, norm_gain), columns))
    return lax.all_to_all(ready, "dp", 0, 0, tiled=True)[None]


def per_device(sent_rows, norm_gain, qkv_weight, route_counts, response_lengths, prefix_lengths):
    groups = lax.axis_size("dp")
    slot = sent_rows.shape[0] // groups
    column = lax.dynamic_slice_in_dim(route_counts, lax.axis_index("dp"), 1, 1)[:, 0]
    pick = pick_of(column, slot, TOK_DEV)
    sequence, position = positions_of(response_lengths[0], prefix_lengths[0], TOK_DEV)
    allowed = (sequence[:, None] == sequence[None, :]) & (position[None, :] <= position[:, None])
    cosine, sine = rotary(position)
    if lax.axis_size("parts") == 2 and groups == 8 and qkv_weight.shape[1] % (2 * BLOCK) == 0:
        arrived = paired(sent_rows, norm_gain, qkv_weight, groups)
    else:
        arrived = single(sent_rows, norm_gain, qkv_weight)
    planes, _, width = arrived.shape
    heads = width * planes // HD
    packed = jnp.einsum("qs,psc->qpc", pick, arrived, preferred_element_type=jnp.float32)
    if planes == 2:
        packed = packed.reshape(TOK_DEV, 2, width // BLOCK, BLOCK).transpose(0, 2, 1, 3)
    packed = packed.reshape(TOK_DEV, heads, HD)
    queries = rotate(packed[:, :-2], cosine, sine).astype(jnp.bfloat16)
    new_keys = rotate(packed[:, -2], cosine, sine).astype(jnp.bfloat16)
    new_values = packed[:, -1].astype(jnp.bfloat16)
    out = attend(queries, new_keys, new_values, allowed)
    return (new_keys, new_values, out.reshape(TOK_DEV, (heads - 2) * HD))


def solution(mesh):
    in_specs = (
        P(("parts", "dp"), "tensor"),
        P("tensor"),
        P("tensor", "dp"),
        P("parts", None),
        P(("parts", "dp"), None),
        P(("parts", "dp"), None),
    )
    out_specs = (P(("parts", "dp"), None), P(("parts", "dp"), None), P(("parts", "dp"), "tensor"))
    return jax.shard_map(
        per_device, mesh=mesh, in_specs=in_specs, out_specs=out_specs, check_vma=False
    )
```

```python
import jax
import jax.numpy as jnp
from jax import lax
from jax.experimental import pallas as pl
from jax.experimental.pallas import tpu as pltpu
from jax.sharding import PartitionSpec as P

D = 8192
HD = 128
HQ = 8
TOK_DEV = 128
BLOCK = 16


def rotary(positions):
    half = HD // 2
    freq = jnp.exp(-jnp.log(500000.0) * jnp.arange(half, dtype=jnp.float32) * 2.0 / HD)
    angle = positions.astype(jnp.float32)[:, None] * freq[None, :]
    return (jnp.cos(angle), jnp.sin(angle))


def rotate(block, cosine, sine):
    half = HD // 2
    if block.ndim == 3:
        cosine = cosine[:, None, :]
        sine = sine[:, None, :]
    first = block[..., :half]
    second = block[..., half:]
    return jnp.concatenate(
        [first * cosine - second * sine, second * cosine + first * sine], axis=-1
    )


def members(lengths, count):
    ends = jnp.cumsum(lengths)
    starts = ends - lengths
    place = jnp.arange(count, dtype=jnp.int32)
    member = (place[:, None] >= starts[None, :]) & (place[:, None] < ends[None, :])
    return (member, place[:, None] - starts[None, :])


def positions_of(lengths, prefix, count):
    member, within = members(lengths, count)
    which = jnp.arange(lengths.shape[0], dtype=jnp.int32)
    sequence = jnp.sum(jnp.where(member, which[None, :], 0), axis=1)
    position = jnp.sum(jnp.where(member, prefix[None, :] + within, 0), axis=1)
    return (sequence, position)


def pick_of(column, slot, count):
    member, within = members(column, count)
    source = jnp.arange(column.shape[0], dtype=jnp.int32)
    index = jnp.sum(jnp.where(member, source[None, :] * slot + within, 0), axis=1)
    slots = jnp.arange(column.shape[0] * slot, dtype=jnp.int32)
    return (index[:, None] == slots[None, :]).astype(jnp.bfloat16)


def attend(queries, keys, values, allowed):
    scores = jnp.einsum(
        "qhd,kd->hqk", queries, keys, preferred_element_type=jnp.float32
    ) / jnp.sqrt(jnp.float32(HD))
    scores = jnp.where(allowed[None, :, :], scores, jnp.float32(-1e30))
    top = jnp.max(scores, axis=-1, keepdims=True)
    expo = jnp.exp(scores - top)
    weights = (expo / jnp.sum(expo, axis=-1, keepdims=True)).astype(jnp.bfloat16)
    out = jnp.einsum("hqk,kd->qhd", weights, values, preferred_element_type=jnp.float32)
    return out.astype(jnp.bfloat16)


def scale_of(rows):
    wide = rows.astype(jnp.float32)
    total = lax.psum(jnp.sum(wide * wide, axis=1), "tensor")
    return lax.rsqrt(total / D + 1e-05)


def scaled(rows, scale, norm_gain):
    return (rows.astype(jnp.float32) * scale[:, None] * norm_gain[None, :]).astype(jnp.bfloat16)


def product(rows, columns):
    return lax.dot_general(
        rows, columns, (((1,), (1,)), ((), ())), preferred_element_type=jnp.float32
    )


def cut(partial, width, core):
    share = width // lax.axis_size("tensor")
    mine = lax.dynamic_slice_in_dim(partial, core * share, share, 1)
    return jnp.concatenate([mine, partial[:, width:]], axis=1)


def sum_cores(partial):
    width = HQ * HD * partial.shape[1] // (HQ * HD + 2 * HD)
    core = lax.axis_index("tensor")
    other = lax.ppermute(cut(partial, width, 1 - core), "tensor", [(0, 1), (1, 0)])
    return (cut(partial, width, core) + other).astype(jnp.bfloat16)


def over(block, low, high):
    return lax.ppermute(block, "dp", [(i, i ^ 1) for i in range(2 * low, 2 * high)])


def along(block, low, high, step):
    return lax.ppermute(block, "dp", [(i, i + 2 * step) for i in range(2 * low, 2 * high)])


def gather_line(mine):
    own = (mine, over(mine, 0, 4))
    up1 = along(mine, 0, 3, 1)
    down1 = along(mine, 1, 4, -1)
    up2 = along(up1, 1, 3, 1)
    down2 = along(down1, 1, 3, -1)
    up1 = (up1, over(up1, 1, 4))
    down1 = (down1, over(down1, 0, 3))
    up3 = along(up2, 2, 3, 1)
    down3 = along(down2, 1, 2, -1)
    up2 = (up2, over(up2, 2, 4))
    down2 = (down2, over(down2, 0, 2))
    up3 = (up3, over(up3, 3, 4))
    down3 = (down3, over(down3, 0, 1))
    return own + up1 + down1 + up2 + down2, up3 + down3


def early_kernel(at, *refs):
    pieces, rows, out, whole, sems = refs[:10], refs[10:12], refs[12], refs[13], refs[14]
    z, x, part = at[0], at[1], at[2]
    size = pieces[0].shape[0]

    def copies(k, place):
        found = []
        for side in range(2):
            where = x if side == 0 else 1 - x
            start = pl.multiple_of((2 * place + where) * size, BLOCK)
            found.append(
                pltpu.make_async_copy(
                    pieces[2 * k + side], whole.at[pl.ds(start, size)], sems.at[2 * k + side]
                )
            )
        return found

    always = copies(0, z) + copies(1, (z + 3) % 4) + copies(2, (z + 1) % 4)
    from_low = copies(3, (z + 2) % 4)
    from_high = copies(4, (z + 2) % 4)
    for copy in always:
        copy.start()

    @pl.when(z >= 2)
    def _():
        for copy in from_low:
            copy.start()
        for copy in from_low:
            copy.wait()

    @pl.when(z < 2)
    def _():
        for copy in from_high:
            copy.start()
        for copy in from_high:
            copy.wait()

    for copy in always:
        copy.wait()
    count = rows[0].shape[0]
    for k in range(2):
        index = part if k == 0 else 1 - part
        start = pl.multiple_of(index * count, count)
        for low in range(0, whole.shape[0], 256):
            high = min(low + 256, whole.shape[0])
            out[pl.ds(start, count), low:high] = product(rows[k][...], whole[low:high, :])


def late_kernel(at, first, up, up_over, down, down_over, own, theirs, keep, send, last, sums, sems):
    z, x, part, core = at[0], at[1], at[2], at[3]
    size = up.shape[0]
    count = own.shape[0]
    width = first.shape[1]
    heads = width * HQ // (HQ + 2)
    share = heads // 2
    edge = 2 * size
    span = 256

    def finish(piece, piece_over, offset, low):
        found = []
        for side, ref in ((0, piece), (1, piece_over)):
            where = x if side == 0 else 1 - x
            start = pl.multiple_of(offset + where * size, BLOCK)
            found.append(
                pltpu.make_async_copy(ref, last.at[pl.ds(start, size)], sems.at[side])
            )
        for copy in found:
            copy.start()
        for copy in found:
            copy.wait()
        column = lax.broadcasted_iota(jnp.int32, (count, span), 1)
        new = (column >= offset) & (column < offset + edge)
        for k, rows in ((0, own), (1, theirs)):
            index = part if k == 0 else 1 - part
            start = pl.multiple_of(index * count, count)
            block = product(rows[...], last[...])
            old = first[pl.ds(start, count), low : low + span]
            sums[pl.ds(start, count), :] = jnp.where(new, block, old)

    for t in range(2):

        @pl.when(core == t)
        def _():
            for ref, c in ((keep, t), (send, 1 - t)):
                ref[:, :share] = first[:, c * share : (c + 1) * share]
                ref[:, share:] = first[:, heads:]

    @pl.when(z == 0)
    def _():
        low = width - span
        finish(down, down_over, span - edge, low)
        for t in range(2):

            @pl.when(core == t)
            def _():
                for ref, c in ((keep, t), (send, 1 - t)):
                    if c == 1:
                        ref[:, share - (heads - low) : share] = sums[:, : heads - low]
                    ref[:, share:] = sums[:, heads - low :]

    @pl.when(z == 3)
    def _():
        finish(up, up_over, 0, 0)
        for t in range(2):

            @pl.when(core == t)
            def _():
                for ref, c in ((keep, t), (send, 1 - t)):
                    if c == 0:
                        ref[:, :share] = sums[...]


def paired(sent_rows, norm_gain, qkv_weight, groups):
    part = lax.axis_index("parts")
    group = lax.axis_index("dp")
    at = jnp.stack([group // 2, group % 2, part, lax.axis_index("tensor")]).astype(jnp.int32)
    turned = qkv_weight.T
    depth = turned.shape[1]
    count = turned.shape[0] // (2 * BLOCK)
    size = count * BLOCK
    mine = lax.dynamic_index_in_dim(
        turned.reshape(count, 2, BLOCK, depth), part, 1, False
    ).reshape(size, depth)
    swap = [(0, 1), (1, 0)]
    raw = lax.ppermute(sent_rows, "parts", swap)
    scale = scale_of(sent_rows)
    normed = scaled(sent_rows, scale, norm_gain)
    theirs = scaled(raw, lax.ppermute(scale, "parts", swap), norm_gain)
    early, late = gather_line(mine)
    slots = sent_rows.shape[0]
    width = groups * size
    whole = pl.BlockSpec(memory_space=pltpu.VMEM)
    anywhere = pl.BlockSpec(memory_space=pl.ANY)
    scalars = pl.BlockSpec(memory_space=pltpu.SMEM)
    first = pl.pallas_call(
        early_kernel,
        out_shape=jax.ShapeDtypeStruct((2 * slots, width), jnp.float32),
        in_specs=[scalars] + [anywhere] * 10 + [whole] * 2,
        out_specs=whole,
        scratch_shapes=[
            pltpu.VMEM((width, depth), jnp.bfloat16),
            pltpu.SemaphoreType.DMA((10,)),
        ],
        compiler_params=pltpu.CompilerParams(vmem_limit_bytes=24 << 20),
        cost_estimate=pl.CostEstimate(
            flops=4 * slots * width * depth, bytes_accessed=12 << 20, transcendentals=0
        ),
        name="project_early",
    )(at, *early, normed, theirs)
    share = width * HQ // (HQ + 2) // 2 + width * 2 // (HQ + 2)
    half = jax.ShapeDtypeStruct((2 * slots, share), jnp.float32)
    keep, send = pl.pallas_call(
        late_kernel,
        out_shape=(half, half),
        in_specs=[scalars, whole] + [anywhere] * 4 + [whole] * 2,
        out_specs=(whole, whole),
        scratch_shapes=[
            pltpu.VMEM((256, depth), jnp.bfloat16),
            pltpu.VMEM((2 * slots, 256), jnp.float32),
            pltpu.SemaphoreType.DMA((2,)),
        ],
        compiler_params=pltpu.CompilerParams(vmem_limit_bytes=24 << 20),
        cost_estimate=pl.CostEstimate(
            flops=4 * slots * 256 * depth, bytes_accessed=8 << 20, transcendentals=0
        ),
        name="project_late",
    )(at, first, *late, normed, theirs)
    ready = (keep + lax.ppermute(send, "tensor", swap)).astype(jnp.bfloat16)
    arrived = lax.all_to_all(ready, ("parts", "dp"), 0, 0, tiled=True)
    return arrived.reshape(2, slots, share)


def single(sent_rows, norm_gain, qkv_weight):
    columns = lax.all_gather(qkv_weight.T, "dp", axis=0, tiled=True)
    ready = sum_cores(product(scaled(sent_rows, scale_of(sent_rows), norm_gain), columns))
    return lax.all_to_all(ready, "dp", 0, 0, tiled=True)[None]


def per_device(sent_rows, norm_gain, qkv_weight, route_counts, response_lengths, prefix_lengths):
    groups = lax.axis_size("dp")
    slot = sent_rows.shape[0] // groups
    column = lax.dynamic_slice_in_dim(route_counts, lax.axis_index("dp"), 1, 1)[:, 0]
    pick = pick_of(column, slot, TOK_DEV)
    sequence, position = positions_of(response_lengths[0], prefix_lengths[0], TOK_DEV)
    allowed = (sequence[:, None] == sequence[None, :]) & (position[None, :] <= position[:, None])
    cosine, sine = rotary(position)
    if lax.axis_size("parts") == 2 and groups == 8 and qkv_weight.shape[1] == 160:
        arrived = paired(sent_rows, norm_gain, qkv_weight, groups)
    else:
        arrived = single(sent_rows, norm_gain, qkv_weight)
    planes, _, width = arrived.shape
    heads = width * planes // HD
    packed = jnp.einsum("qs,psc->qpc", pick, arrived, preferred_element_type=jnp.float32)
    if planes == 2:
        packed = packed.reshape(TOK_DEV, 2, width // BLOCK, BLOCK).transpose(0, 2, 1, 3)
    packed = packed.reshape(TOK_DEV, heads, HD)
    queries = rotate(packed[:, :-2], cosine, sine).astype(jnp.bfloat16)
    new_keys = rotate(packed[:, -2], cosine, sine).astype(jnp.bfloat16)
    new_values = packed[:, -1].astype(jnp.bfloat16)
    out = attend(queries, new_keys, new_values, allowed)
    return (new_keys, new_values, out.reshape(TOK_DEV, (heads - 2) * HD))


def solution(mesh):
    in_specs = (
        P(("parts", "dp"), "tensor"),
        P("tensor"),
        P("tensor", "dp"),
        P("parts", None),
        P(("parts", "dp"), None),
        P(("parts", "dp"), None),
    )
    out_specs = (P(("parts", "dp"), None), P(("parts", "dp"), None), P(("parts", "dp"), "tensor"))
    return jax.shard_map(
        per_device, mesh=mesh, in_specs=in_specs, out_specs=out_specs, check_vma=False
    )
```

```python
import math

import jax
import jax.numpy as jnp
from jax import lax
from jax.experimental import pallas as pl
from jax.experimental.pallas import tpu as pltpu
from jax.sharding import PartitionSpec as P

D = 8192
HD = 128
HQ = 8
TOK_DEV = 128
BLOCK = 16


def rotary(positions):
    half = HD // 2
    freq = jnp.exp(-jnp.log(500000.0) * jnp.arange(half, dtype=jnp.float32) * 2.0 / HD)
    angle = positions.astype(jnp.float32)[:, None] * freq[None, :]
    return (jnp.cos(angle), jnp.sin(angle))


def rotate(block, cosine, sine):
    half = HD // 2
    if block.ndim == 3:
        cosine = cosine[:, None, :]
        sine = sine[:, None, :]
    first = block[..., :half]
    second = block[..., half:]
    return jnp.concatenate(
        [first * cosine - second * sine, second * cosine + first * sine], axis=-1
    )


def members(lengths, count):
    ends = jnp.cumsum(lengths)
    starts = ends - lengths
    place = jnp.arange(count, dtype=jnp.int32)
    member = (place[:, None] >= starts[None, :]) & (place[:, None] < ends[None, :])
    return (member, place[:, None] - starts[None, :])


def positions_of(lengths, prefix, count):
    member, within = members(lengths, count)
    which = jnp.arange(lengths.shape[0], dtype=jnp.int32)
    sequence = jnp.sum(jnp.where(member, which[None, :], 0), axis=1)
    position = jnp.sum(jnp.where(member, prefix[None, :] + within, 0), axis=1)
    return (sequence, position)


def pick_of(column, slot, count):
    member, within = members(column, count)
    source = jnp.arange(column.shape[0], dtype=jnp.int32)
    index = jnp.sum(jnp.where(member, source[None, :] * slot + within, 0), axis=1)
    slots = jnp.arange(column.shape[0] * slot, dtype=jnp.int32)
    return (index[:, None] == slots[None, :]).astype(jnp.bfloat16)


def attend(queries, keys, values, allowed):
    scores = jnp.einsum(
        "qhd,kd->hqk", queries, keys, preferred_element_type=jnp.float32
    ) / jnp.sqrt(jnp.float32(HD))
    scores = jnp.where(allowed[None, :, :], scores, jnp.float32(-1e30))
    top = jnp.max(scores, axis=-1, keepdims=True)
    expo = jnp.exp(scores - top)
    weights = (expo / jnp.sum(expo, axis=-1, keepdims=True)).astype(jnp.bfloat16)
    out = jnp.einsum("hqk,kd->qhd", weights, values, preferred_element_type=jnp.float32)
    return out.astype(jnp.bfloat16)


def scale_of(rows):
    wide = rows.astype(jnp.float32)
    total = lax.psum(jnp.sum(wide * wide, axis=1), "tensor")
    return lax.rsqrt(total / D + 1e-05)


def scaled(rows, scale, norm_gain):
    return (rows.astype(jnp.float32) * scale[:, None] * norm_gain[None, :]).astype(jnp.bfloat16)


def product(rows, columns):
    return lax.dot_general(
        rows, columns, (((1,), (1,)), ((), ())), preferred_element_type=jnp.float32
    )


def cut(partial, width, core):
    share = width // lax.axis_size("tensor")
    mine = lax.dynamic_slice_in_dim(partial, core * share, share, 1)
    return jnp.concatenate([mine, partial[:, width:]], axis=1)


def sum_cores(partial):
    width = HQ * HD * partial.shape[1] // (HQ * HD + 2 * HD)
    core = lax.axis_index("tensor")
    other = lax.ppermute(cut(partial, width, 1 - core), "tensor", [(0, 1), (1, 0)])
    return (cut(partial, width, core) + other).astype(jnp.bfloat16)


def over(block, low, high):
    return lax.ppermute(block, "dp", [(i, i ^ 1) for i in range(2 * low, 2 * high)])


def along(block, low, high, step):
    return lax.ppermute(block, "dp", [(i, i + 2 * step) for i in range(2 * low, 2 * high)])


def gather_line(mine):
    up1 = along(mine, 0, 3, 1)
    down1 = along(mine, 1, 4, -1)
    mine, side, up1, down1 = lax.optimization_barrier((mine, over(mine, 0, 4), up1, down1))
    own = (mine, side)
    up2 = along(up1, 1, 3, 1)
    down2 = along(down1, 1, 3, -1)
    up1 = (up1, over(up1, 1, 4))
    down1 = (down1, over(down1, 0, 3))
    up3 = along(up2, 2, 3, 1)
    down3 = along(down2, 1, 2, -1)
    up2 = (up2, over(up2, 2, 4))
    down2 = (down2, over(down2, 0, 2))
    up3 = (up3, over(up3, 3, 4))
    down3 = (down3, over(down3, 0, 1))
    return own + up1 + down1 + up2 + down2, up3 + down3


def early_kernel(at, *refs):
    pieces, rows, out, whole, sems = refs[:10], refs[10:12], refs[12], refs[13], refs[14]
    z, x, part = at[0], at[1], at[2]
    size = pieces[0].shape[0]

    def copies(k, place):
        found = []
        for side in range(2):
            where = x if side == 0 else 1 - x
            start = pl.multiple_of((2 * place + where) * size, BLOCK)
            found.append(
                pltpu.make_async_copy(
                    pieces[2 * k + side], whole.at[pl.ds(start, size)], sems.at[2 * k + side]
                )
            )
        return found

    always = copies(0, z) + copies(1, (z + 3) % 4) + copies(2, (z + 1) % 4)
    from_low = copies(3, (z + 2) % 4)
    from_high = copies(4, (z + 2) % 4)
    for copy in always:
        copy.start()

    @pl.when(z >= 2)
    def _():
        for copy in from_low:
            copy.start()
        for copy in from_low:
            copy.wait()

    @pl.when(z < 2)
    def _():
        for copy in from_high:
            copy.start()
        for copy in from_high:
            copy.wait()

    for copy in always:
        copy.wait()
    count = rows[0].shape[0]
    for k in range(2):
        index = part if k == 0 else 1 - part
        start = pl.multiple_of(index * count, count)
        for low in range(0, whole.shape[0], 256):
            high = min(low + 256, whole.shape[0])
            out[pl.ds(start, count), low:high] = product(rows[k][...], whole[low:high, :])


def late_kernel(at, first, up, up_over, down, down_over, own, theirs, keep, send, last, sums, sems):
    z, x, part, core = at[0], at[1], at[2], at[3]
    size = up.shape[0]
    count = own.shape[0]
    width = first.shape[1]
    heads = width * HQ // (HQ + 2)
    share = heads // 2
    edge = 2 * size
    span = 256

    def finish(piece, piece_over, offset, low):
        found = []
        for side, ref in ((0, piece), (1, piece_over)):
            where = x if side == 0 else 1 - x
            start = pl.multiple_of(offset + where * size, BLOCK)
            found.append(
                pltpu.make_async_copy(ref, last.at[pl.ds(start, size)], sems.at[side])
            )
        for copy in found:
            copy.start()
        for copy in found:
            copy.wait()
        column = lax.broadcasted_iota(jnp.int32, (count, span), 1)
        new = (column >= offset) & (column < offset + edge)
        for k, rows in ((0, own), (1, theirs)):
            index = part if k == 0 else 1 - part
            start = pl.multiple_of(index * count, count)
            block = product(rows[...], last[...])
            old = first[pl.ds(start, count), low : low + span]
            sums[pl.ds(start, count), :] = jnp.where(new, block, old)

    for t in range(2):

        @pl.when(core == t)
        def _():
            for ref, c in ((keep, t), (send, 1 - t)):
                ref[:, :share] = first[:, c * share : (c + 1) * share]
                ref[:, share:] = first[:, heads:]

    @pl.when(z == 0)
    def _():
        low = width - span
        finish(down, down_over, span - edge, low)
        for t in range(2):

            @pl.when(core == t)
            def _():
                for ref, c in ((keep, t), (send, 1 - t)):
                    if c == 1:
                        ref[:, share - (heads - low) : share] = sums[:, : heads - low]
                    ref[:, share:] = sums[:, heads - low :]

    @pl.when(z == 3)
    def _():
        finish(up, up_over, 0, 0)
        for t in range(2):

            @pl.when(core == t)
            def _():
                for ref, c in ((keep, t), (send, 1 - t)):
                    if c == 0:
                        ref[:, :share] = sums[...]


def sum_kernel(keep, other, out):
    out[...] = (keep[...] + other[...]).astype(out.dtype)


def finish_kernel(pick, arrived, cosine, sine, allowed, keys, values, out):
    width = arrived.shape[2]
    count = 2 * width // HD
    chosen = pick[...]
    planes = [
        jnp.dot(chosen, arrived[y], preferred_element_type=jnp.float32).astype(jnp.bfloat16)
        for y in range(2)
    ]
    source = lax.broadcasted_iota(jnp.int32, (HD, 2 * HD), 0)
    target = lax.broadcasted_iota(jnp.int32, (HD, 2 * HD), 1)
    heads = []
    for pair in range(count // 2):
        total = None
        for y in range(2):
            place = source // BLOCK * (2 * BLOCK) + y * BLOCK + source % BLOCK
            order = (place == target).astype(jnp.float32).astype(jnp.bfloat16)
            part = jnp.dot(
                planes[y][:, pair * HD : (pair + 1) * HD],
                order,
                preferred_element_type=jnp.float32,
            )
            total = part if total is None else total + part
        heads += [total[:, :HD], total[:, HD:]]

    def turn(block):
        other = pltpu.roll(block, HD // 2, 1)
        return (block * cosine[...] + other * sine[...]).astype(jnp.bfloat16)

    key = turn(heads[-2])
    value = heads[-1].astype(jnp.bfloat16)
    keys[...] = key
    values[...] = value
    mask = allowed[...] > 0
    for h in range(count - 2):
        scores = product(turn(heads[h]), key) / math.sqrt(HD)
        scores = jnp.where(mask, scores, jnp.float32(-1e30))
        expo = jnp.exp(scores - jnp.max(scores, axis=-1, keepdims=True))
        weights = (expo / jnp.sum(expo, axis=-1, keepdims=True)).astype(jnp.bfloat16)
        out[:, h * HD : (h + 1) * HD] = jnp.dot(
            weights, value, preferred_element_type=jnp.float32
        ).astype(out.dtype)


def finish(pick, arrived, cosine, sine, allowed):
    whole = pl.BlockSpec(memory_space=pltpu.VMEM)
    heads = 2 * arrived.shape[2] // HD - 2
    single = jax.ShapeDtypeStruct((TOK_DEV, HD), jnp.bfloat16)
    return pl.pallas_call(
        finish_kernel,
        out_shape=(single, single, jax.ShapeDtypeStruct((TOK_DEV, heads * HD), jnp.bfloat16)),
        in_specs=[whole] * 5,
        out_specs=(whole,) * 3,
        name="attend",
    )(
        pick,
        arrived,
        jnp.concatenate([cosine, cosine], axis=1),
        jnp.concatenate([-sine, sine], axis=1),
        allowed.astype(jnp.float32),
    )


def paired(sent_rows, norm_gain, qkv_weight, groups):
    part = lax.axis_index("parts")
    group = lax.axis_index("dp")
    at = jnp.stack([group // 2, group % 2, part, lax.axis_index("tensor")]).astype(jnp.int32)
    turned = qkv_weight.T
    depth = turned.shape[1]
    count = turned.shape[0] // (2 * BLOCK)
    size = count * BLOCK
    mine = lax.dynamic_index_in_dim(
        turned.reshape(count, 2, BLOCK, depth), part, 1, False
    ).reshape(size, depth)
    swap = [(0, 1), (1, 0)]
    normed = scaled(sent_rows, scale_of(sent_rows), norm_gain)
    theirs = lax.ppermute(normed, "parts", swap)
    early, late = gather_line(mine)
    slots = sent_rows.shape[0]
    width = groups * size
    whole = pl.BlockSpec(memory_space=pltpu.VMEM)
    anywhere = pl.BlockSpec(memory_space=pl.ANY)
    scalars = pl.BlockSpec(memory_space=pltpu.SMEM)
    first = pl.pallas_call(
        early_kernel,
        out_shape=jax.ShapeDtypeStruct((2 * slots, width), jnp.float32),
        in_specs=[scalars] + [anywhere] * 10 + [whole] * 2,
        out_specs=whole,
        scratch_shapes=[
            pltpu.VMEM((width, depth), jnp.bfloat16),
            pltpu.SemaphoreType.DMA((10,)),
        ],
        compiler_params=pltpu.CompilerParams(vmem_limit_bytes=24 << 20),
        cost_estimate=pl.CostEstimate(
            flops=4 * slots * width * depth, bytes_accessed=12 << 20, transcendentals=0
        ),
        name="project_early",
    )(at, *early, normed, theirs)
    share = width * HQ // (HQ + 2) // 2 + width * 2 // (HQ + 2)
    half = jax.ShapeDtypeStruct((2 * slots, share), jnp.float32)
    keep, send = pl.pallas_call(
        late_kernel,
        out_shape=(half, half),
        in_specs=[scalars, whole] + [anywhere] * 4 + [whole] * 2,
        out_specs=(whole, whole),
        scratch_shapes=[
            pltpu.VMEM((256, depth), jnp.bfloat16),
            pltpu.VMEM((2 * slots, 256), jnp.float32),
            pltpu.SemaphoreType.DMA((2,)),
        ],
        compiler_params=pltpu.CompilerParams(vmem_limit_bytes=24 << 20),
        cost_estimate=pl.CostEstimate(
            flops=4 * slots * 256 * depth, bytes_accessed=8 << 20, transcendentals=0
        ),
        name="project_late",
    )(at, first, *late, normed, theirs)
    ready = pl.pallas_call(
        sum_kernel,
        out_shape=jax.ShapeDtypeStruct(keep.shape, jnp.bfloat16),
        in_specs=[whole, whole],
        out_specs=whole,
        name="sum_halves",
    )(keep, lax.ppermute(send, "tensor", swap))
    arrived = lax.all_to_all(ready, ("parts", "dp"), 0, 0, tiled=True)
    return arrived.reshape(2, slots, share)


def single(sent_rows, norm_gain, qkv_weight):
    columns = lax.all_gather(qkv_weight.T, "dp", axis=0, tiled=True)
    ready = sum_cores(product(scaled(sent_rows, scale_of(sent_rows), norm_gain), columns))
    return lax.all_to_all(ready, "dp", 0, 0, tiled=True)


def per_device(sent_rows, norm_gain, qkv_weight, route_counts, response_lengths, prefix_lengths):
    groups = lax.axis_size("dp")
    slot = sent_rows.shape[0] // groups
    column = lax.dynamic_slice_in_dim(route_counts, lax.axis_index("dp"), 1, 1)[:, 0]
    pick = pick_of(column, slot, TOK_DEV)
    sequence, position = positions_of(response_lengths[0], prefix_lengths[0], TOK_DEV)
    allowed = (sequence[:, None] == sequence[None, :]) & (position[None, :] <= position[:, None])
    cosine, sine = rotary(position)
    if lax.axis_size("parts") == 2 and groups == 8 and qkv_weight.shape[1] == 160:
        arrived = paired(sent_rows, norm_gain, qkv_weight, groups)
        return finish(pick, arrived, cosine, sine, allowed)
    arrived = single(sent_rows, norm_gain, qkv_weight)
    heads = arrived.shape[1] // HD
    packed = jnp.dot(pick, arrived, preferred_element_type=jnp.float32)
    packed = packed.reshape(TOK_DEV, heads, HD)
    queries = rotate(packed[:, :-2], cosine, sine).astype(jnp.bfloat16)
    new_keys = rotate(packed[:, -2], cosine, sine).astype(jnp.bfloat16)
    new_values = packed[:, -1].astype(jnp.bfloat16)
    out = attend(queries, new_keys, new_values, allowed)
    return (new_keys, new_values, out.reshape(TOK_DEV, (heads - 2) * HD))


def solution(mesh):
    in_specs = (
        P(("parts", "dp"), "tensor"),
        P("tensor"),
        P("tensor", "dp"),
        P("parts", None),
        P(("parts", "dp"), None),
        P(("parts", "dp"), None),
    )
    out_specs = (P(("parts", "dp"), None), P(("parts", "dp"), None), P(("parts", "dp"), "tensor"))
    return jax.shard_map(
        per_device, mesh=mesh, in_specs=in_specs, out_specs=out_specs, check_vma=False
    )
```

```python
import math

import jax
import jax.numpy as jnp
from jax import lax
from jax.experimental import pallas as pl
from jax.experimental.pallas import tpu as pltpu
from jax.sharding import PartitionSpec as P

D = 8192
HD = 128
HQ = 8
TOK_DEV = 128
BLOCK = 16


def rotary(positions):
    half = HD // 2
    freq = jnp.exp(-jnp.log(500000.0) * jnp.arange(half, dtype=jnp.float32) * 2.0 / HD)
    angle = positions.astype(jnp.float32)[:, None] * freq[None, :]
    return (jnp.cos(angle), jnp.sin(angle))


def rotate(block, cosine, sine):
    half = HD // 2
    if block.ndim == 3:
        cosine = cosine[:, None, :]
        sine = sine[:, None, :]
    first = block[..., :half]
    second = block[..., half:]
    return jnp.concatenate(
        [first * cosine - second * sine, second * cosine + first * sine], axis=-1
    )


def members(lengths, count):
    ends = jnp.cumsum(lengths)
    starts = ends - lengths
    place = jnp.arange(count, dtype=jnp.int32)
    member = (place[:, None] >= starts[None, :]) & (place[:, None] < ends[None, :])
    return (member, place[:, None] - starts[None, :])


def positions_of(lengths, prefix, count):
    member, within = members(lengths, count)
    which = jnp.arange(lengths.shape[0], dtype=jnp.int32)
    sequence = jnp.sum(jnp.where(member, which[None, :], 0), axis=1)
    position = jnp.sum(jnp.where(member, prefix[None, :] + within, 0), axis=1)
    return (sequence, position)


def pick_of(column, slot, count):
    member, within = members(column, count)
    source = jnp.arange(column.shape[0], dtype=jnp.int32)
    index = jnp.sum(jnp.where(member, source[None, :] * slot + within, 0), axis=1)
    slots = jnp.arange(column.shape[0] * slot, dtype=jnp.int32)
    return (index[:, None] == slots[None, :]).astype(jnp.bfloat16)


def attend(queries, keys, values, allowed):
    scores = jnp.einsum(
        "qhd,kd->hqk", queries, keys, preferred_element_type=jnp.float32
    ) / jnp.sqrt(jnp.float32(HD))
    scores = jnp.where(allowed[None, :, :], scores, jnp.float32(-1e30))
    top = jnp.max(scores, axis=-1, keepdims=True)
    expo = jnp.exp(scores - top)
    weights = (expo / jnp.sum(expo, axis=-1, keepdims=True)).astype(jnp.bfloat16)
    out = jnp.einsum("hqk,kd->qhd", weights, values, preferred_element_type=jnp.float32)
    return out.astype(jnp.bfloat16)


def scale_of(rows):
    wide = rows.astype(jnp.float32)
    total = lax.psum(jnp.sum(wide * wide, axis=1), "tensor")
    return lax.rsqrt(total / D + 1e-05)


def scaled(rows, scale, norm_gain):
    return (rows.astype(jnp.float32) * scale[:, None] * norm_gain[None, :]).astype(jnp.bfloat16)


def product(rows, columns):
    return lax.dot_general(
        rows, columns, (((1,), (1,)), ((), ())), preferred_element_type=jnp.float32
    )


def cut(partial, width, core):
    share = width // lax.axis_size("tensor")
    mine = lax.dynamic_slice_in_dim(partial, core * share, share, 1)
    return jnp.concatenate([mine, partial[:, width:]], axis=1)


def sum_cores(partial):
    width = HQ * HD * partial.shape[1] // (HQ * HD + 2 * HD)
    core = lax.axis_index("tensor")
    other = lax.ppermute(cut(partial, width, 1 - core), "tensor", [(0, 1), (1, 0)])
    return (cut(partial, width, core) + other).astype(jnp.bfloat16)


def over(block, places):
    return lax.ppermute(block, "dp", [(2 * z + x, 2 * z + 1 - x) for z in places for x in range(2)])


def along(block, moves):
    return lax.ppermute(block, "dp", [(2 * a + x, 2 * b + x) for a, b in moves for x in range(2)])


PAIRS = ((0, 1), (1, 0), (2, 3), (3, 2))
ACROSS = ((1, 2), (2, 1))
OUTWARD = ((1, 0), (2, 3))


def gather_line(mine, at_end, normed):
    everywhere = range(4)
    near = along(mine, PAIRS)
    middle = along(mine, ACROSS)
    side, near, middle, _ = lax.optimization_barrier(
        (over(mine, everywhere), near, middle, normed)
    )
    far = along(near, ACROSS)
    second = along(jnp.where(at_end, side, middle), PAIRS)
    first_over = over(jnp.where(at_end, near, middle), everywhere)
    last = along(far, OUTWARD)
    second_over = over(jnp.where(at_end, second, far), everywhere)
    last_over = over(last, (0, 3))
    early = (mine, side, near, middle, far, second, first_over, second_over)
    return early, (last, last_over)


def early_kernel(
    at, mine, side, near, middle, far, second, first_over, second_over, own, theirs, out, whole, sems
):
    z, x, part = at[0], at[1], at[2]
    size = mine.shape[0]

    def place(pairs):
        found = []
        for k, (where, pieces) in enumerate(pairs):
            for j, piece in enumerate(pieces):
                column = x if j == 0 else 1 - x
                start = pl.multiple_of((2 * where + column) * size, BLOCK)
                found.append(
                    pltpu.make_async_copy(
                        piece, whole.at[pl.ds(start, size)], sems.at[2 * k + j]
                    )
                )
        for copy in found:
            copy.start()
        for copy in found:
            copy.wait()

    at_end = (z == 0) | (z == 3)
    pair = z + 1 - 2 * (z % 2)

    @pl.when(at_end)
    def _():
        place(
            (
                (z, (mine, side)),
                (pair, (near, first_over)),
                ((z + 2) % 4, (second, second_over)),
                (3 - z, (mine, side)),
            )
        )

    @pl.when(jnp.logical_not(at_end))
    def _():
        place(
            (
                (z, (mine, side)),
                (pair, (near, second)),
                ((z + 2) % 4, (far, second_over)),
                (3 - z, (middle, first_over)),
            )
        )

    count = own.shape[0]
    for k, rows in ((0, own), (1, theirs)):
        index = part if k == 0 else 1 - part
        start = pl.multiple_of(index * count, count)
        for low in range(0, whole.shape[0], 256):
            high = min(low + 256, whole.shape[0])
            out[pl.ds(start, count), low:high] = product(rows[...], whole[low:high, :])


def late_kernel(at, first, piece, piece_over, own, theirs, keep, send, last, sums, sems):
    z, x, part, core = at[0], at[1], at[2], at[3]
    size = piece.shape[0]
    count = own.shape[0]
    width = first.shape[1]
    heads = width * HQ // (HQ + 2)
    share = heads // 2
    edge = 2 * size
    span = 256

    def complete(offset, low):
        found = []
        for side, ref in ((0, piece), (1, piece_over)):
            where = x if side == 0 else 1 - x
            start = pl.multiple_of(offset + where * size, BLOCK)
            found.append(
                pltpu.make_async_copy(ref, last.at[pl.ds(start, size)], sems.at[side])
            )
        for copy in found:
            copy.start()
        for copy in found:
            copy.wait()
        column = lax.broadcasted_iota(jnp.int32, (count, span), 1)
        new = (column >= offset) & (column < offset + edge)
        for k, rows in ((0, own), (1, theirs)):
            index = part if k == 0 else 1 - part
            start = pl.multiple_of(index * count, count)
            block = product(rows[...], last[...])
            old = first[pl.ds(start, count), low : low + span]
            sums[pl.ds(start, count), :] = jnp.where(new, block, old)

    for t in range(2):

        @pl.when(core == t)
        def _():
            for ref, c in ((keep, t), (send, 1 - t)):
                ref[:, :share] = first[:, c * share : (c + 1) * share]
                ref[:, share:] = first[:, heads:]

    @pl.when(z == 0)
    def _():
        low = width - span
        complete(span - edge, low)
        for t in range(2):

            @pl.when(core == t)
            def _():
                for ref, c in ((keep, t), (send, 1 - t)):
                    if c == 1:
                        ref[:, share - (heads - low) : share] = sums[:, : heads - low]
                    ref[:, share:] = sums[:, heads - low :]

    @pl.when(z == 3)
    def _():
        complete(0, 0)
        for t in range(2):

            @pl.when(core == t)
            def _():
                for ref, c in ((keep, t), (send, 1 - t)):
                    if c == 0:
                        ref[:, :share] = sums[...]


def sum_kernel(keep, other, out):
    out[...] = (keep[...] + other[...]).astype(out.dtype)


def finish_kernel(pick, arrived, cosine, sine, allowed, keys, values, out):
    width = arrived.shape[2]
    count = 2 * width // HD
    chosen = pick[...]
    planes = [
        jnp.dot(chosen, arrived[y], preferred_element_type=jnp.float32).astype(jnp.bfloat16)
        for y in range(2)
    ]
    source = lax.broadcasted_iota(jnp.int32, (HD, 2 * HD), 0)
    target = lax.broadcasted_iota(jnp.int32, (HD, 2 * HD), 1)
    heads = []
    for pair in range(count // 2):
        total = None
        for y in range(2):
            place = source // BLOCK * (2 * BLOCK) + y * BLOCK + source % BLOCK
            order = (place == target).astype(jnp.float32).astype(jnp.bfloat16)
            part = jnp.dot(
                planes[y][:, pair * HD : (pair + 1) * HD],
                order,
                preferred_element_type=jnp.float32,
            )
            total = part if total is None else total + part
        heads += [total[:, :HD], total[:, HD:]]

    def turn(block):
        other = pltpu.roll(block, HD // 2, 1)
        return (block * cosine[...] + other * sine[...]).astype(jnp.bfloat16)

    key = turn(heads[-2])
    value = heads[-1].astype(jnp.bfloat16)
    keys[...] = key
    values[...] = value
    mask = allowed[...] > 0
    for h in range(count - 2):
        scores = product(turn(heads[h]), key) / math.sqrt(HD)
        scores = jnp.where(mask, scores, jnp.float32(-1e30))
        expo = jnp.exp(scores - jnp.max(scores, axis=-1, keepdims=True))
        weights = (expo / jnp.sum(expo, axis=-1, keepdims=True)).astype(jnp.bfloat16)
        out[:, h * HD : (h + 1) * HD] = jnp.dot(
            weights, value, preferred_element_type=jnp.float32
        ).astype(out.dtype)


def finish(pick, arrived, cosine, sine, allowed):
    whole = pl.BlockSpec(memory_space=pltpu.VMEM)
    heads = 2 * arrived.shape[2] // HD - 2
    single = jax.ShapeDtypeStruct((TOK_DEV, HD), jnp.bfloat16)
    return pl.pallas_call(
        finish_kernel,
        out_shape=(single, single, jax.ShapeDtypeStruct((TOK_DEV, heads * HD), jnp.bfloat16)),
        in_specs=[whole] * 5,
        out_specs=(whole,) * 3,
        compiler_params=pltpu.CompilerParams(vmem_limit_bytes=6 << 20),
        name="attend",
    )(
        pick,
        arrived,
        jnp.concatenate([cosine, cosine], axis=1),
        jnp.concatenate([-sine, sine], axis=1),
        allowed.astype(jnp.float32),
    )


def paired(sent_rows, norm_gain, qkv_weight, groups):
    part = lax.axis_index("parts")
    group = lax.axis_index("dp")
    at = jnp.stack([group // 2, group % 2, part, lax.axis_index("tensor")]).astype(jnp.int32)
    turned = qkv_weight.T
    depth = turned.shape[1]
    count = turned.shape[0] // (2 * BLOCK)
    size = count * BLOCK
    mine = lax.dynamic_index_in_dim(
        turned.reshape(count, 2, BLOCK, depth), part, 1, False
    ).reshape(size, depth)
    swap = [(0, 1), (1, 0)]
    normed = scaled(sent_rows, scale_of(sent_rows), norm_gain)
    theirs = lax.ppermute(normed, "parts", swap)
    at_end = (group < 2) | (group >= groups - 2)
    early, late = gather_line(mine, at_end, normed)
    slots = sent_rows.shape[0]
    width = groups * size
    whole = pl.BlockSpec(memory_space=pltpu.VMEM)
    anywhere = pl.BlockSpec(memory_space=pl.ANY)
    scalars = pl.BlockSpec(memory_space=pltpu.SMEM)
    first = pl.pallas_call(
        early_kernel,
        out_shape=jax.ShapeDtypeStruct((2 * slots, width), jnp.float32),
        in_specs=[scalars] + [anywhere] * 8 + [whole] * 2,
        out_specs=whole,
        scratch_shapes=[
            pltpu.VMEM((width, depth), jnp.bfloat16),
            pltpu.SemaphoreType.DMA((8,)),
        ],
        compiler_params=pltpu.CompilerParams(vmem_limit_bytes=24 << 20),
        cost_estimate=pl.CostEstimate(
            flops=4 * slots * width * depth, bytes_accessed=12 << 20, transcendentals=0
        ),
        name="project_early",
    )(at, *early, normed, theirs)
    share = width * HQ // (HQ + 2) // 2 + width * 2 // (HQ + 2)
    half = jax.ShapeDtypeStruct((2 * slots, share), jnp.float32)
    keep, send = pl.pallas_call(
        late_kernel,
        out_shape=(half, half),
        in_specs=[scalars, whole] + [anywhere] * 2 + [whole] * 2,
        out_specs=(whole, whole),
        scratch_shapes=[
            pltpu.VMEM((256, depth), jnp.bfloat16),
            pltpu.VMEM((2 * slots, 256), jnp.float32),
            pltpu.SemaphoreType.DMA((2,)),
        ],
        compiler_params=pltpu.CompilerParams(vmem_limit_bytes=24 << 20),
        cost_estimate=pl.CostEstimate(
            flops=4 * slots * 256 * depth, bytes_accessed=8 << 20, transcendentals=0
        ),
        name="project_late",
    )(at, first, *late, normed, theirs)
    ready = pl.pallas_call(
        sum_kernel,
        out_shape=jax.ShapeDtypeStruct(keep.shape, jnp.bfloat16),
        in_specs=[whole, whole],
        out_specs=whole,
        compiler_params=pltpu.CompilerParams(vmem_limit_bytes=6 << 20),
        name="sum_halves",
    )(keep, lax.ppermute(send, "tensor", swap))
    arrived = lax.all_to_all(ready, ("parts", "dp"), 0, 0, tiled=True)
    return arrived.reshape(2, slots, share)


def single(sent_rows, norm_gain, qkv_weight):
    columns = lax.all_gather(qkv_weight.T, "dp", axis=0, tiled=True)
    ready = sum_cores(product(scaled(sent_rows, scale_of(sent_rows), norm_gain), columns))
    return lax.all_to_all(ready, "dp", 0, 0, tiled=True)


def per_device(sent_rows, norm_gain, qkv_weight, route_counts, response_lengths, prefix_lengths):
    groups = lax.axis_size("dp")
    slot = sent_rows.shape[0] // groups
    column = lax.dynamic_slice_in_dim(route_counts, lax.axis_index("dp"), 1, 1)[:, 0]
    pick = pick_of(column, slot, TOK_DEV)
    sequence, position = positions_of(response_lengths[0], prefix_lengths[0], TOK_DEV)
    allowed = (sequence[:, None] == sequence[None, :]) & (position[None, :] <= position[:, None])
    cosine, sine = rotary(position)
    if lax.axis_size("parts") == 2 and groups == 8 and qkv_weight.shape[1] == 160:
        arrived = paired(sent_rows, norm_gain, qkv_weight, groups)
        return finish(pick, arrived, cosine, sine, allowed)
    arrived = single(sent_rows, norm_gain, qkv_weight)
    heads = arrived.shape[1] // HD
    packed = jnp.dot(pick, arrived, preferred_element_type=jnp.float32)
    packed = packed.reshape(TOK_DEV, heads, HD)
    queries = rotate(packed[:, :-2], cosine, sine).astype(jnp.bfloat16)
    new_keys = rotate(packed[:, -2], cosine, sine).astype(jnp.bfloat16)
    new_values = packed[:, -1].astype(jnp.bfloat16)
    out = attend(queries, new_keys, new_values, allowed)
    return (new_keys, new_values, out.reshape(TOK_DEV, (heads - 2) * HD))


def solution(mesh):
    in_specs = (
        P(("parts", "dp"), "tensor"),
        P("tensor"),
        P("tensor", "dp"),
        P("parts", None),
        P(("parts", "dp"), None),
        P(("parts", "dp"), None),
    )
    out_specs = (P(("parts", "dp"), None), P(("parts", "dp"), None), P(("parts", "dp"), "tensor"))
    return jax.shard_map(
        per_device, mesh=mesh, in_specs=in_specs, out_specs=out_specs, check_vma=False
    )
```

```python
import math

import jax
import jax.numpy as jnp
from jax import lax
from jax.experimental import pallas as pl
from jax.experimental.pallas import tpu as pltpu
from jax.sharding import PartitionSpec as P

D = 8192
HD = 128
HQ = 8
TOK_DEV = 128
BLOCK = 16


def rotary(positions):
    half = HD // 2
    freq = jnp.exp(-jnp.log(500000.0) * jnp.arange(half, dtype=jnp.float32) * 2.0 / HD)
    angle = positions.astype(jnp.float32)[:, None] * freq[None, :]
    return (jnp.cos(angle), jnp.sin(angle))


def rotate(block, cosine, sine):
    half = HD // 2
    if block.ndim == 3:
        cosine = cosine[:, None, :]
        sine = sine[:, None, :]
    first = block[..., :half]
    second = block[..., half:]
    return jnp.concatenate(
        [first * cosine - second * sine, second * cosine + first * sine], axis=-1
    )


def members(lengths, count):
    ends = jnp.cumsum(lengths)
    starts = ends - lengths
    place = jnp.arange(count, dtype=jnp.int32)
    member = (place[:, None] >= starts[None, :]) & (place[:, None] < ends[None, :])
    return (member, place[:, None] - starts[None, :])


def positions_of(lengths, prefix, count):
    member, within = members(lengths, count)
    which = jnp.arange(lengths.shape[0], dtype=jnp.int32)
    sequence = jnp.sum(jnp.where(member, which[None, :], 0), axis=1)
    position = jnp.sum(jnp.where(member, prefix[None, :] + within, 0), axis=1)
    return (sequence, position)


def pick_of(column, slot, count):
    member, within = members(column, count)
    source = jnp.arange(column.shape[0], dtype=jnp.int32)
    index = jnp.sum(jnp.where(member, source[None, :] * slot + within, 0), axis=1)
    slots = jnp.arange(column.shape[0] * slot, dtype=jnp.int32)
    return (index[:, None] == slots[None, :]).astype(jnp.bfloat16)


def attend(queries, keys, values, allowed):
    scores = jnp.einsum(
        "qhd,kd->hqk", queries, keys, preferred_element_type=jnp.float32
    ) / jnp.sqrt(jnp.float32(HD))
    scores = jnp.where(allowed[None, :, :], scores, jnp.float32(-1e30))
    top = jnp.max(scores, axis=-1, keepdims=True)
    expo = jnp.exp(scores - top)
    weights = (expo / jnp.sum(expo, axis=-1, keepdims=True)).astype(jnp.bfloat16)
    out = jnp.einsum("hqk,kd->qhd", weights, values, preferred_element_type=jnp.float32)
    return out.astype(jnp.bfloat16)


def scale_of(rows):
    wide = rows.astype(jnp.float32)
    total = lax.psum(jnp.sum(wide * wide, axis=1), "tensor")
    return lax.rsqrt(total / D + 1e-05)


def scaled(rows, scale, norm_gain):
    return (rows.astype(jnp.float32) * scale[:, None] * norm_gain[None, :]).astype(jnp.bfloat16)


def product(rows, columns):
    return lax.dot_general(
        rows, columns, (((1,), (1,)), ((), ())), preferred_element_type=jnp.float32
    )


def cut(partial, width, core):
    share = width // lax.axis_size("tensor")
    mine = lax.dynamic_slice_in_dim(partial, core * share, share, 1)
    return jnp.concatenate([mine, partial[:, width:]], axis=1)


def sum_cores(partial):
    width = HQ * HD * partial.shape[1] // (HQ * HD + 2 * HD)
    core = lax.axis_index("tensor")
    other = lax.ppermute(cut(partial, width, 1 - core), "tensor", [(0, 1), (1, 0)])
    return (cut(partial, width, core) + other).astype(jnp.bfloat16)


def over(block, places):
    return lax.ppermute(block, "dp", [(2 * z + x, 2 * z + 1 - x) for z in places for x in range(2)])


def along(block, moves):
    return lax.ppermute(block, "dp", [(2 * a + x, 2 * b + x) for a, b in moves for x in range(2)])


PAIRS = ((0, 1), (1, 0), (2, 3), (3, 2))
ACROSS = ((1, 2), (2, 1))
OUTWARD = ((1, 0), (2, 3))
ENDS = (0, 3)
MIDDLE = (1, 2)


def overs(places):
    return [(2 * z + x, 2 * z + 1 - x) for z in places for x in range(2)]


def alongs(moves):
    return [(2 * a + x, 2 * b + x) for a, b in moves for x in range(2)]


def gather_line(mine, at_end, normed):
    def send(block, pairs):
        return lax.ppermute(block, "dp", pairs)

    near = send(mine, alongs(PAIRS))
    cross = send(mine, alongs(ACROSS) + overs(ENDS))
    side = send(mine, overs(MIDDLE))
    near, cross, side, normed = lax.optimization_barrier((near, cross, side, normed))
    second = send(cross, alongs(PAIRS))
    far = send(near, alongs(ACROSS))
    near_over = send(near, overs(ENDS))
    cross_over = send(cross, overs(MIDDLE))
    last = send(far, alongs(OUTWARD))
    second_over = send(jnp.where(at_end, second, far), overs(range(4)))
    last_over = send(last, overs(ENDS))
    early = (mine, near, cross, side, second, far, near_over, cross_over, second_over)
    return early, (last, last_over), normed


def early_kernel(
    at, mine, near, cross, side, second, far, near_over, cross_over, second_over,
    own, theirs, keep, send, whole, sems,
):
    z, x, part, core = at[0], at[1], at[2], at[3]
    size = mine.shape[0]

    def place(pairs):
        found = []
        for k, (where, pieces) in enumerate(pairs):
            for j, piece in enumerate(pieces):
                column = x if j == 0 else 1 - x
                start = pl.multiple_of((2 * where + column) * size, BLOCK)
                found.append(
                    pltpu.make_async_copy(
                        piece, whole.at[pl.ds(start, size)], sems.at[2 * k + j]
                    )
                )
        for copy in found:
            copy.start()
        for copy in found:
            copy.wait()

    at_end = (z == 0) | (z == 3)
    pair = z + 1 - 2 * (z % 2)

    @pl.when(at_end)
    def _():
        place(
            (
                (z, (mine, cross)),
                (pair, (near, near_over)),
                ((z + 2) % 4, (second, second_over)),
                (3 - z, (mine, cross)),
            )
        )

    @pl.when(jnp.logical_not(at_end))
    def _():
        place(
            (
                (z, (mine, side)),
                (pair, (near, second)),
                ((z + 2) % 4, (far, second_over)),
                (3 - z, (cross, cross_over)),
            )
        )

    count = own.shape[0]
    share = whole.shape[0] * HQ // (HQ + 2) // 2
    for k, rows in ((0, own), (1, theirs)):
        index = part if k == 0 else 1 - part
        start = pl.multiple_of(index * count, count)
        halves = [
            product(rows[...], whole[c * share : (c + 1) * share, :]) for c in range(2)
        ]
        rest = product(rows[...], whole[2 * share :, :])
        for ref in (keep, send):
            ref[pl.ds(start, count), share:] = rest
        for t in range(2):

            @pl.when(core == t)
            def _():
                keep[pl.ds(start, count), :share] = halves[t]
                send[pl.ds(start, count), :share] = halves[1 - t]


def late_kernel(
    at, first_keep, first_send, piece, piece_over, own, theirs, keep, send, last, sems
):
    z, x, part, core = at[0], at[1], at[2], at[3]
    size = piece.shape[0]
    count = own.shape[0]
    share = last.shape[0]
    edge = 2 * size
    gap = share - edge

    def fetch(offset):
        found = []
        for side, ref in ((0, piece), (1, piece_over)):
            where = x if side == 0 else 1 - x
            start = pl.multiple_of(offset + where * size, BLOCK)
            found.append(
                pltpu.make_async_copy(ref, last.at[pl.ds(start, size)], sems.at[side])
            )
        for copy in found:
            copy.start()
        for copy in found:
            copy.wait()

    def blocks():
        for k, rows in ((0, own), (1, theirs)):
            index = part if k == 0 else 1 - part
            start = pl.multiple_of(index * count, count)
            yield pl.ds(start, count), product(rows[...], last[...])

    def merge(ref, source, place, lanes, block, new):
        ref[place, lanes] = jnp.where(new, block, source[place, lanes])

    keep[...] = first_keep[...]
    send[...] = first_send[...]
    lane = lax.broadcasted_iota(jnp.int32, (count, share), 1)

    @pl.when(z == 0)
    def _():
        fetch(gap)
        for place, block in blocks():
            for ref in (keep, send):
                ref[place, share:] = block[:, share // 2 :]
            head = block[:, : share // 2]
            new = lane[:, : share // 2] >= gap
            lanes = slice(share // 2, share)

            @pl.when(core == 1)
            def _():
                merge(keep, first_keep, place, lanes, head, new)

            @pl.when(core == 0)
            def _():
                merge(send, first_send, place, lanes, head, new)

    @pl.when(z == 3)
    def _():
        fetch(0)
        for place, block in blocks():
            lanes = slice(0, share)

            @pl.when(core == 0)
            def _():
                merge(keep, first_keep, place, lanes, block, lane < edge)

            @pl.when(core == 1)
            def _():
                merge(send, first_send, place, lanes, block, lane < edge)


def sum_kernel(keep, other, out):
    out[...] = (keep[...] + other[...]).astype(out.dtype)


def finish_kernel(pick, arrived, cosine, sine, allowed, keys, values, out):
    width = arrived.shape[2]
    count = 2 * width // HD
    chosen = pick[...]
    planes = [
        jnp.dot(chosen, arrived[y], preferred_element_type=jnp.float32).astype(jnp.bfloat16)
        for y in range(2)
    ]
    source = lax.broadcasted_iota(jnp.int32, (HD, 2 * HD), 0)
    target = lax.broadcasted_iota(jnp.int32, (HD, 2 * HD), 1)
    heads = []
    for pair in range(count // 2):
        total = None
        for y in range(2):
            place = source // BLOCK * (2 * BLOCK) + y * BLOCK + source % BLOCK
            order = (place == target).astype(jnp.float32).astype(jnp.bfloat16)
            part = jnp.dot(
                planes[y][:, pair * HD : (pair + 1) * HD],
                order,
                preferred_element_type=jnp.float32,
            )
            total = part if total is None else total + part
        heads += [total[:, :HD], total[:, HD:]]

    def turn(block):
        other = pltpu.roll(block, HD // 2, 1)
        return (block * cosine[...] + other * sine[...]).astype(jnp.bfloat16)

    key = turn(heads[-2])
    value = heads[-1].astype(jnp.bfloat16)
    keys[...] = key
    values[...] = value
    mask = allowed[...] > 0
    for h in range(count - 2):
        scores = product(turn(heads[h]), key) / math.sqrt(HD)
        scores = jnp.where(mask, scores, jnp.float32(-1e30))
        expo = jnp.exp(scores - jnp.max(scores, axis=-1, keepdims=True))
        weights = (expo / jnp.sum(expo, axis=-1, keepdims=True)).astype(jnp.bfloat16)
        out[:, h * HD : (h + 1) * HD] = jnp.dot(
            weights, value, preferred_element_type=jnp.float32
        ).astype(out.dtype)


def finish(pick, arrived, cosine, sine, allowed):
    whole = pl.BlockSpec(memory_space=pltpu.VMEM)
    heads = 2 * arrived.shape[2] // HD - 2
    single = jax.ShapeDtypeStruct((TOK_DEV, HD), jnp.bfloat16)
    return pl.pallas_call(
        finish_kernel,
        out_shape=(single, single, jax.ShapeDtypeStruct((TOK_DEV, heads * HD), jnp.bfloat16)),
        in_specs=[whole] * 5,
        out_specs=(whole,) * 3,
        compiler_params=pltpu.CompilerParams(vmem_limit_bytes=6 << 20),
        name="attend",
    )(
        pick,
        arrived,
        jnp.concatenate([cosine, cosine], axis=1),
        jnp.concatenate([-sine, sine], axis=1),
        allowed.astype(jnp.float32),
    )


def paired(sent_rows, norm_gain, qkv_weight, groups):
    part = lax.axis_index("parts")
    group = lax.axis_index("dp")
    at = jnp.stack([group // 2, group % 2, part, lax.axis_index("tensor")]).astype(jnp.int32)
    turned = qkv_weight.T
    depth = turned.shape[1]
    count = turned.shape[0] // (2 * BLOCK)
    size = count * BLOCK
    mine = lax.dynamic_index_in_dim(
        turned.reshape(count, 2, BLOCK, depth), part, 1, False
    ).reshape(size, depth)
    swap = [(0, 1), (1, 0)]
    raw = lax.ppermute(sent_rows, "parts", swap)
    normed = scaled(sent_rows, scale_of(sent_rows), norm_gain)
    theirs = scaled(raw, scale_of(raw), norm_gain)
    at_end = (group < 2) | (group >= groups - 2)
    early, late, normed = gather_line(mine, at_end, normed)
    slots = sent_rows.shape[0]
    width = groups * size
    whole = pl.BlockSpec(memory_space=pltpu.VMEM)
    anywhere = pl.BlockSpec(memory_space=pl.ANY)
    scalars = pl.BlockSpec(memory_space=pltpu.SMEM)
    heads = width * HQ // (HQ + 2)
    half = jax.ShapeDtypeStruct((2 * slots, heads // 2 + width - heads), jnp.float32)
    first = pl.pallas_call(
        early_kernel,
        out_shape=(half, half),
        in_specs=[scalars] + [anywhere] * 9 + [whole] * 2,
        out_specs=(whole, whole),
        scratch_shapes=[
            pltpu.VMEM((width, depth), jnp.bfloat16),
            pltpu.SemaphoreType.DMA((8,)),
        ],
        compiler_params=pltpu.CompilerParams(vmem_limit_bytes=24 << 20),
        cost_estimate=pl.CostEstimate(
            flops=4 * slots * width * depth, bytes_accessed=12 << 20, transcendentals=0
        ),
        name="project_early",
    )(at, *early, normed, theirs)
    keep, send = pl.pallas_call(
        late_kernel,
        out_shape=(half, half),
        in_specs=[scalars] + [whole] * 2 + [anywhere] * 2 + [whole] * 2,
        out_specs=(whole, whole),
        scratch_shapes=[
            pltpu.VMEM((heads // 2, depth), jnp.bfloat16),
            pltpu.SemaphoreType.DMA((2,)),
        ],
        input_output_aliases={1: 0, 2: 1},
        compiler_params=pltpu.CompilerParams(vmem_limit_bytes=16 << 20),
        cost_estimate=pl.CostEstimate(
            flops=2 * slots * heads * depth, bytes_accessed=6 << 20, transcendentals=0
        ),
        name="project_late",
    )(at, *first, *late, normed, theirs)
    ready = pl.pallas_call(
        sum_kernel,
        out_shape=jax.ShapeDtypeStruct(keep.shape, jnp.bfloat16),
        in_specs=[whole, whole],
        out_specs=whole,
        compiler_params=pltpu.CompilerParams(vmem_limit_bytes=6 << 20),
        name="sum_halves",
    )(keep, lax.ppermute(send, "tensor", swap))
    arrived = lax.all_to_all(ready, ("parts", "dp"), 0, 0, tiled=True)
    return arrived.reshape(2, slots, half.shape[1])


def single(sent_rows, norm_gain, qkv_weight):
    columns = lax.all_gather(qkv_weight.T, "dp", axis=0, tiled=True)
    ready = sum_cores(product(scaled(sent_rows, scale_of(sent_rows), norm_gain), columns))
    return lax.all_to_all(ready, "dp", 0, 0, tiled=True)


def per_device(sent_rows, norm_gain, qkv_weight, route_counts, response_lengths, prefix_lengths):
    groups = lax.axis_size("dp")
    slot = sent_rows.shape[0] // groups
    column = lax.dynamic_slice_in_dim(route_counts, lax.axis_index("dp"), 1, 1)[:, 0]
    pick = pick_of(column, slot, TOK_DEV)
    sequence, position = positions_of(response_lengths[0], prefix_lengths[0], TOK_DEV)
    allowed = (sequence[:, None] == sequence[None, :]) & (position[None, :] <= position[:, None])
    cosine, sine = rotary(position)
    if lax.axis_size("parts") == 2 and groups == 8 and qkv_weight.shape[1] == 160:
        arrived = paired(sent_rows, norm_gain, qkv_weight, groups)
        return finish(pick, arrived, cosine, sine, allowed)
    arrived = single(sent_rows, norm_gain, qkv_weight)
    heads = arrived.shape[1] // HD
    packed = jnp.dot(pick, arrived, preferred_element_type=jnp.float32)
    packed = packed.reshape(TOK_DEV, heads, HD)
    queries = rotate(packed[:, :-2], cosine, sine).astype(jnp.bfloat16)
    new_keys = rotate(packed[:, -2], cosine, sine).astype(jnp.bfloat16)
    new_values = packed[:, -1].astype(jnp.bfloat16)
    out = attend(queries, new_keys, new_values, allowed)
    return (new_keys, new_values, out.reshape(TOK_DEV, (heads - 2) * HD))


def solution(mesh):
    in_specs = (
        P(("parts", "dp"), "tensor"),
        P("tensor"),
        P("tensor", "dp"),
        P("parts", None),
        P(("parts", "dp"), None),
        P(("parts", "dp"), None),
    )
    out_specs = (P(("parts", "dp"), None), P(("parts", "dp"), None), P(("parts", "dp"), "tensor"))
    return jax.shard_map(
        per_device, mesh=mesh, in_specs=in_specs, out_specs=out_specs, check_vma=False
    )
```

```python
import math

import jax
import jax.numpy as jnp
from jax import lax
from jax.experimental import pallas as pl
from jax.experimental.pallas import tpu as pltpu
from jax.sharding import PartitionSpec as P

D = 8192
HD = 128
HQ = 8
TOK_DEV = 128
BLOCK = 16


def rotary(positions):
    half = HD // 2
    freq = jnp.exp(-jnp.log(500000.0) * jnp.arange(half, dtype=jnp.float32) * 2.0 / HD)
    angle = positions.astype(jnp.float32)[:, None] * freq[None, :]
    return (jnp.cos(angle), jnp.sin(angle))


def rotate(block, cosine, sine):
    half = HD // 2
    if block.ndim == 3:
        cosine = cosine[:, None, :]
        sine = sine[:, None, :]
    first = block[..., :half]
    second = block[..., half:]
    return jnp.concatenate(
        [first * cosine - second * sine, second * cosine + first * sine], axis=-1
    )


def members(lengths, count):
    ends = jnp.cumsum(lengths)
    starts = ends - lengths
    place = jnp.arange(count, dtype=jnp.int32)
    member = (place[:, None] >= starts[None, :]) & (place[:, None] < ends[None, :])
    return (member, place[:, None] - starts[None, :])


def positions_of(lengths, prefix, count):
    member, within = members(lengths, count)
    which = jnp.arange(lengths.shape[0], dtype=jnp.int32)
    sequence = jnp.sum(jnp.where(member, which[None, :], 0), axis=1)
    position = jnp.sum(jnp.where(member, prefix[None, :] + within, 0), axis=1)
    return (sequence, position)


def pick_of(column, slot, count):
    member, within = members(column, count)
    source = jnp.arange(column.shape[0], dtype=jnp.int32)
    index = jnp.sum(jnp.where(member, source[None, :] * slot + within, 0), axis=1)
    slots = jnp.arange(column.shape[0] * slot, dtype=jnp.int32)
    return (index[:, None] == slots[None, :]).astype(jnp.bfloat16)


def attend(queries, keys, values, allowed):
    scores = jnp.einsum(
        "qhd,kd->hqk", queries, keys, preferred_element_type=jnp.float32
    ) / jnp.sqrt(jnp.float32(HD))
    scores = jnp.where(allowed[None, :, :], scores, jnp.float32(-1e30))
    top = jnp.max(scores, axis=-1, keepdims=True)
    expo = jnp.exp(scores - top)
    weights = (expo / jnp.sum(expo, axis=-1, keepdims=True)).astype(jnp.bfloat16)
    out = jnp.einsum("hqk,kd->qhd", weights, values, preferred_element_type=jnp.float32)
    return out.astype(jnp.bfloat16)


def squares(rows):
    wide = rows.astype(jnp.float32)
    return jnp.sum(wide * wide, axis=1)


def scale_of(total):
    return lax.rsqrt(total / D + 1e-05)


def scaled(rows, scale, norm_gain):
    return (rows.astype(jnp.float32) * scale * norm_gain).astype(jnp.bfloat16)


def product(rows, columns):
    return lax.dot_general(
        rows, columns, (((1,), (1,)), ((), ())), preferred_element_type=jnp.float32
    )


def cut(partial, width, core):
    share = width // lax.axis_size("tensor")
    mine = lax.dynamic_slice_in_dim(partial, core * share, share, 1)
    return jnp.concatenate([mine, partial[:, width:]], axis=1)


def sum_cores(partial):
    width = HQ * HD * partial.shape[1] // (HQ * HD + 2 * HD)
    core = lax.axis_index("tensor")
    other = lax.ppermute(cut(partial, width, 1 - core), "tensor", [(0, 1), (1, 0)])
    return (cut(partial, width, core) + other).astype(jnp.bfloat16)


def over(block, places):
    return lax.ppermute(block, "dp", [(2 * z + x, 2 * z + 1 - x) for z in places for x in range(2)])


def along(block, moves):
    return lax.ppermute(block, "dp", [(2 * a + x, 2 * b + x) for a, b in moves for x in range(2)])


PAIRS = ((0, 1), (1, 0), (2, 3), (3, 2))
ACROSS = ((1, 2), (2, 1))
OUTWARD = ((1, 0), (2, 3))
ENDS = (0, 3)
MIDDLE = (1, 2)


def overs(places):
    return [(2 * z + x, 2 * z + 1 - x) for z in places for x in range(2)]


def alongs(moves):
    return [(2 * a + x, 2 * b + x) for a, b in moves for x in range(2)]


def gather_line(mine, at_end, total):
    def send(block, pairs):
        return lax.ppermute(block, "dp", pairs)

    near = send(mine, alongs(PAIRS))
    cross = send(mine, alongs(ACROSS) + overs(ENDS))
    side = send(mine, overs(MIDDLE))
    near, cross, side, total = lax.optimization_barrier((near, cross, side, total))
    second = send(cross, alongs(PAIRS))
    far = send(near, alongs(ACROSS))
    near_over = send(near, overs(ENDS))
    cross_over = send(cross, overs(MIDDLE))
    last = send(far, alongs(OUTWARD))
    second_over = send(jnp.where(at_end, second, far), overs(range(4)))
    last_over = send(last, overs(ENDS))
    early = (mine, near, cross, side, second, far, near_over, cross_over, second_over)
    return early, (last, last_over), total


def early_kernel(
    at, mine, near, cross, side, second, far, near_over, cross_over, second_over,
    own, theirs, own_scale, their_scale, gain, keep, send, rows, whole, sems,
):
    z, x, part, core = at[0], at[1], at[2], at[3]
    size = mine.shape[0]

    def place(pairs):
        found = []
        for k, (where, pieces) in enumerate(pairs):
            for j, piece in enumerate(pieces):
                column = x if j == 0 else 1 - x
                start = pl.multiple_of((2 * where + column) * size, BLOCK)
                found.append(
                    pltpu.make_async_copy(
                        piece, whole.at[pl.ds(start, size)], sems.at[2 * k + j]
                    )
                )
        for copy in found:
            copy.start()
        for copy in found:
            copy.wait()

    count = own.shape[0]
    step = 2 * BLOCK
    for k, (source, scale) in enumerate(((own, own_scale), (theirs, their_scale))):
        index = part if k == 0 else 1 - part
        for low in range(0, count, step):
            start = pl.multiple_of(index * count + low, step)
            rows[pl.ds(start, step), :] = scaled(
                source[low : low + step, :], scale[low : low + step, :], gain[...]
            )

    at_end = (z == 0) | (z == 3)
    pair = z + 1 - 2 * (z % 2)

    @pl.when(at_end)
    def _():
        place(
            (
                (z, (mine, cross)),
                (pair, (near, near_over)),
                ((z + 2) % 4, (second, second_over)),
                (3 - z, (mine, cross)),
            )
        )

    @pl.when(jnp.logical_not(at_end))
    def _():
        place(
            (
                (z, (mine, side)),
                (pair, (near, second)),
                ((z + 2) % 4, (far, second_over)),
                (3 - z, (cross, cross_over)),
            )
        )

    share = whole.shape[0] * HQ // (HQ + 2) // 2
    halves = [product(rows[...], whole[c * share : (c + 1) * share, :]) for c in range(2)]
    rest = product(rows[...], whole[2 * share :, :])
    for ref in (keep, send):
        ref[:, share:] = rest
    for t in range(2):

        @pl.when(core == t)
        def _():
            keep[:, :share] = halves[t]
            send[:, :share] = halves[1 - t]


def late_kernel(at, first_keep, first_send, piece, piece_over, rows, keep, send, last, sems):
    z, x, core = at[0], at[1], at[3]
    size = piece.shape[0]
    share = last.shape[0]
    edge = 2 * size
    gap = share - edge

    def fetch(offset):
        found = []
        for side, ref in ((0, piece), (1, piece_over)):
            where = x if side == 0 else 1 - x
            start = pl.multiple_of(offset + where * size, BLOCK)
            found.append(
                pltpu.make_async_copy(ref, last.at[pl.ds(start, size)], sems.at[side])
            )
        for copy in found:
            copy.start()
        for copy in found:
            copy.wait()
        return product(rows[...], last[...])

    def merge(ref, source, lanes, block, new):
        ref[:, lanes] = jnp.where(new, block, source[:, lanes])

    keep[...] = first_keep[...]
    send[...] = first_send[...]
    lane = lax.broadcasted_iota(jnp.int32, (rows.shape[0], share), 1)

    @pl.when(z == 0)
    def _():
        block = fetch(gap)
        for ref in (keep, send):
            ref[:, share:] = block[:, share // 2 :]
        head = block[:, : share // 2]
        new = lane[:, : share // 2] >= gap
        lanes = slice(share // 2, share)

        @pl.when(core == 1)
        def _():
            merge(keep, first_keep, lanes, head, new)

        @pl.when(core == 0)
        def _():
            merge(send, first_send, lanes, head, new)

    @pl.when(z == 3)
    def _():
        block = fetch(0)
        lanes = slice(0, share)

        @pl.when(core == 0)
        def _():
            merge(keep, first_keep, lanes, block, lane < edge)

        @pl.when(core == 1)
        def _():
            merge(send, first_send, lanes, block, lane < edge)


def sum_kernel(keep, other, out):
    out[...] = (keep[...] + other[...]).astype(out.dtype)


def finish_kernel(pick, arrived, cosine, sine, allowed, keys, values, out):
    width = arrived.shape[2]
    count = 2 * width // HD
    chosen = pick[...]
    planes = [
        jnp.dot(chosen, arrived[y], preferred_element_type=jnp.float32).astype(jnp.bfloat16)
        for y in range(2)
    ]
    source = lax.broadcasted_iota(jnp.int32, (HD, 2 * HD), 0)
    target = lax.broadcasted_iota(jnp.int32, (HD, 2 * HD), 1)
    heads = []
    for pair in range(count // 2):
        total = None
        for y in range(2):
            place = source // BLOCK * (2 * BLOCK) + y * BLOCK + source % BLOCK
            order = (place == target).astype(jnp.float32).astype(jnp.bfloat16)
            part = jnp.dot(
                planes[y][:, pair * HD : (pair + 1) * HD],
                order,
                preferred_element_type=jnp.float32,
            )
            total = part if total is None else total + part
        heads += [total[:, :HD], total[:, HD:]]

    def turn(block):
        other = pltpu.roll(block, HD // 2, 1)
        return (block * cosine[...] + other * sine[...]).astype(jnp.bfloat16)

    key = turn(heads[-2])
    value = heads[-1].astype(jnp.bfloat16)
    keys[...] = key
    values[...] = value
    mask = allowed[...] > 0
    for h in range(count - 2):
        scores = product(turn(heads[h]), key) / math.sqrt(HD)
        scores = jnp.where(mask, scores, jnp.float32(-1e30))
        expo = jnp.exp(scores - jnp.max(scores, axis=-1, keepdims=True))
        weights = (expo / jnp.sum(expo, axis=-1, keepdims=True)).astype(jnp.bfloat16)
        out[:, h * HD : (h + 1) * HD] = jnp.dot(
            weights, value, preferred_element_type=jnp.float32
        ).astype(out.dtype)


def finish(pick, arrived, cosine, sine, allowed):
    whole = pl.BlockSpec(memory_space=pltpu.VMEM)
    heads = 2 * arrived.shape[2] // HD - 2
    single = jax.ShapeDtypeStruct((TOK_DEV, HD), jnp.bfloat16)
    return pl.pallas_call(
        finish_kernel,
        out_shape=(single, single, jax.ShapeDtypeStruct((TOK_DEV, heads * HD), jnp.bfloat16)),
        in_specs=[whole] * 5,
        out_specs=(whole,) * 3,
        compiler_params=pltpu.CompilerParams(vmem_limit_bytes=6 << 20),
        name="attend",
    )(
        pick,
        arrived,
        jnp.concatenate([cosine, cosine], axis=1),
        jnp.concatenate([-sine, sine], axis=1),
        allowed.astype(jnp.float32),
    )


def paired(sent_rows, norm_gain, qkv_weight, groups):
    part = lax.axis_index("parts")
    group = lax.axis_index("dp")
    at = jnp.stack([group // 2, group % 2, part, lax.axis_index("tensor")]).astype(jnp.int32)
    turned = qkv_weight.T
    depth = turned.shape[1]
    count = turned.shape[0] // (2 * BLOCK)
    size = count * BLOCK
    mine = lax.dynamic_index_in_dim(
        turned.reshape(count, 2, BLOCK, depth), part, 1, False
    ).reshape(size, depth)
    swap = [(0, 1), (1, 0)]
    raw = lax.ppermute(sent_rows, "parts", swap)
    total = lax.psum(squares(sent_rows), "tensor")
    at_end = (group < 2) | (group >= groups - 2)
    early, late, total = gather_line(mine, at_end, total)
    share = squares(raw)
    their_total = share + lax.ppermute(share, "tensor", swap)
    slots = sent_rows.shape[0]
    width = groups * size
    whole = pl.BlockSpec(memory_space=pltpu.VMEM)
    anywhere = pl.BlockSpec(memory_space=pl.ANY)
    scalars = pl.BlockSpec(memory_space=pltpu.SMEM)
    heads = width * HQ // (HQ + 2)
    half = jax.ShapeDtypeStruct((2 * slots, heads // 2 + width - heads), jnp.float32)
    keep, send, rows = pl.pallas_call(
        early_kernel,
        out_shape=(half, half, jax.ShapeDtypeStruct((2 * slots, depth), jnp.bfloat16)),
        in_specs=[scalars] + [anywhere] * 9 + [whole] * 5,
        out_specs=(whole,) * 3,
        scratch_shapes=[
            pltpu.VMEM((width, depth), jnp.bfloat16),
            pltpu.SemaphoreType.DMA((8,)),
        ],
        compiler_params=pltpu.CompilerParams(vmem_limit_bytes=28 << 20),
        cost_estimate=pl.CostEstimate(
            flops=4 * slots * width * depth, bytes_accessed=12 << 20, transcendentals=0
        ),
        name="project_early",
    )(
        at,
        *early,
        sent_rows,
        raw,
        scale_of(total)[:, None],
        scale_of(their_total)[:, None],
        norm_gain[None, :],
    )
    keep, send = pl.pallas_call(
        late_kernel,
        out_shape=(half, half),
        in_specs=[scalars] + [whole] * 2 + [anywhere] * 2 + [whole],
        out_specs=(whole, whole),
        scratch_shapes=[
            pltpu.VMEM((heads // 2, depth), jnp.bfloat16),
            pltpu.SemaphoreType.DMA((2,)),
        ],
        input_output_aliases={1: 0, 2: 1},
        compiler_params=pltpu.CompilerParams(vmem_limit_bytes=16 << 20),
        cost_estimate=pl.CostEstimate(
            flops=2 * slots * heads * depth, bytes_accessed=6 << 20, transcendentals=0
        ),
        name="project_late",
    )(at, keep, send, *late, rows)
    ready = pl.pallas_call(
        sum_kernel,
        out_shape=jax.ShapeDtypeStruct(keep.shape, jnp.bfloat16),
        in_specs=[whole, whole],
        out_specs=whole,
        compiler_params=pltpu.CompilerParams(vmem_limit_bytes=6 << 20),
        name="sum_halves",
    )(keep, lax.ppermute(send, "tensor", swap))
    arrived = lax.all_to_all(ready, ("parts", "dp"), 0, 0, tiled=True)
    return arrived.reshape(2, slots, half.shape[1])


def single(sent_rows, norm_gain, qkv_weight):
    columns = lax.all_gather(qkv_weight.T, "dp", axis=0, tiled=True)
    scale = scale_of(lax.psum(squares(sent_rows), "tensor"))
    ready = sum_cores(product(scaled(sent_rows, scale[:, None], norm_gain[None, :]), columns))
    return lax.all_to_all(ready, "dp", 0, 0, tiled=True)


def per_device(sent_rows, norm_gain, qkv_weight, route_counts, response_lengths, prefix_lengths):
    groups = lax.axis_size("dp")
    slot = sent_rows.shape[0] // groups
    column = lax.dynamic_slice_in_dim(route_counts, lax.axis_index("dp"), 1, 1)[:, 0]
    pick = pick_of(column, slot, TOK_DEV)
    sequence, position = positions_of(response_lengths[0], prefix_lengths[0], TOK_DEV)
    allowed = (sequence[:, None] == sequence[None, :]) & (position[None, :] <= position[:, None])
    cosine, sine = rotary(position)
    if lax.axis_size("parts") == 2 and groups == 8 and qkv_weight.shape[1] == 160:
        arrived = paired(sent_rows, norm_gain, qkv_weight, groups)
        return finish(pick, arrived, cosine, sine, allowed)
    arrived = single(sent_rows, norm_gain, qkv_weight)
    heads = arrived.shape[1] // HD
    packed = jnp.dot(pick, arrived, preferred_element_type=jnp.float32)
    packed = packed.reshape(TOK_DEV, heads, HD)
    queries = rotate(packed[:, :-2], cosine, sine).astype(jnp.bfloat16)
    new_keys = rotate(packed[:, -2], cosine, sine).astype(jnp.bfloat16)
    new_values = packed[:, -1].astype(jnp.bfloat16)
    out = attend(queries, new_keys, new_values, allowed)
    return (new_keys, new_values, out.reshape(TOK_DEV, (heads - 2) * HD))


def solution(mesh):
    in_specs = (
        P(("parts", "dp"), "tensor"),
        P("tensor"),
        P("tensor", "dp"),
        P("parts", None),
        P(("parts", "dp"), None),
        P(("parts", "dp"), None),
    )
    out_specs = (P(("parts", "dp"), None), P(("parts", "dp"), None), P(("parts", "dp"), "tensor"))
    return jax.shard_map(
        per_device, mesh=mesh, in_specs=in_specs, out_specs=out_specs, check_vma=False
    )
```

```python
import math

import jax
import jax.numpy as jnp
from jax import lax
from jax.experimental import pallas as pl
from jax.experimental.pallas import tpu as pltpu
from jax.sharding import PartitionSpec as P

D = 8192
HD = 128
HQ = 8
TOK_DEV = 128
BLOCK = 16


def rotary(positions):
    half = HD // 2
    freq = jnp.exp(-jnp.log(500000.0) * jnp.arange(half, dtype=jnp.float32) * 2.0 / HD)
    angle = positions.astype(jnp.float32)[:, None] * freq[None, :]
    return (jnp.cos(angle), jnp.sin(angle))


def rotate(block, cosine, sine):
    half = HD // 2
    if block.ndim == 3:
        cosine = cosine[:, None, :]
        sine = sine[:, None, :]
    first = block[..., :half]
    second = block[..., half:]
    return jnp.concatenate(
        [first * cosine - second * sine, second * cosine + first * sine], axis=-1
    )


def members(lengths, count):
    ends = jnp.cumsum(lengths)
    starts = ends - lengths
    place = jnp.arange(count, dtype=jnp.int32)
    member = (place[:, None] >= starts[None, :]) & (place[:, None] < ends[None, :])
    return (member, place[:, None] - starts[None, :])


def positions_of(lengths, prefix, count):
    member, within = members(lengths, count)
    which = jnp.arange(lengths.shape[0], dtype=jnp.int32)
    sequence = jnp.sum(jnp.where(member, which[None, :], 0), axis=1)
    position = jnp.sum(jnp.where(member, prefix[None, :] + within, 0), axis=1)
    return (sequence, position)


def pick_of(column, slot, count):
    member, within = members(column, count)
    source = jnp.arange(column.shape[0], dtype=jnp.int32)
    index = jnp.sum(jnp.where(member, source[None, :] * slot + within, 0), axis=1)
    slots = jnp.arange(column.shape[0] * slot, dtype=jnp.int32)
    return (index[:, None] == slots[None, :]).astype(jnp.bfloat16)


def attend(queries, keys, values, allowed):
    scores = jnp.einsum(
        "qhd,kd->hqk", queries, keys, preferred_element_type=jnp.float32
    ) / jnp.sqrt(jnp.float32(HD))
    scores = jnp.where(allowed[None, :, :], scores, jnp.float32(-1e30))
    top = jnp.max(scores, axis=-1, keepdims=True)
    expo = jnp.exp(scores - top)
    weights = (expo / jnp.sum(expo, axis=-1, keepdims=True)).astype(jnp.bfloat16)
    out = jnp.einsum("hqk,kd->qhd", weights, values, preferred_element_type=jnp.float32)
    return out.astype(jnp.bfloat16)


def squares(rows):
    wide = rows.astype(jnp.float32)
    return jnp.sum(wide * wide, axis=1)


def scale_of(total):
    return lax.rsqrt(total / D + 1e-05)


def scaled(rows, scale, norm_gain):
    return (rows.astype(jnp.float32) * scale * norm_gain).astype(jnp.bfloat16)


def product(rows, columns):
    return lax.dot_general(
        rows, columns, (((1,), (1,)), ((), ())), preferred_element_type=jnp.float32
    )


def cut(partial, width, core):
    share = width // lax.axis_size("tensor")
    mine = lax.dynamic_slice_in_dim(partial, core * share, share, 1)
    return jnp.concatenate([mine, partial[:, width:]], axis=1)


def sum_cores(partial):
    width = HQ * HD * partial.shape[1] // (HQ * HD + 2 * HD)
    core = lax.axis_index("tensor")
    other = lax.ppermute(cut(partial, width, 1 - core), "tensor", [(0, 1), (1, 0)])
    return (cut(partial, width, core) + other).astype(jnp.bfloat16)


def over(block, places):
    return lax.ppermute(block, "dp", [(2 * z + x, 2 * z + 1 - x) for z in places for x in range(2)])


def along(block, moves):
    return lax.ppermute(block, "dp", [(2 * a + x, 2 * b + x) for a, b in moves for x in range(2)])


PAIRS = ((0, 1), (1, 0), (2, 3), (3, 2))
ACROSS = ((1, 2), (2, 1))
OUTWARD = ((1, 0), (2, 3))
ENDS = (0, 3)
MIDDLE = (1, 2)


def overs(places):
    return [(2 * z + x, 2 * z + 1 - x) for z in places for x in range(2)]


def alongs(moves):
    return [(2 * a + x, 2 * b + x) for a, b in moves for x in range(2)]


def gather_line(mine, at_end, total, ahead):
    def send(block, pairs):
        return lax.ppermute(block, "dp", pairs)

    near = send(mine, alongs(PAIRS))
    cross = send(mine, alongs(ACROSS) + overs(ENDS))
    side = send(mine, overs(MIDDLE))
    near, cross, total, ahead = lax.optimization_barrier((near, cross, total, ahead))
    second = send(cross, alongs(PAIRS))
    far = send(near, alongs(ACROSS))
    near_next, cross_next, side = lax.optimization_barrier((near, cross, side))
    near_over = send(near_next, overs(ENDS))
    cross_over = send(cross_next, overs(MIDDLE))
    far, total = lax.optimization_barrier((far, total))
    last = send(far, alongs(OUTWARD))
    second_over = send(jnp.where(at_end, second, far), overs(range(4)))
    last_over = send(last, overs(ENDS))
    early = (mine, near, cross, side, second, far, near_over, cross_over, second_over)
    return early, (last, last_over), total, ahead


def early_kernel(
    at, mine, near, cross, side, second, far, near_over, cross_over, second_over,
    own, ahead, behind, own_scale, their_scale, gain, keep, send, rows, whole,
):
    z, x, part, core = at[0], at[1], at[2], at[3]
    size = mine.shape[0]

    def place(pairs):
        for where, pieces in pairs:
            for j, piece in enumerate(pieces):
                column = x if j == 0 else 1 - x
                start = pl.multiple_of((2 * where + column) * size, BLOCK)
                whole[pl.ds(start, size), :] = piece[...]

    count = own.shape[0]
    for index, sources, scale in (
        (part, (own,), own_scale),
        (1 - part, (ahead, behind), their_scale),
    ):
        upright = jnp.broadcast_to(scale[...], (HD, count)).T[:, :1]
        done = 0
        for source in sources:
            for low in range(0, source.shape[0], BLOCK):
                start = pl.multiple_of(index * count + done + low, BLOCK)
                rows[pl.ds(start, BLOCK), :] = scaled(
                    source[low : low + BLOCK, :],
                    upright[done + low : done + low + BLOCK, :],
                    gain[...],
                )
            done += source.shape[0]

    at_end = (z == 0) | (z == 3)
    pair = z + 1 - 2 * (z % 2)

    @pl.when(at_end)
    def _():
        place(
            (
                (z, (mine, cross)),
                (pair, (near, near_over)),
                ((z + 2) % 4, (second, second_over)),
                (3 - z, (mine, cross)),
            )
        )

    @pl.when(jnp.logical_not(at_end))
    def _():
        place(
            (
                (z, (mine, side)),
                (pair, (near, second)),
                ((z + 2) % 4, (far, second_over)),
                (3 - z, (cross, cross_over)),
            )
        )

    share = whole.shape[0] * HQ // (HQ + 2) // 2
    halves = [product(rows[...], whole[c * share : (c + 1) * share, :]) for c in range(2)]
    rest = product(rows[...], whole[2 * share :, :])
    for ref in (keep, send):
        ref[:, share:] = rest
    for t in range(2):

        @pl.when(core == t)
        def _():
            keep[:, :share] = halves[t]
            send[:, :share] = halves[1 - t]


def late_kernel(at, first_keep, first_send, piece, piece_over, rows, keep, send, last):
    z, x, core = at[0], at[1], at[3]
    size = piece.shape[0]
    share = last.shape[0]
    edge = 2 * size
    gap = share - edge

    def fetch(offset):
        for side, ref in ((0, piece), (1, piece_over)):
            where = x if side == 0 else 1 - x
            start = pl.multiple_of(offset + where * size, BLOCK)
            last[pl.ds(start, size), :] = ref[...]
        return product(rows[...], last[...])

    def merge(ref, source, lanes, block, new):
        ref[:, lanes] = jnp.where(new, block, source[:, lanes])

    keep[...] = first_keep[...]
    send[...] = first_send[...]
    lane = lax.broadcasted_iota(jnp.int32, (rows.shape[0], share), 1)

    @pl.when(z == 0)
    def _():
        block = fetch(gap)
        for ref in (keep, send):
            ref[:, share:] = block[:, share // 2 :]
        head = block[:, : share // 2]
        new = lane[:, : share // 2] >= gap
        lanes = slice(share // 2, share)

        @pl.when(core == 1)
        def _():
            merge(keep, first_keep, lanes, head, new)

        @pl.when(core == 0)
        def _():
            merge(send, first_send, lanes, head, new)

    @pl.when(z == 3)
    def _():
        block = fetch(0)
        lanes = slice(0, share)

        @pl.when(core == 0)
        def _():
            merge(keep, first_keep, lanes, block, lane < edge)

        @pl.when(core == 1)
        def _():
            merge(send, first_send, lanes, block, lane < edge)


def sum_kernel(keep, other, out):
    out[...] = (keep[...] + other[...]).astype(out.dtype)


def finish_kernel(pick, arrived, cosine, sine, allowed, keys, values, out):
    width = arrived.shape[2]
    count = 2 * width // HD
    chosen = pick[...]
    planes = [
        jnp.dot(chosen, arrived[y], preferred_element_type=jnp.float32).astype(jnp.bfloat16)
        for y in range(2)
    ]
    source = lax.broadcasted_iota(jnp.int32, (HD, 2 * HD), 0)
    target = lax.broadcasted_iota(jnp.int32, (HD, 2 * HD), 1)
    heads = []
    for pair in range(count // 2):
        total = None
        for y in range(2):
            place = source // BLOCK * (2 * BLOCK) + y * BLOCK + source % BLOCK
            order = (place == target).astype(jnp.float32).astype(jnp.bfloat16)
            part = jnp.dot(
                planes[y][:, pair * HD : (pair + 1) * HD],
                order,
                preferred_element_type=jnp.float32,
            )
            total = part if total is None else total + part
        heads += [total[:, :HD], total[:, HD:]]

    def turn(block):
        other = pltpu.roll(block, HD // 2, 1)
        return (block * cosine[...] + other * sine[...]).astype(jnp.bfloat16)

    key = turn(heads[-2])
    value = heads[-1].astype(jnp.bfloat16)
    keys[...] = key
    values[...] = value
    mask = allowed[...] > 0
    for h in range(count - 2):
        scores = product(turn(heads[h]), key) / math.sqrt(HD)
        scores = jnp.where(mask, scores, jnp.float32(-1e30))
        expo = jnp.exp(scores - jnp.max(scores, axis=-1, keepdims=True))
        weights = (expo / jnp.sum(expo, axis=-1, keepdims=True)).astype(jnp.bfloat16)
        out[:, h * HD : (h + 1) * HD] = jnp.dot(
            weights, value, preferred_element_type=jnp.float32
        ).astype(out.dtype)


def finish(pick, arrived, cosine, sine, allowed):
    whole = pl.BlockSpec(memory_space=pltpu.VMEM)
    heads = 2 * arrived.shape[2] // HD - 2
    single = jax.ShapeDtypeStruct((TOK_DEV, HD), jnp.bfloat16)
    return pl.pallas_call(
        finish_kernel,
        out_shape=(single, single, jax.ShapeDtypeStruct((TOK_DEV, heads * HD), jnp.bfloat16)),
        in_specs=[whole] * 5,
        out_specs=(whole,) * 3,
        compiler_params=pltpu.CompilerParams(vmem_limit_bytes=6 << 20),
        name="attend",
    )(
        pick,
        arrived,
        jnp.concatenate([cosine, cosine], axis=1),
        jnp.concatenate([-sine, sine], axis=1),
        allowed.astype(jnp.float32),
    )


def paired(sent_rows, norm_gain, qkv_weight, groups):
    part = lax.axis_index("parts")
    group = lax.axis_index("dp")
    at = jnp.stack([group // 2, group % 2, part, lax.axis_index("tensor")]).astype(jnp.int32)
    turned = qkv_weight.T
    depth = turned.shape[1]
    count = turned.shape[0] // (2 * BLOCK)
    size = count * BLOCK
    mine = lax.dynamic_index_in_dim(
        turned.reshape(count, 2, BLOCK, depth), part, 1, False
    ).reshape(size, depth)
    swap = [(0, 1), (1, 0)]
    ahead = lax.ppermute(sent_rows[:size], "parts", swap)
    behind = lax.ppermute(sent_rows[size:], "parts", swap)
    total = lax.psum(squares(sent_rows), "tensor")
    at_end = (group < 2) | (group >= groups - 2)
    early, late, total, ahead = gather_line(mine, at_end, total, ahead)
    scale = scale_of(total)
    their_scale = lax.ppermute(scale, "parts", swap)
    slots = sent_rows.shape[0]
    width = groups * size
    whole = pl.BlockSpec(memory_space=pltpu.VMEM)
    scalars = pl.BlockSpec(memory_space=pltpu.SMEM)
    heads = width * HQ // (HQ + 2)
    half = jax.ShapeDtypeStruct((2 * slots, heads // 2 + width - heads), jnp.float32)
    keep, send, rows = pl.pallas_call(
        early_kernel,
        out_shape=(half, half, jax.ShapeDtypeStruct((2 * slots, depth), jnp.bfloat16)),
        in_specs=[scalars] + [whole] * 15,
        out_specs=(whole,) * 3,
        scratch_shapes=[pltpu.VMEM((width, depth), jnp.bfloat16)],
        compiler_params=pltpu.CompilerParams(vmem_limit_bytes=28 << 20),
        cost_estimate=pl.CostEstimate(
            flops=4 * slots * width * depth, bytes_accessed=12 << 20, transcendentals=0
        ),
        name="project_early",
    )(
        at,
        *early,
        sent_rows,
        ahead,
        behind,
        scale[None, :],
        their_scale[None, :],
        norm_gain[None, :],
    )
    keep, send = pl.pallas_call(
        late_kernel,
        out_shape=(half, half),
        in_specs=[scalars] + [whole] * 5,
        out_specs=(whole, whole),
        scratch_shapes=[pltpu.VMEM((heads // 2, depth), jnp.bfloat16)],
        input_output_aliases={1: 0, 2: 1},
        compiler_params=pltpu.CompilerParams(vmem_limit_bytes=16 << 20),
        cost_estimate=pl.CostEstimate(
            flops=2 * slots * heads * depth, bytes_accessed=6 << 20, transcendentals=0
        ),
        name="project_late",
    )(at, keep, send, *late, rows)
    ready = pl.pallas_call(
        sum_kernel,
        out_shape=jax.ShapeDtypeStruct(keep.shape, jnp.bfloat16),
        in_specs=[whole, whole],
        out_specs=whole,
        compiler_params=pltpu.CompilerParams(vmem_limit_bytes=6 << 20),
        name="sum_halves",
    )(keep, lax.ppermute(send, "tensor", swap))
    arrived = lax.all_to_all(ready, ("parts", "dp"), 0, 0, tiled=True)
    return arrived.reshape(2, slots, half.shape[1])


def single(sent_rows, norm_gain, qkv_weight):
    columns = lax.all_gather(qkv_weight.T, "dp", axis=0, tiled=True)
    scale = scale_of(lax.psum(squares(sent_rows), "tensor"))
    ready = sum_cores(product(scaled(sent_rows, scale[:, None], norm_gain[None, :]), columns))
    return lax.all_to_all(ready, "dp", 0, 0, tiled=True)


def per_device(sent_rows, norm_gain, qkv_weight, route_counts, response_lengths, prefix_lengths):
    groups = lax.axis_size("dp")
    slot = sent_rows.shape[0] // groups
    column = lax.dynamic_slice_in_dim(route_counts, lax.axis_index("dp"), 1, 1)[:, 0]
    pick = pick_of(column, slot, TOK_DEV)
    sequence, position = positions_of(response_lengths[0], prefix_lengths[0], TOK_DEV)
    allowed = (sequence[:, None] == sequence[None, :]) & (position[None, :] <= position[:, None])
    cosine, sine = rotary(position)
    if lax.axis_size("parts") == 2 and groups == 8 and qkv_weight.shape[1] == 160:
        arrived = paired(sent_rows, norm_gain, qkv_weight, groups)
        return finish(pick, arrived, cosine, sine, allowed)
    arrived = single(sent_rows, norm_gain, qkv_weight)
    heads = arrived.shape[1] // HD
    packed = jnp.dot(pick, arrived, preferred_element_type=jnp.float32)
    packed = packed.reshape(TOK_DEV, heads, HD)
    queries = rotate(packed[:, :-2], cosine, sine).astype(jnp.bfloat16)
    new_keys = rotate(packed[:, -2], cosine, sine).astype(jnp.bfloat16)
    new_values = packed[:, -1].astype(jnp.bfloat16)
    out = attend(queries, new_keys, new_values, allowed)
    return (new_keys, new_values, out.reshape(TOK_DEV, (heads - 2) * HD))


def solution(mesh):
    in_specs = (
        P(("parts", "dp"), "tensor"),
        P("tensor"),
        P("tensor", "dp"),
        P("parts", None),
        P(("parts", "dp"), None),
        P(("parts", "dp"), None),
    )
    out_specs = (P(("parts", "dp"), None), P(("parts", "dp"), None), P(("parts", "dp"), "tensor"))
    return jax.shard_map(
        per_device, mesh=mesh, in_specs=in_specs, out_specs=out_specs, check_vma=False
    )
```

```python
import math

import jax
import jax.numpy as jnp
from jax import lax
from jax.experimental import pallas as pl
from jax.experimental.pallas import tpu as pltpu
from jax.sharding import PartitionSpec as P

D = 8192
HD = 128
HQ = 8
TOK_DEV = 128
BLOCK = 16


def rotary(positions):
    half = HD // 2
    freq = jnp.exp(-jnp.log(500000.0) * jnp.arange(half, dtype=jnp.float32) * 2.0 / HD)
    angle = positions.astype(jnp.float32)[:, None] * freq[None, :]
    return (jnp.cos(angle), jnp.sin(angle))


def rotate(block, cosine, sine):
    half = HD // 2
    if block.ndim == 3:
        cosine = cosine[:, None, :]
        sine = sine[:, None, :]
    first = block[..., :half]
    second = block[..., half:]
    return jnp.concatenate(
        [first * cosine - second * sine, second * cosine + first * sine], axis=-1
    )


def members(lengths, count):
    ends = jnp.cumsum(lengths)
    starts = ends - lengths
    place = jnp.arange(count, dtype=jnp.int32)
    member = (place[:, None] >= starts[None, :]) & (place[:, None] < ends[None, :])
    return (member, place[:, None] - starts[None, :])


def positions_of(lengths, prefix, count):
    member, within = members(lengths, count)
    which = jnp.arange(lengths.shape[0], dtype=jnp.int32)
    sequence = jnp.sum(jnp.where(member, which[None, :], 0), axis=1)
    position = jnp.sum(jnp.where(member, prefix[None, :] + within, 0), axis=1)
    return (sequence, position)


def pick_of(column, slot, count):
    member, within = members(column, count)
    source = jnp.arange(column.shape[0], dtype=jnp.int32)
    index = jnp.sum(jnp.where(member, source[None, :] * slot + within, 0), axis=1)
    slots = jnp.arange(column.shape[0] * slot, dtype=jnp.int32)
    return (index[:, None] == slots[None, :]).astype(jnp.bfloat16)


def attend(queries, keys, values, allowed):
    scores = jnp.einsum(
        "qhd,kd->hqk", queries, keys, preferred_element_type=jnp.float32
    ) / jnp.sqrt(jnp.float32(HD))
    scores = jnp.where(allowed[None, :, :], scores, jnp.float32(-1e30))
    top = jnp.max(scores, axis=-1, keepdims=True)
    expo = jnp.exp(scores - top)
    weights = (expo / jnp.sum(expo, axis=-1, keepdims=True)).astype(jnp.bfloat16)
    out = jnp.einsum("hqk,kd->qhd", weights, values, preferred_element_type=jnp.float32)
    return out.astype(jnp.bfloat16)


def squares(rows):
    wide = rows.astype(jnp.float32)
    return jnp.sum(wide * wide, axis=1)


def scale_of(total):
    return lax.rsqrt(total / D + 1e-05)


def scaled(rows, scale, norm_gain):
    return (rows.astype(jnp.float32) * scale * norm_gain).astype(jnp.bfloat16)


def product(rows, columns):
    return lax.dot_general(
        rows, columns, (((1,), (1,)), ((), ())), preferred_element_type=jnp.float32
    )


def cut(partial, width, core):
    share = width // lax.axis_size("tensor")
    mine = lax.dynamic_slice_in_dim(partial, core * share, share, 1)
    return jnp.concatenate([mine, partial[:, width:]], axis=1)


def sum_cores(partial):
    width = HQ * HD * partial.shape[1] // (HQ * HD + 2 * HD)
    core = lax.axis_index("tensor")
    other = lax.ppermute(cut(partial, width, 1 - core), "tensor", [(0, 1), (1, 0)])
    return (cut(partial, width, core) + other).astype(jnp.bfloat16)


def over(block, places):
    return lax.ppermute(block, "dp", [(2 * z + x, 2 * z + 1 - x) for z in places for x in range(2)])


def along(block, moves):
    return lax.ppermute(block, "dp", [(2 * a + x, 2 * b + x) for a, b in moves for x in range(2)])


PAIRS = ((0, 1), (1, 0), (2, 3), (3, 2))
ACROSS = ((1, 2), (2, 1))
OUTWARD = ((1, 0), (2, 3))
ENDS = (0, 3)
MIDDLE = (1, 2)


def overs(places):
    return [(2 * z + x, 2 * z + 1 - x) for z in places for x in range(2)]


def alongs(moves):
    return [(2 * a + x, 2 * b + x) for a, b in moves for x in range(2)]


def gather_line(mine, first):
    def send(block, pairs):
        return lax.ppermute(block, "dp", pairs)

    near = send(mine, alongs(PAIRS))
    cross = send(mine, alongs(ACROSS) + overs(ENDS))
    side = send(mine, overs(MIDDLE))
    near, cross, side, first = lax.optimization_barrier((near, cross, side, first))
    second = send(cross, alongs(PAIRS))
    onward = send(near, alongs(ACROSS) + overs(ENDS))
    cross_over = send(cross, overs(MIDDLE))
    onward, cross_over = lax.optimization_barrier((onward, cross_over))
    last = send(onward, alongs(OUTWARD))
    far_over = send(onward, overs(MIDDLE))
    second_over = send(second, overs(ENDS))
    last_over = send(last, overs(ENDS))
    early = (mine, near, cross, side, second, onward, cross_over, far_over, second_over)
    return early, (last, last_over), first


def early_kernel(
    at, mine, near, cross, side, second, onward, cross_over, far_over, second_over,
    own, ahead, behind, own_scale, their_scale, gain, keep, send, rows, whole,
):
    z, x, part, core = at[0], at[1], at[2], at[3]
    size = mine.shape[0]

    def place(pairs):
        for where, pieces in pairs:
            for j, piece in enumerate(pieces):
                column = x if j == 0 else 1 - x
                start = pl.multiple_of((2 * where + column) * size, BLOCK)
                whole[pl.ds(start, size), :] = piece[...]

    count = own.shape[0]
    for index, sources, scale in (
        (part, (own,), own_scale),
        (1 - part, (ahead, behind), their_scale),
    ):
        upright = jnp.broadcast_to(scale[...], (HD, count)).T[:, :1]
        done = 0
        for source in sources:
            for low in range(0, source.shape[0], BLOCK):
                start = pl.multiple_of(index * count + done + low, BLOCK)
                rows[pl.ds(start, BLOCK), :] = scaled(
                    source[low : low + BLOCK, :],
                    upright[done + low : done + low + BLOCK, :],
                    gain[...],
                )
            done += source.shape[0]

    at_end = (z == 0) | (z == 3)
    pair = z + 1 - 2 * (z % 2)

    @pl.when(at_end)
    def _():
        place(
            (
                (z, (mine, cross)),
                (pair, (near, onward)),
                ((z + 2) % 4, (second, second_over)),
                (3 - z, (mine, cross)),
            )
        )

    @pl.when(jnp.logical_not(at_end))
    def _():
        place(
            (
                (z, (mine, side)),
                (pair, (near, second)),
                ((z + 2) % 4, (onward, far_over)),
                (3 - z, (cross, cross_over)),
            )
        )

    share = whole.shape[0] * HQ // (HQ + 2) // 2
    halves = [product(rows[...], whole[c * share : (c + 1) * share, :]) for c in range(2)]
    rest = product(rows[...], whole[2 * share :, :])
    for ref in (keep, send):
        ref[:, share:] = rest
    for t in range(2):

        @pl.when(core == t)
        def _():
            keep[:, :share] = halves[t]
            send[:, :share] = halves[1 - t]


def late_kernel(at, first_keep, first_send, piece, piece_over, rows, keep, send, last):
    z, x, core = at[0], at[1], at[3]
    size = piece.shape[0]
    share = last.shape[0]
    edge = 2 * size
    gap = share - edge

    def fetch(offset):
        for side, ref in ((0, piece), (1, piece_over)):
            where = x if side == 0 else 1 - x
            start = pl.multiple_of(offset + where * size, BLOCK)
            last[pl.ds(start, size), :] = ref[...]
        return product(rows[...], last[...])

    def merge(ref, source, lanes, block, new):
        ref[:, lanes] = jnp.where(new, block, source[:, lanes])

    keep[...] = first_keep[...]
    send[...] = first_send[...]
    lane = lax.broadcasted_iota(jnp.int32, (rows.shape[0], share), 1)

    @pl.when(z == 0)
    def _():
        block = fetch(gap)
        for ref in (keep, send):
            ref[:, share:] = block[:, share // 2 :]
        head = block[:, : share // 2]
        new = lane[:, : share // 2] >= gap
        lanes = slice(share // 2, share)

        @pl.when(core == 1)
        def _():
            merge(keep, first_keep, lanes, head, new)

        @pl.when(core == 0)
        def _():
            merge(send, first_send, lanes, head, new)

    @pl.when(z == 3)
    def _():
        block = fetch(0)
        lanes = slice(0, share)

        @pl.when(core == 0)
        def _():
            merge(keep, first_keep, lanes, block, lane < edge)

        @pl.when(core == 1)
        def _():
            merge(send, first_send, lanes, block, lane < edge)


def sum_kernel(keep, other, out):
    out[...] = (keep[...] + other[...]).astype(out.dtype)


def finish_kernel(pick, arrived, cosine, sine, allowed, keys, values, out):
    width = arrived.shape[2]
    count = 2 * width // HD
    chosen = pick[...]
    planes = [
        jnp.dot(chosen, arrived[y], preferred_element_type=jnp.float32).astype(jnp.bfloat16)
        for y in range(2)
    ]
    source = lax.broadcasted_iota(jnp.int32, (HD, 2 * HD), 0)
    target = lax.broadcasted_iota(jnp.int32, (HD, 2 * HD), 1)
    heads = []
    for pair in range(count // 2):
        total = None
        for y in range(2):
            place = source // BLOCK * (2 * BLOCK) + y * BLOCK + source % BLOCK
            order = (place == target).astype(jnp.float32).astype(jnp.bfloat16)
            part = jnp.dot(
                planes[y][:, pair * HD : (pair + 1) * HD],
                order,
                preferred_element_type=jnp.float32,
            )
            total = part if total is None else total + part
        heads += [total[:, :HD], total[:, HD:]]

    def turn(block):
        other = pltpu.roll(block, HD // 2, 1)
        return (block * cosine[...] + other * sine[...]).astype(jnp.bfloat16)

    key = turn(heads[-2])
    value = heads[-1].astype(jnp.bfloat16)
    keys[...] = key
    values[...] = value
    mask = allowed[...] > 0
    for h in range(count - 2):
        scores = product(turn(heads[h]), key) / math.sqrt(HD)
        scores = jnp.where(mask, scores, jnp.float32(-1e30))
        expo = jnp.exp(scores - jnp.max(scores, axis=-1, keepdims=True))
        weights = (expo / jnp.sum(expo, axis=-1, keepdims=True)).astype(jnp.bfloat16)
        out[:, h * HD : (h + 1) * HD] = jnp.dot(
            weights, value, preferred_element_type=jnp.float32
        ).astype(out.dtype)


def finish(pick, arrived, cosine, sine, allowed):
    whole = pl.BlockSpec(memory_space=pltpu.VMEM)
    heads = 2 * arrived.shape[2] // HD - 2
    single = jax.ShapeDtypeStruct((TOK_DEV, HD), jnp.bfloat16)
    return pl.pallas_call(
        finish_kernel,
        out_shape=(single, single, jax.ShapeDtypeStruct((TOK_DEV, heads * HD), jnp.bfloat16)),
        in_specs=[whole] * 5,
        out_specs=(whole,) * 3,
        compiler_params=pltpu.CompilerParams(vmem_limit_bytes=6 << 20),
        name="attend",
    )(
        pick,
        arrived,
        jnp.concatenate([cosine, cosine], axis=1),
        jnp.concatenate([-sine, sine], axis=1),
        allowed.astype(jnp.float32),
    )


def paired(sent_rows, norm_gain, qkv_weight, groups):
    part = lax.axis_index("parts")
    group = lax.axis_index("dp")
    at = jnp.stack([group // 2, group % 2, part, lax.axis_index("tensor")]).astype(jnp.int32)
    turned = qkv_weight.T
    depth = turned.shape[1]
    count = turned.shape[0] // (2 * BLOCK)
    size = count * BLOCK
    mine = lax.dynamic_index_in_dim(
        turned.reshape(count, 2, BLOCK, depth), part, 1, False
    ).reshape(size, depth)
    swap = [(0, 1), (1, 0)]
    cut_at = sent_rows.shape[0] // 4
    ahead = lax.ppermute(sent_rows[:cut_at], "parts", swap)
    scale = scale_of(lax.psum(squares(sent_rows), "tensor"))
    early, late, (ahead, rest, scale) = gather_line(mine, (ahead, sent_rows[cut_at:], scale))
    behind = lax.ppermute(rest, "parts", swap)
    their_scale = lax.ppermute(scale, "parts", swap)
    slots = sent_rows.shape[0]
    width = groups * size
    whole = pl.BlockSpec(memory_space=pltpu.VMEM)
    scalars = pl.BlockSpec(memory_space=pltpu.SMEM)
    heads = width * HQ // (HQ + 2)
    half = jax.ShapeDtypeStruct((2 * slots, heads // 2 + width - heads), jnp.float32)
    keep, send, rows = pl.pallas_call(
        early_kernel,
        out_shape=(half, half, jax.ShapeDtypeStruct((2 * slots, depth), jnp.bfloat16)),
        in_specs=[scalars] + [whole] * 15,
        out_specs=(whole,) * 3,
        scratch_shapes=[pltpu.VMEM((width, depth), jnp.bfloat16)],
        compiler_params=pltpu.CompilerParams(vmem_limit_bytes=28 << 20),
        cost_estimate=pl.CostEstimate(
            flops=4 * slots * width * depth, bytes_accessed=12 << 20, transcendentals=0
        ),
        name="project_early",
    )(
        at,
        *early,
        sent_rows,
        ahead,
        behind,
        scale[None, :],
        their_scale[None, :],
        norm_gain[None, :],
    )
    keep, send = pl.pallas_call(
        late_kernel,
        out_shape=(half, half),
        in_specs=[scalars] + [whole] * 5,
        out_specs=(whole, whole),
        scratch_shapes=[pltpu.VMEM((heads // 2, depth), jnp.bfloat16)],
        input_output_aliases={1: 0, 2: 1},
        compiler_params=pltpu.CompilerParams(vmem_limit_bytes=16 << 20),
        cost_estimate=pl.CostEstimate(
            flops=2 * slots * heads * depth, bytes_accessed=6 << 20, transcendentals=0
        ),
        name="project_late",
    )(at, keep, send, *late, rows)
    ready = pl.pallas_call(
        sum_kernel,
        out_shape=jax.ShapeDtypeStruct(keep.shape, jnp.bfloat16),
        in_specs=[whole, whole],
        out_specs=whole,
        compiler_params=pltpu.CompilerParams(vmem_limit_bytes=6 << 20),
        name="sum_halves",
    )(keep, lax.ppermute(send, "tensor", swap))
    arrived = lax.all_to_all(ready, ("parts", "dp"), 0, 0, tiled=True)
    return arrived.reshape(2, slots, half.shape[1])


def single(sent_rows, norm_gain, qkv_weight):
    columns = lax.all_gather(qkv_weight.T, "dp", axis=0, tiled=True)
    scale = scale_of(lax.psum(squares(sent_rows), "tensor"))
    ready = sum_cores(product(scaled(sent_rows, scale[:, None], norm_gain[None, :]), columns))
    return lax.all_to_all(ready, "dp", 0, 0, tiled=True)


def per_device(sent_rows, norm_gain, qkv_weight, route_counts, response_lengths, prefix_lengths):
    groups = lax.axis_size("dp")
    slot = sent_rows.shape[0] // groups
    column = lax.dynamic_slice_in_dim(route_counts, lax.axis_index("dp"), 1, 1)[:, 0]
    pick = pick_of(column, slot, TOK_DEV)
    sequence, position = positions_of(response_lengths[0], prefix_lengths[0], TOK_DEV)
    allowed = (sequence[:, None] == sequence[None, :]) & (position[None, :] <= position[:, None])
    cosine, sine = rotary(position)
    if lax.axis_size("parts") == 2 and groups == 8 and qkv_weight.shape[1] == 160:
        arrived = paired(sent_rows, norm_gain, qkv_weight, groups)
        return finish(pick, arrived, cosine, sine, allowed)
    arrived = single(sent_rows, norm_gain, qkv_weight)
    heads = arrived.shape[1] // HD
    packed = jnp.dot(pick, arrived, preferred_element_type=jnp.float32)
    packed = packed.reshape(TOK_DEV, heads, HD)
    queries = rotate(packed[:, :-2], cosine, sine).astype(jnp.bfloat16)
    new_keys = rotate(packed[:, -2], cosine, sine).astype(jnp.bfloat16)
    new_values = packed[:, -1].astype(jnp.bfloat16)
    out = attend(queries, new_keys, new_values, allowed)
    return (new_keys, new_values, out.reshape(TOK_DEV, (heads - 2) * HD))


def solution(mesh):
    in_specs = (
        P(("parts", "dp"), "tensor"),
        P("tensor"),
        P("tensor", "dp"),
        P("parts", None),
        P(("parts", "dp"), None),
        P(("parts", "dp"), None),
    )
    out_specs = (P(("parts", "dp"), None), P(("parts", "dp"), None), P(("parts", "dp"), "tensor"))
    return jax.shard_map(
        per_device, mesh=mesh, in_specs=in_specs, out_specs=out_specs, check_vma=False
    )
```

```python
import math

import jax
import jax.numpy as jnp
from jax import lax
from jax.experimental import pallas as pl
from jax.experimental.pallas import tpu as pltpu
from jax.sharding import PartitionSpec as P

D = 8192
HD = 128
HQ = 8
TOK_DEV = 128
BLOCK = 16


def rotary(positions):
    half = HD // 2
    freq = jnp.exp(-jnp.log(500000.0) * jnp.arange(half, dtype=jnp.float32) * 2.0 / HD)
    angle = positions.astype(jnp.float32)[:, None] * freq[None, :]
    return (jnp.cos(angle), jnp.sin(angle))


def rotate(block, cosine, sine):
    half = HD // 2
    if block.ndim == 3:
        cosine = cosine[:, None, :]
        sine = sine[:, None, :]
    first = block[..., :half]
    second = block[..., half:]
    return jnp.concatenate(
        [first * cosine - second * sine, second * cosine + first * sine], axis=-1
    )


def members(lengths, count):
    ends = jnp.cumsum(lengths)
    starts = ends - lengths
    place = jnp.arange(count, dtype=jnp.int32)
    member = (place[:, None] >= starts[None, :]) & (place[:, None] < ends[None, :])
    return (member, place[:, None] - starts[None, :])


def positions_of(lengths, prefix, count):
    member, within = members(lengths, count)
    which = jnp.arange(lengths.shape[0], dtype=jnp.int32)
    sequence = jnp.sum(jnp.where(member, which[None, :], 0), axis=1)
    position = jnp.sum(jnp.where(member, prefix[None, :] + within, 0), axis=1)
    return (sequence, position)


def pick_of(column, slot, count):
    member, within = members(column, count)
    source = jnp.arange(column.shape[0], dtype=jnp.int32)
    index = jnp.sum(jnp.where(member, source[None, :] * slot + within, 0), axis=1)
    slots = jnp.arange(column.shape[0] * slot, dtype=jnp.int32)
    return (index[:, None] == slots[None, :]).astype(jnp.bfloat16)


def attend(queries, keys, values, allowed):
    scores = jnp.einsum(
        "qhd,kd->hqk", queries, keys, preferred_element_type=jnp.float32
    ) / jnp.sqrt(jnp.float32(HD))
    scores = jnp.where(allowed[None, :, :], scores, jnp.float32(-1e30))
    top = jnp.max(scores, axis=-1, keepdims=True)
    expo = jnp.exp(scores - top)
    weights = (expo / jnp.sum(expo, axis=-1, keepdims=True)).astype(jnp.bfloat16)
    out = jnp.einsum("hqk,kd->qhd", weights, values, preferred_element_type=jnp.float32)
    return out.astype(jnp.bfloat16)


def squares(rows):
    wide = rows.astype(jnp.float32)
    return jnp.sum(wide * wide, axis=1)


def scale_of(total):
    return lax.rsqrt(total / D + 1e-05)


def scaled(rows, scale, norm_gain):
    return (rows.astype(jnp.float32) * scale * norm_gain).astype(jnp.bfloat16)


def product(rows, columns):
    return lax.dot_general(
        rows, columns, (((1,), (1,)), ((), ())), preferred_element_type=jnp.float32
    )


def cut(partial, width, core):
    share = width // lax.axis_size("tensor")
    mine = lax.dynamic_slice_in_dim(partial, core * share, share, 1)
    return jnp.concatenate([mine, partial[:, width:]], axis=1)


def sum_cores(partial):
    width = HQ * HD * partial.shape[1] // (HQ * HD + 2 * HD)
    core = lax.axis_index("tensor")
    other = lax.ppermute(cut(partial, width, 1 - core), "tensor", [(0, 1), (1, 0)])
    return (cut(partial, width, core) + other).astype(jnp.bfloat16)


def over(block, places):
    return lax.ppermute(block, "dp", [(2 * z + x, 2 * z + 1 - x) for z in places for x in range(2)])


def along(block, moves):
    return lax.ppermute(block, "dp", [(2 * a + x, 2 * b + x) for a, b in moves for x in range(2)])


PAIRS = ((0, 1), (1, 0), (2, 3), (3, 2))
ACROSS = ((1, 2), (2, 1))
OUTWARD = ((1, 0), (2, 3))
ENDS = (0, 3)
MIDDLE = (1, 2)


def overs(places):
    return [(2 * z + x, 2 * z + 1 - x) for z in places for x in range(2)]


def alongs(moves):
    return [(2 * a + x, 2 * b + x) for a, b in moves for x in range(2)]


def gather_line(mine, first):
    def send(block, pairs):
        return lax.ppermute(block, "dp", pairs)

    near = send(mine, alongs(PAIRS))
    cross = send(mine, alongs(ACROSS) + overs(ENDS))
    side = send(mine, overs(MIDDLE))
    near, cross, side, first = lax.optimization_barrier((near, cross, side, first))
    second = send(cross, alongs(PAIRS))
    onward = send(near, alongs(ACROSS) + overs(ENDS))
    cross_over = send(cross, overs(MIDDLE))
    last = send(onward, alongs(OUTWARD))
    onward, cross_over = lax.optimization_barrier((onward, cross_over))
    far_over = send(onward, overs(MIDDLE))
    second_over = send(second, overs(ENDS))
    last_over = send(last, overs(ENDS))
    early = (mine, near, cross, side, second, onward, cross_over, far_over, second_over)
    return early, (last, last_over), first


def early_kernel(
    at, mine, near, cross, side, second, onward, cross_over, far_over, second_over,
    own, ahead, behind, own_scale, their_scale, gain, keep, send, rows,
    raw, whole, row_sems, sems,
):
    z, x, part, core = at[0], at[1], at[2], at[3]
    size = mine.shape[0]
    count = own.shape[0]
    cut_at = ahead.shape[0]
    arrivals = (
        pltpu.make_async_copy(own, raw.at[pl.ds(0, count)], row_sems.at[0]),
        pltpu.make_async_copy(ahead, raw.at[pl.ds(count, cut_at)], row_sems.at[1]),
        pltpu.make_async_copy(
            behind, raw.at[pl.ds(count + cut_at, count - cut_at)], row_sems.at[2]
        ),
    )
    for copy in arrivals:
        copy.start()

    def place(pairs):
        for where, pieces in pairs:
            for j, piece in enumerate(pieces):
                index = 2 * where + (x if j == 0 else 1 - x)
                start = pl.multiple_of(index * size, BLOCK)
                pltpu.make_async_copy(
                    piece, whole.at[pl.ds(start, size)], sems.at[index]
                ).start()

    at_end = (z == 0) | (z == 3)
    pair = z + 1 - 2 * (z % 2)

    @pl.when(at_end)
    def _():
        place(
            (
                (z, (mine, cross)),
                (pair, (near, onward)),
                ((z + 2) % 4, (second, second_over)),
                (3 - z, (mine, cross)),
            )
        )

    @pl.when(jnp.logical_not(at_end))
    def _():
        place(
            (
                (z, (mine, side)),
                (pair, (near, second)),
                ((z + 2) % 4, (onward, far_over)),
                (3 - z, (cross, cross_over)),
            )
        )

    for k, (index, scale, waits) in enumerate(
        ((part, own_scale, arrivals[:1]), (1 - part, their_scale, arrivals[1:]))
    ):
        upright = jnp.broadcast_to(scale[...], (HD, count)).T[:, :1]
        for copy in waits:
            copy.wait()
        for low in range(0, count, BLOCK):
            start = pl.multiple_of(index * count + low, BLOCK)
            rows[pl.ds(start, BLOCK), :] = scaled(
                raw[k * count + low : k * count + low + BLOCK, :],
                upright[low : low + BLOCK, :],
                gain[...],
            )

    share = whole.shape[0] * HQ // (HQ + 2) // 2
    held = 0
    for low, high in ((0, share), (share, 2 * share), (2 * share, whole.shape[0])):
        while held * size < high:
            pltpu.make_async_copy(
                mine, whole.at[pl.ds(held * size, size)], sems.at[held]
            ).wait()
            held += 1
        block = product(rows[...], whole[low:high, :])
        if low == 2 * share:
            keep[:, share:] = block
            send[:, share:] = block
        else:

            @pl.when(core == low // share)
            def _():
                keep[:, :share] = block

            @pl.when(core != low // share)
            def _():
                send[:, :share] = block


def late_kernel(at, first_keep, first_send, piece, piece_over, rows, keep, send, last, sems):
    z, x, core = at[0], at[1], at[3]
    size = piece.shape[0]
    share = last.shape[0]
    edge = 2 * size
    gap = share - edge

    def fetch(offset):
        found = []
        for side, ref in ((0, piece), (1, piece_over)):
            where = x if side == 0 else 1 - x
            start = pl.multiple_of(offset + where * size, BLOCK)
            copy = pltpu.make_async_copy(ref, last.at[pl.ds(start, size)], sems.at[side])
            copy.start()
            found.append(copy)
        for copy in found:
            copy.wait()
        return product(rows[...], last[...])

    def merge(ref, source, lanes, block, new):
        ref[:, lanes] = jnp.where(new, block, source[:, lanes])

    keep[...] = first_keep[...]
    send[...] = first_send[...]
    lane = lax.broadcasted_iota(jnp.int32, (rows.shape[0], share), 1)

    @pl.when(z == 0)
    def _():
        block = fetch(gap)
        for ref in (keep, send):
            ref[:, share:] = block[:, share // 2 :]
        head = block[:, : share // 2]
        new = lane[:, : share // 2] >= gap
        lanes = slice(share // 2, share)

        @pl.when(core == 1)
        def _():
            merge(keep, first_keep, lanes, head, new)

        @pl.when(core == 0)
        def _():
            merge(send, first_send, lanes, head, new)

    @pl.when(z == 3)
    def _():
        block = fetch(0)
        lanes = slice(0, share)

        @pl.when(core == 0)
        def _():
            merge(keep, first_keep, lanes, block, lane < edge)

        @pl.when(core == 1)
        def _():
            merge(send, first_send, lanes, block, lane < edge)


def sum_kernel(keep, other, out):
    out[...] = (keep[...] + other[...]).astype(out.dtype)


def finish_kernel(pick, arrived, cosine, sine, allowed, keys, values, out):
    width = arrived.shape[2]
    count = 2 * width // HD
    chosen = pick[...]
    planes = [
        jnp.dot(chosen, arrived[y], preferred_element_type=jnp.float32).astype(jnp.bfloat16)
        for y in range(2)
    ]
    source = lax.broadcasted_iota(jnp.int32, (HD, 2 * HD), 0)
    target = lax.broadcasted_iota(jnp.int32, (HD, 2 * HD), 1)
    heads = []
    for pair in range(count // 2):
        total = None
        for y in range(2):
            place = source // BLOCK * (2 * BLOCK) + y * BLOCK + source % BLOCK
            order = (place == target).astype(jnp.float32).astype(jnp.bfloat16)
            part = jnp.dot(
                planes[y][:, pair * HD : (pair + 1) * HD],
                order,
                preferred_element_type=jnp.float32,
            )
            total = part if total is None else total + part
        heads += [total[:, :HD], total[:, HD:]]

    def turn(block):
        other = pltpu.roll(block, HD // 2, 1)
        return (block * cosine[...] + other * sine[...]).astype(jnp.bfloat16)

    key = turn(heads[-2])
    value = heads[-1].astype(jnp.bfloat16)
    keys[...] = key
    values[...] = value
    mask = allowed[...] > 0
    for h in range(count - 2):
        scores = product(turn(heads[h]), key) / math.sqrt(HD)
        scores = jnp.where(mask, scores, jnp.float32(-1e30))
        expo = jnp.exp(scores - jnp.max(scores, axis=-1, keepdims=True))
        weights = (expo / jnp.sum(expo, axis=-1, keepdims=True)).astype(jnp.bfloat16)
        out[:, h * HD : (h + 1) * HD] = jnp.dot(
            weights, value, preferred_element_type=jnp.float32
        ).astype(out.dtype)


def finish(pick, arrived, cosine, sine, allowed):
    whole = pl.BlockSpec(memory_space=pltpu.VMEM)
    heads = 2 * arrived.shape[2] // HD - 2
    single = jax.ShapeDtypeStruct((TOK_DEV, HD), jnp.bfloat16)
    return pl.pallas_call(
        finish_kernel,
        out_shape=(single, single, jax.ShapeDtypeStruct((TOK_DEV, heads * HD), jnp.bfloat16)),
        in_specs=[whole] * 5,
        out_specs=(whole,) * 3,
        compiler_params=pltpu.CompilerParams(vmem_limit_bytes=6 << 20),
        name="attend",
    )(
        pick,
        arrived,
        jnp.concatenate([cosine, cosine], axis=1),
        jnp.concatenate([-sine, sine], axis=1),
        allowed.astype(jnp.float32),
    )


def paired(sent_rows, norm_gain, qkv_weight, groups):
    part = lax.axis_index("parts")
    group = lax.axis_index("dp")
    at = jnp.stack([group // 2, group % 2, part, lax.axis_index("tensor")]).astype(jnp.int32)
    turned = qkv_weight.T
    depth = turned.shape[1]
    count = turned.shape[0] // (2 * BLOCK)
    size = count * BLOCK
    mine = lax.dynamic_index_in_dim(
        turned.reshape(count, 2, BLOCK, depth), part, 1, False
    ).reshape(size, depth)
    swap = [(0, 1), (1, 0)]
    cut_at = sent_rows.shape[0] // 8
    ahead = lax.ppermute(sent_rows[:cut_at], "parts", swap)
    scale = scale_of(lax.psum(squares(sent_rows), "tensor"))
    their_scale = lax.ppermute(scale, "parts", swap)
    early, late, (ahead, rest, their_scale) = gather_line(
        mine, (ahead, sent_rows[cut_at:], their_scale)
    )
    behind = lax.ppermute(rest, "parts", swap)
    slots = sent_rows.shape[0]
    width = groups * size
    whole = pl.BlockSpec(memory_space=pltpu.VMEM)
    anywhere = pl.BlockSpec(memory_space=pl.ANY)
    scalars = pl.BlockSpec(memory_space=pltpu.SMEM)
    heads = width * HQ // (HQ + 2)
    half = jax.ShapeDtypeStruct((2 * slots, heads // 2 + width - heads), jnp.float32)
    keep, send, rows = pl.pallas_call(
        early_kernel,
        out_shape=(half, half, jax.ShapeDtypeStruct((2 * slots, depth), jnp.bfloat16)),
        in_specs=[scalars] + [anywhere] * 12 + [whole] * 3,
        out_specs=(whole,) * 3,
        scratch_shapes=[
            pltpu.VMEM((2 * slots, depth), jnp.bfloat16),
            pltpu.VMEM((width, depth), jnp.bfloat16),
            pltpu.SemaphoreType.DMA((3,)),
            pltpu.SemaphoreType.DMA((groups,)),
        ],
        compiler_params=pltpu.CompilerParams(vmem_limit_bytes=28 << 20),
        cost_estimate=pl.CostEstimate(
            flops=4 * slots * width * depth, bytes_accessed=12 << 20, transcendentals=0
        ),
        name="project_early",
    )(
        at,
        *early,
        sent_rows,
        ahead,
        behind,
        scale[None, :],
        their_scale[None, :],
        norm_gain[None, :],
    )
    keep, send = pl.pallas_call(
        late_kernel,
        out_shape=(half, half),
        in_specs=[scalars] + [whole] * 2 + [anywhere] * 2 + [whole],
        out_specs=(whole, whole),
        scratch_shapes=[
            pltpu.VMEM((heads // 2, depth), jnp.bfloat16),
            pltpu.SemaphoreType.DMA((2,)),
        ],
        input_output_aliases={1: 0, 2: 1},
        compiler_params=pltpu.CompilerParams(vmem_limit_bytes=16 << 20),
        cost_estimate=pl.CostEstimate(
            flops=2 * slots * heads * depth, bytes_accessed=6 << 20, transcendentals=0
        ),
        name="project_late",
    )(at, keep, send, *late, rows)
    ready = pl.pallas_call(
        sum_kernel,
        out_shape=jax.ShapeDtypeStruct(keep.shape, jnp.bfloat16),
        in_specs=[whole, whole],
        out_specs=whole,
        compiler_params=pltpu.CompilerParams(vmem_limit_bytes=6 << 20),
        name="sum_halves",
    )(keep, lax.ppermute(send, "tensor", swap))
    arrived = lax.all_to_all(ready, ("parts", "dp"), 0, 0, tiled=True)
    return arrived.reshape(2, slots, half.shape[1])


def single(sent_rows, norm_gain, qkv_weight):
    columns = lax.all_gather(qkv_weight.T, "dp", axis=0, tiled=True)
    scale = scale_of(lax.psum(squares(sent_rows), "tensor"))
    ready = sum_cores(product(scaled(sent_rows, scale[:, None], norm_gain[None, :]), columns))
    return lax.all_to_all(ready, "dp", 0, 0, tiled=True)


def per_device(sent_rows, norm_gain, qkv_weight, route_counts, response_lengths, prefix_lengths):
    groups = lax.axis_size("dp")
    slot = sent_rows.shape[0] // groups
    column = lax.dynamic_slice_in_dim(route_counts, lax.axis_index("dp"), 1, 1)[:, 0]
    pick = pick_of(column, slot, TOK_DEV)
    sequence, position = positions_of(response_lengths[0], prefix_lengths[0], TOK_DEV)
    allowed = (sequence[:, None] == sequence[None, :]) & (position[None, :] <= position[:, None])
    cosine, sine = rotary(position)
    if lax.axis_size("parts") == 2 and groups == 8 and qkv_weight.shape[1] == 160:
        arrived = paired(sent_rows, norm_gain, qkv_weight, groups)
        return finish(pick, arrived, cosine, sine, allowed)
    arrived = single(sent_rows, norm_gain, qkv_weight)
    heads = arrived.shape[1] // HD
    packed = jnp.dot(pick, arrived, preferred_element_type=jnp.float32)
    packed = packed.reshape(TOK_DEV, heads, HD)
    queries = rotate(packed[:, :-2], cosine, sine).astype(jnp.bfloat16)
    new_keys = rotate(packed[:, -2], cosine, sine).astype(jnp.bfloat16)
    new_values = packed[:, -1].astype(jnp.bfloat16)
    out = attend(queries, new_keys, new_values, allowed)
    return (new_keys, new_values, out.reshape(TOK_DEV, (heads - 2) * HD))


def solution(mesh):
    in_specs = (
        P(("parts", "dp"), "tensor"),
        P("tensor"),
        P("tensor", "dp"),
        P("parts", None),
        P(("parts", "dp"), None),
        P(("parts", "dp"), None),
    )
    out_specs = (P(("parts", "dp"), None), P(("parts", "dp"), None), P(("parts", "dp"), "tensor"))
    return jax.shard_map(
        per_device, mesh=mesh, in_specs=in_specs, out_specs=out_specs, check_vma=False
    )
```

```python
import math

import jax
import jax.numpy as jnp
from jax import lax
from jax.experimental import pallas as pl
from jax.experimental.pallas import tpu as pltpu
from jax.sharding import PartitionSpec as P

D = 8192
HD = 128
HQ = 8
TOK_DEV = 128
BLOCK = 16


def rotary(positions):
    half = HD // 2
    freq = jnp.exp(-jnp.log(500000.0) * jnp.arange(half, dtype=jnp.float32) * 2.0 / HD)
    angle = positions.astype(jnp.float32)[:, None] * freq[None, :]
    return (jnp.cos(angle), jnp.sin(angle))


def rotate(block, cosine, sine):
    half = HD // 2
    if block.ndim == 3:
        cosine = cosine[:, None, :]
        sine = sine[:, None, :]
    first = block[..., :half]
    second = block[..., half:]
    return jnp.concatenate(
        [first * cosine - second * sine, second * cosine + first * sine], axis=-1
    )


def members(lengths, count):
    ends = jnp.cumsum(lengths)
    starts = ends - lengths
    place = jnp.arange(count, dtype=jnp.int32)
    member = (place[:, None] >= starts[None, :]) & (place[:, None] < ends[None, :])
    return (member, place[:, None] - starts[None, :])


def positions_of(lengths, prefix, count):
    member, within = members(lengths, count)
    which = jnp.arange(lengths.shape[0], dtype=jnp.int32)
    sequence = jnp.sum(jnp.where(member, which[None, :], 0), axis=1)
    position = jnp.sum(jnp.where(member, prefix[None, :] + within, 0), axis=1)
    return (sequence, position)


def pick_of(column, slot, count):
    member, within = members(column, count)
    source = jnp.arange(column.shape[0], dtype=jnp.int32)
    index = jnp.sum(jnp.where(member, source[None, :] * slot + within, 0), axis=1)
    slots = jnp.arange(column.shape[0] * slot, dtype=jnp.int32)
    return (index[:, None] == slots[None, :]).astype(jnp.bfloat16)


def attend(queries, keys, values, allowed):
    scores = jnp.einsum(
        "qhd,kd->hqk", queries, keys, preferred_element_type=jnp.float32
    ) / jnp.sqrt(jnp.float32(HD))
    scores = jnp.where(allowed[None, :, :], scores, jnp.float32(-1e30))
    top = jnp.max(scores, axis=-1, keepdims=True)
    expo = jnp.exp(scores - top)
    weights = (expo / jnp.sum(expo, axis=-1, keepdims=True)).astype(jnp.bfloat16)
    out = jnp.einsum("hqk,kd->qhd", weights, values, preferred_element_type=jnp.float32)
    return out.astype(jnp.bfloat16)


def squares(rows):
    wide = rows.astype(jnp.float32)
    return jnp.sum(wide * wide, axis=1)


def scale_of(total):
    return lax.rsqrt(total / D + 1e-05)


def scaled(rows, scale, norm_gain):
    return (rows.astype(jnp.float32) * scale * norm_gain).astype(jnp.bfloat16)


def product(rows, columns):
    return lax.dot_general(
        rows, columns, (((1,), (1,)), ((), ())), preferred_element_type=jnp.float32
    )


def cut(partial, width, core):
    share = width // lax.axis_size("tensor")
    mine = lax.dynamic_slice_in_dim(partial, core * share, share, 1)
    return jnp.concatenate([mine, partial[:, width:]], axis=1)


def sum_cores(partial):
    width = HQ * HD * partial.shape[1] // (HQ * HD + 2 * HD)
    core = lax.axis_index("tensor")
    other = lax.ppermute(cut(partial, width, 1 - core), "tensor", [(0, 1), (1, 0)])
    return (cut(partial, width, core) + other).astype(jnp.bfloat16)


def over(block, places):
    return lax.ppermute(block, "dp", [(2 * z + x, 2 * z + 1 - x) for z in places for x in range(2)])


def along(block, moves):
    return lax.ppermute(block, "dp", [(2 * a + x, 2 * b + x) for a, b in moves for x in range(2)])


PAIRS = ((0, 1), (1, 0), (2, 3), (3, 2))
ACROSS = ((1, 2), (2, 1))
OUTWARD = ((1, 0), (2, 3))
ENDS = (0, 3)
MIDDLE = (1, 2)


def overs(places):
    return [(2 * z + x, 2 * z + 1 - x) for z in places for x in range(2)]


def alongs(moves):
    return [(2 * a + x, 2 * b + x) for a, b in moves for x in range(2)]


def gather_line(mine, first):
    def send(block, pairs):
        return lax.ppermute(block, "dp", pairs)

    near = send(mine, alongs(PAIRS))
    cross = send(mine, alongs(ACROSS) + overs(ENDS))
    side = send(mine, overs(MIDDLE))
    near, cross, first = lax.optimization_barrier((near, cross, first))
    second = send(cross, alongs(PAIRS))
    onward = send(near, alongs(ACROSS) + overs(ENDS))
    cross_next, side = lax.optimization_barrier((cross, side))
    cross_over = send(cross_next, overs(MIDDLE))
    onward_next, _ = lax.optimization_barrier((onward, second))
    last = send(onward_next, alongs(OUTWARD))
    second_over = send(second, overs(ENDS))
    onward_next, _ = lax.optimization_barrier((onward, cross_over))
    far_over = send(onward_next, overs(MIDDLE))
    last_over = send(last, overs(ENDS))
    early = (mine, near, cross, side, second, onward, cross_over, far_over, second_over)
    return early, (last, last_over), first


def early_kernel(
    at, mine, near, cross, side, second, onward, cross_over, far_over, second_over,
    own, ahead, behind, own_scale, their_scale, gain, keep, send, rows, whole,
):
    z, x, part, core = at[0], at[1], at[2], at[3]
    size = mine.shape[0]

    def place(pairs):
        for where, pieces in pairs:
            for j, piece in enumerate(pieces):
                column = x if j == 0 else 1 - x
                start = pl.multiple_of((2 * where + column) * size, BLOCK)
                whole[pl.ds(start, size), :] = piece[...]

    count = own.shape[0]
    for index, sources, scale in (
        (part, (own,), own_scale),
        (1 - part, (ahead, behind), their_scale),
    ):
        upright = jnp.broadcast_to(scale[...], (HD, count)).T[:, :1]
        done = 0
        for source in sources:
            for low in range(0, source.shape[0], BLOCK):
                start = pl.multiple_of(index * count + done + low, BLOCK)
                rows[pl.ds(start, BLOCK), :] = scaled(
                    source[low : low + BLOCK, :],
                    upright[done + low : done + low + BLOCK, :],
                    gain[...],
                )
            done += source.shape[0]

    at_end = (z == 0) | (z == 3)
    pair = z + 1 - 2 * (z % 2)

    @pl.when(at_end)
    def _():
        place(
            (
                (z, (mine, cross)),
                (pair, (near, onward)),
                ((z + 2) % 4, (second, second_over)),
                (3 - z, (mine, cross)),
            )
        )

    @pl.when(jnp.logical_not(at_end))
    def _():
        place(
            (
                (z, (mine, side)),
                (pair, (near, second)),
                ((z + 2) % 4, (onward, far_over)),
                (3 - z, (cross, cross_over)),
            )
        )

    share = whole.shape[0] * HQ // (HQ + 2) // 2
    halves = [product(rows[...], whole[c * share : (c + 1) * share, :]) for c in range(2)]
    rest = product(rows[...], whole[2 * share :, :])
    for ref in (keep, send):
        ref[:, share:] = rest
    for t in range(2):

        @pl.when(core == t)
        def _():
            keep[:, :share] = halves[t]
            send[:, :share] = halves[1 - t]


def late_kernel(at, first_keep, first_send, piece, piece_over, rows, keep, send, last):
    z, x, core = at[0], at[1], at[3]
    size = piece.shape[0]
    share = last.shape[0]
    edge = 2 * size
    gap = share - edge

    def fetch(offset):
        for side, ref in ((0, piece), (1, piece_over)):
            where = x if side == 0 else 1 - x
            start = pl.multiple_of(offset + where * size, BLOCK)
            last[pl.ds(start, size), :] = ref[...]
        return product(rows[...], last[...])

    def merge(ref, source, lanes, block, new):
        ref[:, lanes] = jnp.where(new, block, source[:, lanes])

    keep[...] = first_keep[...]
    send[...] = first_send[...]
    lane = lax.broadcasted_iota(jnp.int32, (rows.shape[0], share), 1)

    @pl.when(z == 0)
    def _():
        block = fetch(gap)
        for ref in (keep, send):
            ref[:, share:] = block[:, share // 2 :]
        head = block[:, : share // 2]
        new = lane[:, : share // 2] >= gap
        lanes = slice(share // 2, share)

        @pl.when(core == 1)
        def _():
            merge(keep, first_keep, lanes, head, new)

        @pl.when(core == 0)
        def _():
            merge(send, first_send, lanes, head, new)

    @pl.when(z == 3)
    def _():
        block = fetch(0)
        lanes = slice(0, share)

        @pl.when(core == 0)
        def _():
            merge(keep, first_keep, lanes, block, lane < edge)

        @pl.when(core == 1)
        def _():
            merge(send, first_send, lanes, block, lane < edge)


def sum_kernel(keep, other, out):
    out[...] = (keep[...] + other[...]).astype(out.dtype)


def finish_kernel(pick, arrived, cosine, sine, allowed, keys, values, out):
    width = arrived.shape[2]
    count = 2 * width // HD
    chosen = pick[...]
    planes = [
        jnp.dot(chosen, arrived[y], preferred_element_type=jnp.float32).astype(jnp.bfloat16)
        for y in range(2)
    ]
    source = lax.broadcasted_iota(jnp.int32, (HD, 2 * HD), 0)
    target = lax.broadcasted_iota(jnp.int32, (HD, 2 * HD), 1)
    heads = []
    for pair in range(count // 2):
        total = None
        for y in range(2):
            place = source // BLOCK * (2 * BLOCK) + y * BLOCK + source % BLOCK
            order = (place == target).astype(jnp.float32).astype(jnp.bfloat16)
            part = jnp.dot(
                planes[y][:, pair * HD : (pair + 1) * HD],
                order,
                preferred_element_type=jnp.float32,
            )
            total = part if total is None else total + part
        heads += [total[:, :HD], total[:, HD:]]

    def turn(block):
        other = pltpu.roll(block, HD // 2, 1)
        return (block * cosine[...] + other * sine[...]).astype(jnp.bfloat16)

    key = turn(heads[-2])
    value = heads[-1].astype(jnp.bfloat16)
    keys[...] = key
    values[...] = value
    mask = allowed[...] > 0
    for h in range(count - 2):
        scores = product(turn(heads[h]), key) / math.sqrt(HD)
        scores = jnp.where(mask, scores, jnp.float32(-1e30))
        expo = jnp.exp(scores - jnp.max(scores, axis=-1, keepdims=True))
        weights = (expo / jnp.sum(expo, axis=-1, keepdims=True)).astype(jnp.bfloat16)
        out[:, h * HD : (h + 1) * HD] = jnp.dot(
            weights, value, preferred_element_type=jnp.float32
        ).astype(out.dtype)


def finish(pick, arrived, cosine, sine, allowed):
    whole = pl.BlockSpec(memory_space=pltpu.VMEM)
    heads = 2 * arrived.shape[2] // HD - 2
    single = jax.ShapeDtypeStruct((TOK_DEV, HD), jnp.bfloat16)
    return pl.pallas_call(
        finish_kernel,
        out_shape=(single, single, jax.ShapeDtypeStruct((TOK_DEV, heads * HD), jnp.bfloat16)),
        in_specs=[whole] * 5,
        out_specs=(whole,) * 3,
        compiler_params=pltpu.CompilerParams(vmem_limit_bytes=6 << 20),
        name="attend",
    )(
        pick,
        arrived,
        jnp.concatenate([cosine, cosine], axis=1),
        jnp.concatenate([-sine, sine], axis=1),
        allowed.astype(jnp.float32),
    )


def paired(sent_rows, norm_gain, qkv_weight, groups):
    part = lax.axis_index("parts")
    group = lax.axis_index("dp")
    at = jnp.stack([group // 2, group % 2, part, lax.axis_index("tensor")]).astype(jnp.int32)
    turned = qkv_weight.T
    depth = turned.shape[1]
    count = turned.shape[0] // (2 * BLOCK)
    size = count * BLOCK
    swap = [(0, 1), (1, 0)]
    cut_at = sent_rows.shape[0] * 3 // 16
    whole = pl.BlockSpec(memory_space=pltpu.VMEM)
    anywhere = pl.BlockSpec(memory_space=pl.ANY)
    scalars = pl.BlockSpec(memory_space=pltpu.SMEM)
    mine = lax.dynamic_index_in_dim(
        turned.reshape(count, 2, BLOCK, depth), part, 1, False
    ).reshape(size, depth)
    ahead = sent_rows[:cut_at]
    ahead = lax.ppermute(ahead, "parts", swap)
    scale = scale_of(lax.psum(squares(sent_rows), "tensor"))
    their_scale = lax.ppermute(scale, "parts", swap)
    early, late, (ahead, rest, their_scale) = gather_line(
        mine, (ahead, sent_rows[cut_at:], their_scale)
    )
    behind = lax.ppermute(rest, "parts", swap)
    slots = sent_rows.shape[0]
    width = groups * size
    heads = width * HQ // (HQ + 2)
    half = jax.ShapeDtypeStruct((2 * slots, heads // 2 + width - heads), jnp.float32)
    keep, send, rows = pl.pallas_call(
        early_kernel,
        out_shape=(half, half, jax.ShapeDtypeStruct((2 * slots, depth), jnp.bfloat16)),
        in_specs=[scalars] + [whole] * 15,
        out_specs=(whole,) * 3,
        scratch_shapes=[pltpu.VMEM((width, depth), jnp.bfloat16)],
        compiler_params=pltpu.CompilerParams(vmem_limit_bytes=28 << 20),
        cost_estimate=pl.CostEstimate(
            flops=4 * slots * width * depth, bytes_accessed=12 << 20, transcendentals=0
        ),
        name="project_early",
    )(
        at,
        *early,
        sent_rows,
        ahead,
        behind,
        scale[None, :],
        their_scale[None, :],
        norm_gain[None, :],
    )
    keep, send = pl.pallas_call(
        late_kernel,
        out_shape=(half, half),
        in_specs=[scalars] + [whole] * 5,
        out_specs=(whole, whole),
        scratch_shapes=[pltpu.VMEM((heads // 2, depth), jnp.bfloat16)],
        input_output_aliases={1: 0, 2: 1},
        compiler_params=pltpu.CompilerParams(vmem_limit_bytes=16 << 20),
        cost_estimate=pl.CostEstimate(
            flops=2 * slots * heads * depth, bytes_accessed=6 << 20, transcendentals=0
        ),
        name="project_late",
    )(at, keep, send, *late, rows)
    ready = pl.pallas_call(
        sum_kernel,
        out_shape=jax.ShapeDtypeStruct(keep.shape, jnp.bfloat16),
        in_specs=[whole, whole],
        out_specs=whole,
        compiler_params=pltpu.CompilerParams(vmem_limit_bytes=6 << 20),
        name="sum_halves",
    )(keep, lax.ppermute(send, "tensor", swap))
    arrived = lax.all_to_all(ready, ("parts", "dp"), 0, 0, tiled=True)
    return arrived.reshape(2, slots, half.shape[1])


def single(sent_rows, norm_gain, qkv_weight):
    columns = lax.all_gather(qkv_weight.T, "dp", axis=0, tiled=True)
    scale = scale_of(lax.psum(squares(sent_rows), "tensor"))
    ready = sum_cores(product(scaled(sent_rows, scale[:, None], norm_gain[None, :]), columns))
    return lax.all_to_all(ready, "dp", 0, 0, tiled=True)


def per_device(sent_rows, norm_gain, qkv_weight, route_counts, response_lengths, prefix_lengths):
    groups = lax.axis_size("dp")
    slot = sent_rows.shape[0] // groups
    column = lax.dynamic_slice_in_dim(route_counts, lax.axis_index("dp"), 1, 1)[:, 0]
    pick = pick_of(column, slot, TOK_DEV)
    sequence, position = positions_of(response_lengths[0], prefix_lengths[0], TOK_DEV)
    allowed = (sequence[:, None] == sequence[None, :]) & (position[None, :] <= position[:, None])
    cosine, sine = rotary(position)
    if lax.axis_size("parts") == 2 and groups == 8 and qkv_weight.shape[1] == 160:
        arrived = paired(sent_rows, norm_gain, qkv_weight, groups)
        return finish(pick, arrived, cosine, sine, allowed)
    arrived = single(sent_rows, norm_gain, qkv_weight)
    heads = arrived.shape[1] // HD
    packed = jnp.dot(pick, arrived, preferred_element_type=jnp.float32)
    packed = packed.reshape(TOK_DEV, heads, HD)
    queries = rotate(packed[:, :-2], cosine, sine).astype(jnp.bfloat16)
    new_keys = rotate(packed[:, -2], cosine, sine).astype(jnp.bfloat16)
    new_values = packed[:, -1].astype(jnp.bfloat16)
    out = attend(queries, new_keys, new_values, allowed)
    return (new_keys, new_values, out.reshape(TOK_DEV, (heads - 2) * HD))


def solution(mesh):
    in_specs = (
        P(("parts", "dp"), "tensor"),
        P("tensor"),
        P("tensor", "dp"),
        P("parts", None),
        P(("parts", "dp"), None),
        P(("parts", "dp"), None),
    )
    out_specs = (P(("parts", "dp"), None), P(("parts", "dp"), None), P(("parts", "dp"), "tensor"))
    return jax.shard_map(
        per_device, mesh=mesh, in_specs=in_specs, out_specs=out_specs, check_vma=False
    )
```

```python
import math

import jax
import jax.numpy as jnp
from jax import lax
from jax.experimental import pallas as pl
from jax.experimental.pallas import tpu as pltpu
from jax.sharding import PartitionSpec as P

D = 8192
HD = 128
HQ = 8
TOK_DEV = 128
BLOCK = 16


def rotary(positions):
    half = HD // 2
    freq = jnp.exp(-jnp.log(500000.0) * jnp.arange(half, dtype=jnp.float32) * 2.0 / HD)
    angle = positions.astype(jnp.float32)[:, None] * freq[None, :]
    return (jnp.cos(angle), jnp.sin(angle))


def rotate(block, cosine, sine):
    half = HD // 2
    if block.ndim == 3:
        cosine = cosine[:, None, :]
        sine = sine[:, None, :]
    first = block[..., :half]
    second = block[..., half:]
    return jnp.concatenate(
        [first * cosine - second * sine, second * cosine + first * sine], axis=-1
    )


def members(lengths, count):
    ends = jnp.cumsum(lengths)
    starts = ends - lengths
    place = jnp.arange(count, dtype=jnp.int32)
    member = (place[:, None] >= starts[None, :]) & (place[:, None] < ends[None, :])
    return (member, place[:, None] - starts[None, :])


def positions_of(lengths, prefix, count):
    member, within = members(lengths, count)
    which = jnp.arange(lengths.shape[0], dtype=jnp.int32)
    sequence = jnp.sum(jnp.where(member, which[None, :], 0), axis=1)
    position = jnp.sum(jnp.where(member, prefix[None, :] + within, 0), axis=1)
    return (sequence, position)


def pick_of(column, slot, count):
    member, within = members(column, count)
    source = jnp.arange(column.shape[0], dtype=jnp.int32)
    index = jnp.sum(jnp.where(member, source[None, :] * slot + within, 0), axis=1)
    slots = jnp.arange(column.shape[0] * slot, dtype=jnp.int32)
    return (index[:, None] == slots[None, :]).astype(jnp.bfloat16)


def attend(queries, keys, values, allowed):
    scores = jnp.einsum(
        "qhd,kd->hqk", queries, keys, preferred_element_type=jnp.float32
    ) / jnp.sqrt(jnp.float32(HD))
    scores = jnp.where(allowed[None, :, :], scores, jnp.float32(-1e30))
    top = jnp.max(scores, axis=-1, keepdims=True)
    expo = jnp.exp(scores - top)
    weights = (expo / jnp.sum(expo, axis=-1, keepdims=True)).astype(jnp.bfloat16)
    out = jnp.einsum("hqk,kd->qhd", weights, values, preferred_element_type=jnp.float32)
    return out.astype(jnp.bfloat16)


def squares(rows):
    wide = rows.astype(jnp.float32)
    return jnp.sum(wide * wide, axis=1)


def scale_of(total):
    return lax.rsqrt(total / D + 1e-05)


def scaled(rows, scale, norm_gain):
    return (rows.astype(jnp.float32) * scale * norm_gain).astype(jnp.bfloat16)


def product(rows, columns):
    return lax.dot_general(
        rows, columns, (((1,), (1,)), ((), ())), preferred_element_type=jnp.float32
    )


def cut(partial, width, core):
    share = width // lax.axis_size("tensor")
    mine = lax.dynamic_slice_in_dim(partial, core * share, share, 1)
    return jnp.concatenate([mine, partial[:, width:]], axis=1)


def sum_cores(partial):
    width = HQ * HD * partial.shape[1] // (HQ * HD + 2 * HD)
    core = lax.axis_index("tensor")
    other = lax.ppermute(cut(partial, width, 1 - core), "tensor", [(0, 1), (1, 0)])
    return (cut(partial, width, core) + other).astype(jnp.bfloat16)


def over(block, places):
    return lax.ppermute(block, "dp", [(2 * z + x, 2 * z + 1 - x) for z in places for x in range(2)])


def along(block, moves):
    return lax.ppermute(block, "dp", [(2 * a + x, 2 * b + x) for a, b in moves for x in range(2)])


PAIRS = ((0, 1), (1, 0), (2, 3), (3, 2))
ACROSS = ((1, 2), (2, 1))
OUTWARD = ((1, 0), (2, 3))
ENDS = (0, 3)
MIDDLE = (1, 2)


def overs(places):
    return [(2 * z + x, 2 * z + 1 - x) for z in places for x in range(2)]


def alongs(moves):
    return [(2 * a + x, 2 * b + x) for a, b in moves for x in range(2)]


def gather_line(mine, first):
    def send(block, pairs):
        return lax.ppermute(block, "dp", pairs)

    near = send(mine, alongs(PAIRS))
    cross = send(mine, alongs(ACROSS) + overs(ENDS))
    side = send(mine, overs(MIDDLE))
    near, cross, first = lax.optimization_barrier((near, cross, first))
    second = send(cross, alongs(PAIRS))
    onward = send(near, alongs(ACROSS) + overs(ENDS))
    cross_next, side = lax.optimization_barrier((cross, side))
    cross_over = send(cross_next, overs(MIDDLE))
    onward_next, _ = lax.optimization_barrier((onward, second))
    last = send(onward_next, alongs(OUTWARD))
    second_next, _ = lax.optimization_barrier((second, cross_over))
    second_over = send(second_next, overs(ENDS))
    far_over = send(onward_next, overs(MIDDLE))
    last_over = send(last, overs(ENDS))
    early = (mine, near, cross, side, second, onward, cross_over, far_over, second_over)
    return early, (last, last_over), first


def early_kernel(
    at, mine, near, cross, side, second, onward, cross_over, far_over, second_over,
    own, ahead, behind, own_scale, their_scale, gain, keep, send, rows, whole,
):
    z, x, part, core = at[0], at[1], at[2], at[3]
    size = mine.shape[0]

    def place(pairs):
        for where, pieces in pairs:
            for j, piece in enumerate(pieces):
                column = x if j == 0 else 1 - x
                start = pl.multiple_of((2 * where + column) * size, BLOCK)
                whole[pl.ds(start, size), :] = piece[...]

    count = own.shape[0]
    for index, sources, scale in (
        (part, (own,), own_scale),
        (1 - part, (ahead, behind), their_scale),
    ):
        upright = jnp.broadcast_to(scale[...], (HD, count)).T[:, :1]
        done = 0
        for source in sources:
            for low in range(0, source.shape[0], BLOCK):
                start = pl.multiple_of(index * count + done + low, BLOCK)
                rows[pl.ds(start, BLOCK), :] = scaled(
                    source[low : low + BLOCK, :],
                    upright[done + low : done + low + BLOCK, :],
                    gain[...],
                )
            done += source.shape[0]

    at_end = (z == 0) | (z == 3)
    pair = z + 1 - 2 * (z % 2)

    @pl.when(at_end)
    def _():
        place(
            (
                (z, (mine, cross)),
                (pair, (near, onward)),
                ((z + 2) % 4, (second, second_over)),
                (3 - z, (mine, cross)),
            )
        )

    @pl.when(jnp.logical_not(at_end))
    def _():
        place(
            (
                (z, (mine, side)),
                (pair, (near, second)),
                ((z + 2) % 4, (onward, far_over)),
                (3 - z, (cross, cross_over)),
            )
        )

    share = whole.shape[0] * HQ // (HQ + 2) // 2
    halves = [product(rows[...], whole[c * share : (c + 1) * share, :]) for c in range(2)]
    rest = product(rows[...], whole[2 * share :, :])
    for ref in (keep, send):
        ref[:, share:] = rest
    for t in range(2):

        @pl.when(core == t)
        def _():
            keep[:, :share] = halves[t]
            send[:, :share] = halves[1 - t]


def late_kernel(at, first_keep, first_send, piece, piece_over, rows, keep, send, last):
    z, x, core = at[0], at[1], at[3]
    size = piece.shape[0]
    share = last.shape[0]
    edge = 2 * size
    gap = share - edge

    def fetch(offset):
        for side, ref in ((0, piece), (1, piece_over)):
            where = x if side == 0 else 1 - x
            start = pl.multiple_of(offset + where * size, BLOCK)
            last[pl.ds(start, size), :] = ref[...]
        return product(rows[...], last[...])

    def merge(ref, source, lanes, block, new):
        ref[:, lanes] = jnp.where(new, block, source[:, lanes])

    keep[...] = first_keep[...]
    send[...] = first_send[...]
    lane = lax.broadcasted_iota(jnp.int32, (rows.shape[0], share), 1)

    @pl.when(z == 0)
    def _():
        block = fetch(gap)
        for ref in (keep, send):
            ref[:, share:] = block[:, share // 2 :]
        head = block[:, : share // 2]
        new = lane[:, : share // 2] >= gap
        lanes = slice(share // 2, share)

        @pl.when(core == 1)
        def _():
            merge(keep, first_keep, lanes, head, new)

        @pl.when(core == 0)
        def _():
            merge(send, first_send, lanes, head, new)

    @pl.when(z == 3)
    def _():
        block = fetch(0)
        lanes = slice(0, share)

        @pl.when(core == 0)
        def _():
            merge(keep, first_keep, lanes, block, lane < edge)

        @pl.when(core == 1)
        def _():
            merge(send, first_send, lanes, block, lane < edge)


def sum_kernel(keep, other, out):
    out[...] = (keep[...] + other[...]).astype(out.dtype)


def finish_kernel(pick, arrived, cosine, sine, allowed, keys, values, out):
    width = arrived.shape[2]
    count = 2 * width // HD
    chosen = pick[...]
    planes = [
        jnp.dot(chosen, arrived[y], preferred_element_type=jnp.float32).astype(jnp.bfloat16)
        for y in range(2)
    ]
    source = lax.broadcasted_iota(jnp.int32, (HD, 2 * HD), 0)
    target = lax.broadcasted_iota(jnp.int32, (HD, 2 * HD), 1)
    heads = []
    for pair in range(count // 2):
        total = None
        for y in range(2):
            place = source // BLOCK * (2 * BLOCK) + y * BLOCK + source % BLOCK
            order = (place == target).astype(jnp.float32).astype(jnp.bfloat16)
            part = jnp.dot(
                planes[y][:, pair * HD : (pair + 1) * HD],
                order,
                preferred_element_type=jnp.float32,
            )
            total = part if total is None else total + part
        heads += [total[:, :HD], total[:, HD:]]

    def turn(block):
        other = pltpu.roll(block, HD // 2, 1)
        return (block * cosine[...] + other * sine[...]).astype(jnp.bfloat16)

    key = turn(heads[-2])
    value = heads[-1].astype(jnp.bfloat16)
    keys[...] = key
    values[...] = value
    mask = allowed[...] > 0
    for h in range(count - 2):
        scores = product(turn(heads[h]), key) / math.sqrt(HD)
        scores = jnp.where(mask, scores, jnp.float32(-1e30))
        expo = jnp.exp(scores - jnp.max(scores, axis=-1, keepdims=True))
        weights = (expo / jnp.sum(expo, axis=-1, keepdims=True)).astype(jnp.bfloat16)
        out[:, h * HD : (h + 1) * HD] = jnp.dot(
            weights, value, preferred_element_type=jnp.float32
        ).astype(out.dtype)


def finish(pick, arrived, cosine, sine, allowed):
    whole = pl.BlockSpec(memory_space=pltpu.VMEM)
    heads = 2 * arrived.shape[2] // HD - 2
    single = jax.ShapeDtypeStruct((TOK_DEV, HD), jnp.bfloat16)
    return pl.pallas_call(
        finish_kernel,
        out_shape=(single, single, jax.ShapeDtypeStruct((TOK_DEV, heads * HD), jnp.bfloat16)),
        in_specs=[whole] * 5,
        out_specs=(whole,) * 3,
        compiler_params=pltpu.CompilerParams(vmem_limit_bytes=6 << 20),
        name="attend",
    )(
        pick,
        arrived,
        jnp.concatenate([cosine, cosine], axis=1),
        jnp.concatenate([-sine, sine], axis=1),
        allowed.astype(jnp.float32),
    )


def paired(sent_rows, norm_gain, qkv_weight, groups):
    part = lax.axis_index("parts")
    group = lax.axis_index("dp")
    at = jnp.stack([group // 2, group % 2, part, lax.axis_index("tensor")]).astype(jnp.int32)
    turned = qkv_weight.T
    depth = turned.shape[1]
    count = turned.shape[0] // (2 * BLOCK)
    size = count * BLOCK
    swap = [(0, 1), (1, 0)]
    cut_at = sent_rows.shape[0] * 4 // 16
    whole = pl.BlockSpec(memory_space=pltpu.VMEM)
    anywhere = pl.BlockSpec(memory_space=pl.ANY)
    scalars = pl.BlockSpec(memory_space=pltpu.SMEM)
    mine = lax.dynamic_index_in_dim(
        turned.reshape(count, 2, BLOCK, depth), part, 1, False
    ).reshape(size, depth)
    ahead = sent_rows[:cut_at]
    ahead = lax.ppermute(ahead, "parts", swap)
    scale = scale_of(lax.psum(squares(sent_rows), "tensor"))
    their_scale = lax.ppermute(scale, "parts", swap)
    early, late, (ahead, rest, their_scale) = gather_line(
        mine, (ahead, sent_rows[cut_at:], their_scale)
    )
    behind = lax.ppermute(rest, "parts", swap)
    slots = sent_rows.shape[0]
    width = groups * size
    heads = width * HQ // (HQ + 2)
    half = jax.ShapeDtypeStruct((2 * slots, heads // 2 + width - heads), jnp.float32)
    keep, send, rows = pl.pallas_call(
        early_kernel,
        out_shape=(half, half, jax.ShapeDtypeStruct((2 * slots, depth), jnp.bfloat16)),
        in_specs=[scalars] + [whole] * 15,
        out_specs=(whole,) * 3,
        scratch_shapes=[pltpu.VMEM((width, depth), jnp.bfloat16)],
        compiler_params=pltpu.CompilerParams(vmem_limit_bytes=28 << 20),
        cost_estimate=pl.CostEstimate(
            flops=4 * slots * width * depth, bytes_accessed=12 << 20, transcendentals=0
        ),
        name="project_early",
    )(
        at,
        *early,
        sent_rows,
        ahead,
        behind,
        scale[None, :],
        their_scale[None, :],
        norm_gain[None, :],
    )
    keep, send = pl.pallas_call(
        late_kernel,
        out_shape=(half, half),
        in_specs=[scalars] + [whole] * 5,
        out_specs=(whole, whole),
        scratch_shapes=[pltpu.VMEM((heads // 2, depth), jnp.bfloat16)],
        input_output_aliases={1: 0, 2: 1},
        compiler_params=pltpu.CompilerParams(vmem_limit_bytes=16 << 20),
        cost_estimate=pl.CostEstimate(
            flops=2 * slots * heads * depth, bytes_accessed=6 << 20, transcendentals=0
        ),
        name="project_late",
    )(at, keep, send, *late, rows)
    ready = pl.pallas_call(
        sum_kernel,
        out_shape=jax.ShapeDtypeStruct(keep.shape, jnp.bfloat16),
        in_specs=[whole, whole],
        out_specs=whole,
        compiler_params=pltpu.CompilerParams(vmem_limit_bytes=6 << 20),
        name="sum_halves",
    )(keep, lax.ppermute(send, "tensor", swap))
    arrived = lax.all_to_all(ready, ("parts", "dp"), 0, 0, tiled=True)
    return arrived.reshape(2, slots, half.shape[1])


def single(sent_rows, norm_gain, qkv_weight):
    columns = lax.all_gather(qkv_weight.T, "dp", axis=0, tiled=True)
    scale = scale_of(lax.psum(squares(sent_rows), "tensor"))
    ready = sum_cores(product(scaled(sent_rows, scale[:, None], norm_gain[None, :]), columns))
    return lax.all_to_all(ready, "dp", 0, 0, tiled=True)


def per_device(sent_rows, norm_gain, qkv_weight, route_counts, response_lengths, prefix_lengths):
    groups = lax.axis_size("dp")
    slot = sent_rows.shape[0] // groups
    column = lax.dynamic_slice_in_dim(route_counts, lax.axis_index("dp"), 1, 1)[:, 0]
    pick = pick_of(column, slot, TOK_DEV)
    sequence, position = positions_of(response_lengths[0], prefix_lengths[0], TOK_DEV)
    allowed = (sequence[:, None] == sequence[None, :]) & (position[None, :] <= position[:, None])
    cosine, sine = rotary(position)
    if lax.axis_size("parts") == 2 and groups == 8 and qkv_weight.shape[1] == 160:
        arrived = paired(sent_rows, norm_gain, qkv_weight, groups)
        return finish(pick, arrived, cosine, sine, allowed)
    arrived = single(sent_rows, norm_gain, qkv_weight)
    heads = arrived.shape[1] // HD
    packed = jnp.dot(pick, arrived, preferred_element_type=jnp.float32)
    packed = packed.reshape(TOK_DEV, heads, HD)
    queries = rotate(packed[:, :-2], cosine, sine).astype(jnp.bfloat16)
    new_keys = rotate(packed[:, -2], cosine, sine).astype(jnp.bfloat16)
    new_values = packed[:, -1].astype(jnp.bfloat16)
    out = attend(queries, new_keys, new_values, allowed)
    return (new_keys, new_values, out.reshape(TOK_DEV, (heads - 2) * HD))


def solution(mesh):
    in_specs = (
        P(("parts", "dp"), "tensor"),
        P("tensor"),
        P("tensor", "dp"),
        P("parts", None),
        P(("parts", "dp"), None),
        P(("parts", "dp"), None),
    )
    out_specs = (P(("parts", "dp"), None), P(("parts", "dp"), None), P(("parts", "dp"), "tensor"))
    return jax.shard_map(
        per_device, mesh=mesh, in_specs=in_specs, out_specs=out_specs, check_vma=False
    )
```

```python
import math

import jax
import jax.numpy as jnp
from jax import lax
from jax.experimental import pallas as pl
from jax.experimental.pallas import tpu as pltpu
from jax.sharding import PartitionSpec as P

D = 8192
HD = 128
HQ = 8
TOK_DEV = 128
BLOCK = 16


def rotary(positions):
    half = HD // 2
    freq = jnp.exp(-jnp.log(500000.0) * jnp.arange(half, dtype=jnp.float32) * 2.0 / HD)
    angle = positions.astype(jnp.float32)[:, None] * freq[None, :]
    return (jnp.cos(angle), jnp.sin(angle))


def rotate(block, cosine, sine):
    half = HD // 2
    if block.ndim == 3:
        cosine = cosine[:, None, :]
        sine = sine[:, None, :]
    first = block[..., :half]
    second = block[..., half:]
    return jnp.concatenate(
        [first * cosine - second * sine, second * cosine + first * sine], axis=-1
    )


def members(lengths, count):
    ends = jnp.cumsum(lengths)
    starts = ends - lengths
    place = jnp.arange(count, dtype=jnp.int32)
    member = (place[:, None] >= starts[None, :]) & (place[:, None] < ends[None, :])
    return (member, place[:, None] - starts[None, :])


def positions_of(lengths, prefix, count):
    member, within = members(lengths, count)
    which = jnp.arange(lengths.shape[0], dtype=jnp.int32)
    sequence = jnp.sum(jnp.where(member, which[None, :], 0), axis=1)
    position = jnp.sum(jnp.where(member, prefix[None, :] + within, 0), axis=1)
    return (sequence, position)


def pick_of(column, slot, count):
    member, within = members(column, count)
    source = jnp.arange(column.shape[0], dtype=jnp.int32)
    index = jnp.sum(jnp.where(member, source[None, :] * slot + within, 0), axis=1)
    slots = jnp.arange(column.shape[0] * slot, dtype=jnp.int32)
    return (index[:, None] == slots[None, :]).astype(jnp.bfloat16)


def attend(queries, keys, values, allowed):
    scores = jnp.einsum(
        "qhd,kd->hqk", queries, keys, preferred_element_type=jnp.float32
    ) / jnp.sqrt(jnp.float32(HD))
    scores = jnp.where(allowed[None, :, :], scores, jnp.float32(-1e30))
    top = jnp.max(scores, axis=-1, keepdims=True)
    expo = jnp.exp(scores - top)
    weights = (expo / jnp.sum(expo, axis=-1, keepdims=True)).astype(jnp.bfloat16)
    out = jnp.einsum("hqk,kd->qhd", weights, values, preferred_element_type=jnp.float32)
    return out.astype(jnp.bfloat16)


def squares(rows):
    wide = rows.astype(jnp.float32)
    return jnp.sum(wide * wide, axis=1)


def scale_of(total):
    return lax.rsqrt(total / D + 1e-05)


def scaled(rows, scale, norm_gain):
    return (rows.astype(jnp.float32) * scale * norm_gain).astype(jnp.bfloat16)


def product(rows, columns):
    return lax.dot_general(
        rows, columns, (((1,), (1,)), ((), ())), preferred_element_type=jnp.float32
    )


def cut(partial, width, core):
    share = width // lax.axis_size("tensor")
    mine = lax.dynamic_slice_in_dim(partial, core * share, share, 1)
    return jnp.concatenate([mine, partial[:, width:]], axis=1)


def sum_cores(partial):
    width = HQ * HD * partial.shape[1] // (HQ * HD + 2 * HD)
    core = lax.axis_index("tensor")
    other = lax.ppermute(cut(partial, width, 1 - core), "tensor", [(0, 1), (1, 0)])
    return (cut(partial, width, core) + other).astype(jnp.bfloat16)


PAIRS = ((0, 1), (1, 0), (2, 3), (3, 2))
ACROSS = ((1, 2), (2, 1))
OUTWARD = ((1, 0), (2, 3))
ENDS = (0, 3)
MIDDLE = (1, 2)


def overs(places):
    return [(2 * z + x, 2 * z + 1 - x) for z in places for x in range(2)]


def alongs(moves):
    return [(2 * a + x, 2 * b + x) for a, b in moves for x in range(2)]


def gather_line(mine, first):
    def send(block, pairs):
        return lax.ppermute(block, "dp", pairs)

    near = send(mine, alongs(PAIRS))
    cross = send(mine, alongs(ACROSS) + overs(ENDS))
    side = send(mine, overs(MIDDLE))
    near, cross, first = lax.optimization_barrier((near, cross, first))
    second = send(cross, alongs(PAIRS))
    onward = send(near, alongs(ACROSS) + overs(ENDS))
    cross_next, side = lax.optimization_barrier((cross, side))
    cross_over = send(cross_next, overs(MIDDLE))
    onward_next, _ = lax.optimization_barrier((onward, second))
    last = send(onward_next, alongs(OUTWARD))
    second_next, _ = lax.optimization_barrier((second, cross_over))
    second_over = send(second_next, overs(ENDS))
    far_over = send(onward_next, overs(MIDDLE))
    last_over = send(last, overs(ENDS))
    early = (mine, near, cross, side, second, onward, cross_over, far_over, second_over)
    return early, (last, last_over), first


def early_kernel(
    at, mine, near, cross, side, second, onward, cross_over, far_over, second_over,
    own, ahead, behind, own_scale, their_scale, gain, keep, send, rows, whole, sem,
):
    z, x, part, core = at[0], at[1], at[2], at[3]
    size = mine.shape[0]

    at_end = (z == 0) | (z == 3)
    middle = jnp.logical_not(at_end)
    there = pl.multiple_of((2 * (3 - z) + 1 - x) * size, BLOCK)
    fetch = pltpu.make_async_copy(cross_over, whole.at[pl.ds(there, size)], sem)

    @pl.when(middle)
    def _():
        fetch.start()

    def place(pairs):
        for where, pieces in pairs:
            for j, piece in enumerate(pieces):
                column = x if j == 0 else 1 - x
                start = pl.multiple_of((2 * where + column) * size, BLOCK)
                whole[pl.ds(start, size), :] = piece[...]

    count = own.shape[0]
    for index, sources, scale in (
        (part, (own,), own_scale),
        (1 - part, (ahead, behind), their_scale),
    ):
        upright = jnp.broadcast_to(scale[...], (HD, count)).T[:, :1]
        done = 0
        for source in sources:
            for low in range(0, source.shape[0], BLOCK):
                start = pl.multiple_of(index * count + done + low, BLOCK)
                rows[pl.ds(start, BLOCK), :] = scaled(
                    source[low : low + BLOCK, :],
                    upright[done + low : done + low + BLOCK, :],
                    gain[...],
                )
            done += source.shape[0]

    pair = z + 1 - 2 * (z % 2)

    @pl.when(at_end)
    def _():
        place(
            (
                (z, (mine, cross)),
                (pair, (near, onward)),
                ((z + 2) % 4, (second, second_over)),
                (3 - z, (mine, cross)),
            )
        )

    @pl.when(middle)
    def _():
        place(
            (
                (z, (mine, side)),
                (pair, (near, second)),
                ((z + 2) % 4, (onward, far_over)),
                (3 - z, (cross,)),
            )
        )

    @pl.when(middle)
    def _():
        fetch.wait()

    share = whole.shape[0] * HQ // (HQ + 2) // 2
    halves = [product(rows[...], whole[c * share : (c + 1) * share, :]) for c in range(2)]
    rest = product(rows[...], whole[2 * share :, :])
    for ref in (keep, send):
        ref[:, share:] = rest
    for t in range(2):

        @pl.when(core == t)
        def _():
            keep[:, :share] = halves[t]
            send[:, :share] = halves[1 - t]


def late_kernel(at, first_keep, first_send, piece, piece_over, rows, keep, send, last):
    z, x, core = at[0], at[1], at[3]
    size = piece.shape[0]
    share = last.shape[0]
    edge = 2 * size
    gap = share - edge

    def fetch(offset):
        for side, ref in ((0, piece), (1, piece_over)):
            where = x if side == 0 else 1 - x
            start = pl.multiple_of(offset + where * size, BLOCK)
            last[pl.ds(start, size), :] = ref[...]
        return product(rows[...], last[...])

    def merge(ref, source, lanes, block, new):
        ref[:, lanes] = jnp.where(new, block, source[:, lanes])

    keep[...] = first_keep[...]
    send[...] = first_send[...]
    lane = lax.broadcasted_iota(jnp.int32, (rows.shape[0], share), 1)

    @pl.when(z == 0)
    def _():
        block = fetch(gap)
        for ref in (keep, send):
            ref[:, share:] = block[:, share // 2 :]
        head = block[:, : share // 2]
        new = lane[:, : share // 2] >= gap
        lanes = slice(share // 2, share)

        @pl.when(core == 1)
        def _():
            merge(keep, first_keep, lanes, head, new)

        @pl.when(core == 0)
        def _():
            merge(send, first_send, lanes, head, new)

    @pl.when(z == 3)
    def _():
        block = fetch(0)
        lanes = slice(0, share)

        @pl.when(core == 0)
        def _():
            merge(keep, first_keep, lanes, block, lane < edge)

        @pl.when(core == 1)
        def _():
            merge(send, first_send, lanes, block, lane < edge)


def sum_kernel(keep, other, out):
    out[...] = (keep[...] + other[...]).astype(out.dtype)


def finish_kernel(pick, arrived, cosine, sine, allowed, keys, values, out):
    width = arrived.shape[2]
    count = 2 * width // HD
    chosen = pick[...]
    planes = [
        jnp.dot(chosen, arrived[y], preferred_element_type=jnp.float32).astype(jnp.bfloat16)
        for y in range(2)
    ]
    source = lax.broadcasted_iota(jnp.int32, (HD, 2 * HD), 0)
    target = lax.broadcasted_iota(jnp.int32, (HD, 2 * HD), 1)
    heads = []
    for pair in range(count // 2):
        total = None
        for y in range(2):
            place = source // BLOCK * (2 * BLOCK) + y * BLOCK + source % BLOCK
            order = (place == target).astype(jnp.float32).astype(jnp.bfloat16)
            part = jnp.dot(
                planes[y][:, pair * HD : (pair + 1) * HD],
                order,
                preferred_element_type=jnp.float32,
            )
            total = part if total is None else total + part
        heads += [total[:, :HD], total[:, HD:]]

    def turn(block):
        other = pltpu.roll(block, HD // 2, 1)
        return (block * cosine[...] + other * sine[...]).astype(jnp.bfloat16)

    key = turn(heads[-2])
    value = heads[-1].astype(jnp.bfloat16)
    keys[...] = key
    values[...] = value
    mask = allowed[...] > 0
    for h in range(count - 2):
        scores = product(turn(heads[h]), key) / math.sqrt(HD)
        scores = jnp.where(mask, scores, jnp.float32(-1e30))
        expo = jnp.exp(scores - jnp.max(scores, axis=-1, keepdims=True))
        weights = (expo / jnp.sum(expo, axis=-1, keepdims=True)).astype(jnp.bfloat16)
        out[:, h * HD : (h + 1) * HD] = jnp.dot(
            weights, value, preferred_element_type=jnp.float32
        ).astype(out.dtype)


def finish(pick, arrived, cosine, sine, allowed):
    whole = pl.BlockSpec(memory_space=pltpu.VMEM)
    heads = 2 * arrived.shape[2] // HD - 2
    single = jax.ShapeDtypeStruct((TOK_DEV, HD), jnp.bfloat16)
    return pl.pallas_call(
        finish_kernel,
        out_shape=(single, single, jax.ShapeDtypeStruct((TOK_DEV, heads * HD), jnp.bfloat16)),
        in_specs=[whole] * 5,
        out_specs=(whole,) * 3,
        compiler_params=pltpu.CompilerParams(vmem_limit_bytes=6 << 20),
        name="attend",
    )(
        pick,
        arrived,
        jnp.concatenate([cosine, cosine], axis=1),
        jnp.concatenate([-sine, sine], axis=1),
        allowed.astype(jnp.float32),
    )


def paired(sent_rows, norm_gain, qkv_weight, groups):
    part = lax.axis_index("parts")
    group = lax.axis_index("dp")
    at = jnp.stack([group // 2, group % 2, part, lax.axis_index("tensor")]).astype(jnp.int32)
    turned = qkv_weight.T
    depth = turned.shape[1]
    count = turned.shape[0] // (2 * BLOCK)
    size = count * BLOCK
    swap = [(0, 1), (1, 0)]
    cut_at = sent_rows.shape[0] * 3 // 16
    whole = pl.BlockSpec(memory_space=pltpu.VMEM)
    anywhere = pl.BlockSpec(memory_space=pl.ANY)
    scalars = pl.BlockSpec(memory_space=pltpu.SMEM)
    mine = lax.dynamic_index_in_dim(
        turned.reshape(count, 2, BLOCK, depth), part, 1, False
    ).reshape(size, depth)
    ahead = sent_rows[:cut_at]
    ahead = lax.ppermute(ahead, "parts", swap)
    scale = scale_of(lax.psum(squares(sent_rows), "tensor"))
    their_scale = lax.ppermute(scale, "parts", swap)
    early, late, (ahead, rest, their_scale) = gather_line(
        mine, (ahead, sent_rows[cut_at:], their_scale)
    )
    behind = lax.ppermute(rest, "parts", swap)
    slots = sent_rows.shape[0]
    width = groups * size
    heads = width * HQ // (HQ + 2)
    half = jax.ShapeDtypeStruct((2 * slots, heads // 2 + width - heads), jnp.float32)
    keep, send, rows = pl.pallas_call(
        early_kernel,
        out_shape=(half, half, jax.ShapeDtypeStruct((2 * slots, depth), jnp.bfloat16)),
        in_specs=[scalars] + [whole] * 6 + [pl.BlockSpec(memory_space=pltpu.HBM)] + [whole] * 8,
        out_specs=(whole,) * 3,
        scratch_shapes=[pltpu.VMEM((width, depth), jnp.bfloat16), pltpu.SemaphoreType.DMA],
        compiler_params=pltpu.CompilerParams(vmem_limit_bytes=28 << 20),
        cost_estimate=pl.CostEstimate(
            flops=4 * slots * width * depth, bytes_accessed=12 << 20, transcendentals=0
        ),
        name="project_early",
    )(
        at,
        *early,
        sent_rows,
        ahead,
        behind,
        scale[None, :],
        their_scale[None, :],
        norm_gain[None, :],
    )
    keep, send = pl.pallas_call(
        late_kernel,
        out_shape=(half, half),
        in_specs=[scalars] + [whole] * 5,
        out_specs=(whole, whole),
        scratch_shapes=[pltpu.VMEM((heads // 2, depth), jnp.bfloat16)],
        input_output_aliases={1: 0, 2: 1},
        compiler_params=pltpu.CompilerParams(vmem_limit_bytes=16 << 20),
        cost_estimate=pl.CostEstimate(
            flops=2 * slots * heads * depth, bytes_accessed=6 << 20, transcendentals=0
        ),
        name="project_late",
    )(at, keep, send, *late, rows)
    ready = pl.pallas_call(
        sum_kernel,
        out_shape=jax.ShapeDtypeStruct(keep.shape, jnp.bfloat16),
        in_specs=[whole, whole],
        out_specs=whole,
        compiler_params=pltpu.CompilerParams(vmem_limit_bytes=6 << 20),
        name="sum_halves",
    )(keep, lax.ppermute(send, "tensor", swap))
    arrived = lax.all_to_all(ready, ("parts", "dp"), 0, 0, tiled=True)
    return arrived.reshape(2, slots, half.shape[1])


def single(sent_rows, norm_gain, qkv_weight):
    columns = lax.all_gather(qkv_weight.T, "dp", axis=0, tiled=True)
    scale = scale_of(lax.psum(squares(sent_rows), "tensor"))
    ready = sum_cores(product(scaled(sent_rows, scale[:, None], norm_gain[None, :]), columns))
    return lax.all_to_all(ready, "dp", 0, 0, tiled=True)


def per_device(sent_rows, norm_gain, qkv_weight, route_counts, response_lengths, prefix_lengths):
    groups = lax.axis_size("dp")
    slot = sent_rows.shape[0] // groups
    column = lax.dynamic_slice_in_dim(route_counts, lax.axis_index("dp"), 1, 1)[:, 0]
    pick = pick_of(column, slot, TOK_DEV)
    sequence, position = positions_of(response_lengths[0], prefix_lengths[0], TOK_DEV)
    allowed = (sequence[:, None] == sequence[None, :]) & (position[None, :] <= position[:, None])
    cosine, sine = rotary(position)
    if lax.axis_size("parts") == 2 and groups == 8 and qkv_weight.shape[1] == 160:
        arrived = paired(sent_rows, norm_gain, qkv_weight, groups)
        return finish(pick, arrived, cosine, sine, allowed)
    arrived = single(sent_rows, norm_gain, qkv_weight)
    heads = arrived.shape[1] // HD
    packed = jnp.dot(pick, arrived, preferred_element_type=jnp.float32)
    packed = packed.reshape(TOK_DEV, heads, HD)
    queries = rotate(packed[:, :-2], cosine, sine).astype(jnp.bfloat16)
    new_keys = rotate(packed[:, -2], cosine, sine).astype(jnp.bfloat16)
    new_values = packed[:, -1].astype(jnp.bfloat16)
    out = attend(queries, new_keys, new_values, allowed)
    return (new_keys, new_values, out.reshape(TOK_DEV, (heads - 2) * HD))


def solution(mesh):
    in_specs = (
        P(("parts", "dp"), "tensor"),
        P("tensor"),
        P("tensor", "dp"),
        P("parts", None),
        P(("parts", "dp"), None),
        P(("parts", "dp"), None),
    )
    out_specs = (P(("parts", "dp"), None), P(("parts", "dp"), None), P(("parts", "dp"), "tensor"))
    return jax.shard_map(
        per_device, mesh=mesh, in_specs=in_specs, out_specs=out_specs, check_vma=False
    )
```

```python
import math

import jax
import jax.numpy as jnp
from jax import lax
from jax.experimental import pallas as pl
from jax.experimental.pallas import tpu as pltpu
from jax.sharding import PartitionSpec as P

D = 8192
HD = 128
HQ = 8
TOK_DEV = 128
BLOCK = 16


def rotary(positions):
    half = HD // 2
    freq = jnp.exp(-jnp.log(500000.0) * jnp.arange(half, dtype=jnp.float32) * 2.0 / HD)
    angle = positions.astype(jnp.float32)[:, None] * freq[None, :]
    return (jnp.cos(angle), jnp.sin(angle))


def rotate(block, cosine, sine):
    half = HD // 2
    if block.ndim == 3:
        cosine = cosine[:, None, :]
        sine = sine[:, None, :]
    first = block[..., :half]
    second = block[..., half:]
    return jnp.concatenate(
        [first * cosine - second * sine, second * cosine + first * sine], axis=-1
    )


def members(lengths, count):
    ends = jnp.cumsum(lengths)
    starts = ends - lengths
    place = jnp.arange(count, dtype=jnp.int32)
    member = (place[:, None] >= starts[None, :]) & (place[:, None] < ends[None, :])
    return (member, place[:, None] - starts[None, :])


def positions_of(lengths, prefix, count):
    member, within = members(lengths, count)
    which = jnp.arange(lengths.shape[0], dtype=jnp.int32)
    sequence = jnp.sum(jnp.where(member, which[None, :], 0), axis=1)
    position = jnp.sum(jnp.where(member, prefix[None, :] + within, 0), axis=1)
    return (sequence, position)


def pick_of(column, slot, count):
    member, within = members(column, count)
    source = jnp.arange(column.shape[0], dtype=jnp.int32)
    index = jnp.sum(jnp.where(member, source[None, :] * slot + within, 0), axis=1)
    slots = jnp.arange(column.shape[0] * slot, dtype=jnp.int32)
    return (index[:, None] == slots[None, :]).astype(jnp.bfloat16)


def attend(queries, keys, values, allowed):
    scores = jnp.einsum(
        "qhd,kd->hqk", queries, keys, preferred_element_type=jnp.float32
    ) / jnp.sqrt(jnp.float32(HD))
    scores = jnp.where(allowed[None, :, :], scores, jnp.float32(-1e30))
    top = jnp.max(scores, axis=-1, keepdims=True)
    expo = jnp.exp(scores - top)
    weights = (expo / jnp.sum(expo, axis=-1, keepdims=True)).astype(jnp.bfloat16)
    out = jnp.einsum("hqk,kd->qhd", weights, values, preferred_element_type=jnp.float32)
    return out.astype(jnp.bfloat16)


def squares(rows):
    wide = rows.astype(jnp.float32)
    return jnp.sum(wide * wide, axis=1)


def scale_of(total):
    return lax.rsqrt(total / D + 1e-05)


def scaled(rows, scale, norm_gain):
    return (rows.astype(jnp.float32) * scale * norm_gain).astype(jnp.bfloat16)


def product(rows, columns):
    return lax.dot_general(
        rows, columns, (((1,), (1,)), ((), ())), preferred_element_type=jnp.float32
    )


def cut(partial, width, core):
    share = width // lax.axis_size("tensor")
    mine = lax.dynamic_slice_in_dim(partial, core * share, share, 1)
    return jnp.concatenate([mine, partial[:, width:]], axis=1)


def sum_cores(partial):
    width = HQ * HD * partial.shape[1] // (HQ * HD + 2 * HD)
    core = lax.axis_index("tensor")
    other = lax.ppermute(cut(partial, width, 1 - core), "tensor", [(0, 1), (1, 0)])
    return (cut(partial, width, core) + other).astype(jnp.bfloat16)


PAIRS = ((0, 1), (1, 0), (2, 3), (3, 2))
ACROSS = ((1, 2), (2, 1))
OUTWARD = ((1, 0), (2, 3))
ENDS = (0, 3)
MIDDLE = (1, 2)


def overs(places):
    return [(2 * z + x, 2 * z + 1 - x) for z in places for x in range(2)]


def alongs(moves):
    return [(2 * a + x, 2 * b + x) for a, b in moves for x in range(2)]


def gather_line(mine, first):
    def send(block, pairs):
        return lax.ppermute(block, "dp", pairs)

    near = send(mine, alongs(PAIRS))
    cross = send(mine, alongs(ACROSS) + overs(ENDS))
    side = send(mine, overs(MIDDLE))
    near, cross, first = lax.optimization_barrier((near, cross, first))
    second = send(cross, alongs(PAIRS))
    onward = send(near, alongs(ACROSS) + overs(ENDS))
    cross_next, side = lax.optimization_barrier((cross, side))
    cross_over = send(cross_next, overs(MIDDLE))
    onward_next, _ = lax.optimization_barrier((onward, second))
    last = send(onward_next, alongs(OUTWARD))
    second_next, _ = lax.optimization_barrier((second, cross_over))
    second_over = send(second_next, overs(ENDS))
    far_over = send(onward_next, overs(MIDDLE))
    last_over = send(last, overs(ENDS))
    early = (mine, near, cross, side, second, onward, cross_over, far_over, second_over)
    return early, (last, last_over), first


def early_kernel(
    at, mine, near, cross, side, second, onward, cross_over, far_over, second_over,
    own, ahead, behind, own_scale, their_scale, gain, keep, send, rows, whole, sems,
):
    z, x, part, core = at[0], at[1], at[2], at[3]
    size = mine.shape[0]

    at_end = (z == 0) | (z == 3)
    middle = jnp.logical_not(at_end)

    def fetch(k, piece, where):
        start = pl.multiple_of((2 * where + 1 - x) * size, BLOCK)
        return pltpu.make_async_copy(piece, whole.at[pl.ds(start, size)], sems.at[k])

    at_ends = (fetch(0, second_over, (z + 2) % 4),)
    in_middle = (
        fetch(0, far_over, (z + 2) % 4),
        fetch(1, cross_over, 3 - z),
        fetch(2, side, z),
    )
    for here, copies in ((at_end, at_ends), (middle, in_middle)):

        @pl.when(here)
        def _():
            for copy in copies:
                copy.start()

    def place(pairs):
        for where, pieces in pairs:
            for j, piece in enumerate(pieces):
                column = x if j == 0 else 1 - x
                start = pl.multiple_of((2 * where + column) * size, BLOCK)
                whole[pl.ds(start, size), :] = piece[...]

    count = own.shape[0]
    for index, sources, scale in (
        (part, (own,), own_scale),
        (1 - part, (ahead, behind), their_scale),
    ):
        upright = jnp.broadcast_to(scale[...], (HD, count)).T[:, :1]
        done = 0
        for source in sources:
            for low in range(0, source.shape[0], BLOCK):
                start = pl.multiple_of(index * count + done + low, BLOCK)
                rows[pl.ds(start, BLOCK), :] = scaled(
                    source[low : low + BLOCK, :],
                    upright[done + low : done + low + BLOCK, :],
                    gain[...],
                )
            done += source.shape[0]

    pair = z + 1 - 2 * (z % 2)

    @pl.when(at_end)
    def _():
        place(
            (
                (z, (mine, cross)),
                (pair, (near, onward)),
                ((z + 2) % 4, (second,)),
                (3 - z, (mine, cross)),
            )
        )

    @pl.when(middle)
    def _():
        place(
            (
                (z, (mine,)),
                (pair, (near, second)),
                ((z + 2) % 4, (onward,)),
                (3 - z, (cross,)),
            )
        )

    for here, copies in ((at_end, at_ends), (middle, in_middle)):

        @pl.when(here)
        def _():
            for copy in copies:
                copy.wait()

    share = whole.shape[0] * HQ // (HQ + 2) // 2
    halves = [product(rows[...], whole[c * share : (c + 1) * share, :]) for c in range(2)]
    rest = product(rows[...], whole[2 * share :, :])
    for ref in (keep, send):
        ref[:, share:] = rest
    for t in range(2):

        @pl.when(core == t)
        def _():
            keep[:, :share] = halves[t]
            send[:, :share] = halves[1 - t]


def late_kernel(at, first_keep, first_send, piece, piece_over, rows, keep, send, last):
    z, x, core = at[0], at[1], at[3]
    size = piece.shape[0]
    share = last.shape[0]
    edge = 2 * size
    gap = share - edge

    def fetch(offset):
        for side, ref in ((0, piece), (1, piece_over)):
            where = x if side == 0 else 1 - x
            start = pl.multiple_of(offset + where * size, BLOCK)
            last[pl.ds(start, size), :] = ref[...]
        return product(rows[...], last[...])

    def merge(ref, source, lanes, block, new):
        ref[:, lanes] = jnp.where(new, block, source[:, lanes])

    keep[...] = first_keep[...]
    send[...] = first_send[...]
    lane = lax.broadcasted_iota(jnp.int32, (rows.shape[0], share), 1)

    @pl.when(z == 0)
    def _():
        block = fetch(gap)
        for ref in (keep, send):
            ref[:, share:] = block[:, share // 2 :]
        head = block[:, : share // 2]
        new = lane[:, : share // 2] >= gap
        lanes = slice(share // 2, share)

        @pl.when(core == 1)
        def _():
            merge(keep, first_keep, lanes, head, new)

        @pl.when(core == 0)
        def _():
            merge(send, first_send, lanes, head, new)

    @pl.when(z == 3)
    def _():
        block = fetch(0)
        lanes = slice(0, share)

        @pl.when(core == 0)
        def _():
            merge(keep, first_keep, lanes, block, lane < edge)

        @pl.when(core == 1)
        def _():
            merge(send, first_send, lanes, block, lane < edge)


def sum_kernel(keep, other, out):
    out[...] = (keep[...] + other[...]).astype(out.dtype)


def finish_kernel(pick, arrived, cosine, sine, allowed, keys, values, out):
    width = arrived.shape[2]
    count = 2 * width // HD
    chosen = pick[...]
    planes = [
        jnp.dot(chosen, arrived[y], preferred_element_type=jnp.float32).astype(jnp.bfloat16)
        for y in range(2)
    ]
    source = lax.broadcasted_iota(jnp.int32, (HD, 2 * HD), 0)
    target = lax.broadcasted_iota(jnp.int32, (HD, 2 * HD), 1)
    heads = []
    for pair in range(count // 2):
        total = None
        for y in range(2):
            place = source // BLOCK * (2 * BLOCK) + y * BLOCK + source % BLOCK
            order = (place == target).astype(jnp.float32).astype(jnp.bfloat16)
            part = jnp.dot(
                planes[y][:, pair * HD : (pair + 1) * HD],
                order,
                preferred_element_type=jnp.float32,
            )
            total = part if total is None else total + part
        heads += [total[:, :HD], total[:, HD:]]

    def turn(block):
        other = pltpu.roll(block, HD // 2, 1)
        return (block * cosine[...] + other * sine[...]).astype(jnp.bfloat16)

    key = turn(heads[-2])
    value = heads[-1].astype(jnp.bfloat16)
    keys[...] = key
    values[...] = value
    mask = allowed[...] > 0
    for h in range(count - 2):
        scores = product(turn(heads[h]), key) / math.sqrt(HD)
        scores = jnp.where(mask, scores, jnp.float32(-1e30))
        expo = jnp.exp(scores - jnp.max(scores, axis=-1, keepdims=True))
        weights = (expo / jnp.sum(expo, axis=-1, keepdims=True)).astype(jnp.bfloat16)
        out[:, h * HD : (h + 1) * HD] = jnp.dot(
            weights, value, preferred_element_type=jnp.float32
        ).astype(out.dtype)


def finish(pick, arrived, cosine, sine, allowed):
    whole = pl.BlockSpec(memory_space=pltpu.VMEM)
    heads = 2 * arrived.shape[2] // HD - 2
    single = jax.ShapeDtypeStruct((TOK_DEV, HD), jnp.bfloat16)
    return pl.pallas_call(
        finish_kernel,
        out_shape=(single, single, jax.ShapeDtypeStruct((TOK_DEV, heads * HD), jnp.bfloat16)),
        in_specs=[whole] * 5,
        out_specs=(whole,) * 3,
        compiler_params=pltpu.CompilerParams(vmem_limit_bytes=6 << 20),
        name="attend",
    )(
        pick,
        arrived,
        jnp.concatenate([cosine, cosine], axis=1),
        jnp.concatenate([-sine, sine], axis=1),
        allowed.astype(jnp.float32),
    )


def paired(sent_rows, norm_gain, qkv_weight, groups):
    part = lax.axis_index("parts")
    group = lax.axis_index("dp")
    at = jnp.stack([group // 2, group % 2, part, lax.axis_index("tensor")]).astype(jnp.int32)
    turned = qkv_weight.T
    depth = turned.shape[1]
    count = turned.shape[0] // (2 * BLOCK)
    size = count * BLOCK
    swap = [(0, 1), (1, 0)]
    cut_at = sent_rows.shape[0] * 3 // 16
    whole = pl.BlockSpec(memory_space=pltpu.VMEM)
    apart = pl.BlockSpec(memory_space=pltpu.HBM)
    scalars = pl.BlockSpec(memory_space=pltpu.SMEM)
    mine = lax.dynamic_index_in_dim(
        turned.reshape(count, 2, BLOCK, depth), part, 1, False
    ).reshape(size, depth)
    ahead = sent_rows[:cut_at]
    ahead = lax.ppermute(ahead, "parts", swap)
    scale = scale_of(lax.psum(squares(sent_rows), "tensor"))
    their_scale = lax.ppermute(scale, "parts", swap)
    early, late, (ahead, rest, their_scale) = gather_line(
        mine, (ahead, sent_rows[cut_at:], their_scale)
    )
    behind = lax.ppermute(rest, "parts", swap)
    slots = sent_rows.shape[0]
    width = groups * size
    heads = width * HQ // (HQ + 2)
    half = jax.ShapeDtypeStruct((2 * slots, heads // 2 + width - heads), jnp.float32)
    keep, send, rows = pl.pallas_call(
        early_kernel,
        out_shape=(half, half, jax.ShapeDtypeStruct((2 * slots, depth), jnp.bfloat16)),
        in_specs=[scalars] + [whole] * 3 + [apart] + [whole] * 2 + [apart] * 3 + [whole] * 6,
        out_specs=(whole,) * 3,
        scratch_shapes=[pltpu.VMEM((width, depth), jnp.bfloat16), pltpu.SemaphoreType.DMA((3,))],
        compiler_params=pltpu.CompilerParams(vmem_limit_bytes=28 << 20),
        cost_estimate=pl.CostEstimate(
            flops=4 * slots * width * depth, bytes_accessed=12 << 20, transcendentals=0
        ),
        name="project_early",
    )(
        at,
        *early,
        sent_rows,
        ahead,
        behind,
        scale[None, :],
        their_scale[None, :],
        norm_gain[None, :],
    )
    keep, send = pl.pallas_call(
        late_kernel,
        out_shape=(half, half),
        in_specs=[scalars] + [whole] * 5,
        out_specs=(whole, whole),
        scratch_shapes=[pltpu.VMEM((heads // 2, depth), jnp.bfloat16)],
        input_output_aliases={1: 0, 2: 1},
        compiler_params=pltpu.CompilerParams(vmem_limit_bytes=16 << 20),
        cost_estimate=pl.CostEstimate(
            flops=2 * slots * heads * depth, bytes_accessed=6 << 20, transcendentals=0
        ),
        name="project_late",
    )(at, keep, send, *late, rows)
    ready = pl.pallas_call(
        sum_kernel,
        out_shape=jax.ShapeDtypeStruct(keep.shape, jnp.bfloat16),
        in_specs=[whole, whole],
        out_specs=whole,
        compiler_params=pltpu.CompilerParams(vmem_limit_bytes=6 << 20),
        name="sum_halves",
    )(keep, lax.ppermute(send, "tensor", swap))
    arrived = lax.all_to_all(ready, ("parts", "dp"), 0, 0, tiled=True)
    return arrived.reshape(2, slots, half.shape[1])


def single(sent_rows, norm_gain, qkv_weight):
    columns = lax.all_gather(qkv_weight.T, "dp", axis=0, tiled=True)
    scale = scale_of(lax.psum(squares(sent_rows), "tensor"))
    ready = sum_cores(product(scaled(sent_rows, scale[:, None], norm_gain[None, :]), columns))
    return lax.all_to_all(ready, "dp", 0, 0, tiled=True)


def per_device(sent_rows, norm_gain, qkv_weight, route_counts, response_lengths, prefix_lengths):
    groups = lax.axis_size("dp")
    slot = sent_rows.shape[0] // groups
    column = lax.dynamic_slice_in_dim(route_counts, lax.axis_index("dp"), 1, 1)[:, 0]
    pick = pick_of(column, slot, TOK_DEV)
    sequence, position = positions_of(response_lengths[0], prefix_lengths[0], TOK_DEV)
    allowed = (sequence[:, None] == sequence[None, :]) & (position[None, :] <= position[:, None])
    cosine, sine = rotary(position)
    if lax.axis_size("parts") == 2 and groups == 8 and qkv_weight.shape[1] == 160:
        arrived = paired(sent_rows, norm_gain, qkv_weight, groups)
        return finish(pick, arrived, cosine, sine, allowed)
    arrived = single(sent_rows, norm_gain, qkv_weight)
    heads = arrived.shape[1] // HD
    packed = jnp.dot(pick, arrived, preferred_element_type=jnp.float32)
    packed = packed.reshape(TOK_DEV, heads, HD)
    queries = rotate(packed[:, :-2], cosine, sine).astype(jnp.bfloat16)
    new_keys = rotate(packed[:, -2], cosine, sine).astype(jnp.bfloat16)
    new_values = packed[:, -1].astype(jnp.bfloat16)
    out = attend(queries, new_keys, new_values, allowed)
    return (new_keys, new_values, out.reshape(TOK_DEV, (heads - 2) * HD))


def solution(mesh):
    in_specs = (
        P(("parts", "dp"), "tensor"),
        P("tensor"),
        P("tensor", "dp"),
        P("parts", None),
        P(("parts", "dp"), None),
        P(("parts", "dp"), None),
    )
    out_specs = (P(("parts", "dp"), None), P(("parts", "dp"), None), P(("parts", "dp"), "tensor"))
    return jax.shard_map(
        per_device, mesh=mesh, in_specs=in_specs, out_specs=out_specs, check_vma=False
    )
```
